128 devices in a mesh: grp: 2 (over core), tx: 8 (over x_lo, z), ty: 8 (over x_hi, y).
Axes of the slice: x: 4 (x_hi: 2, x_lo: 2; x = x_hi * 2 + x_lo), y: 4, z: 4, core: 2. Of those that a mesh axis runs over, the one named last changes fastest.
Arguments:
- expert_hidden: bfloat16 [2, 64, 8192], P(None, None, 'ty'), may hold values from -400 to 400
- expert_gain: bfloat16 [8192], P('ty'), may hold values from 0.5 to 1.5
- expert_query: bfloat16 [8192, 8192], P('ty', 'tx'), may hold values from -0.0625 to 0.0625
- expert_keys: bfloat16 [8192, 1024], P('ty', 'tx'), may hold values from -0.25 to 0.25
- expert_values: bfloat16 [8192, 1024], P('ty', 'tx'), may hold values from -0.0625 to 0.0625
- expert_output: bfloat16 [8192, 8192], P('tx', 'ty'), may hold values from -0.25 to 0.25
- expert_final: bfloat16 [8192], P('ty'), may hold values from 0.5 to 1.5
- expert_head: bfloat16 [32000, 8192], P(('grp', 'tx'), 'ty'), may hold values from -400 to 400
- expert_keycache: bfloat16 [64, 1024, 1024], P(('grp', 'ty'), None, 'tx'), may hold values from -400 to 400
- expert_valcache: bfloat16 [64, 1024, 1024], P(('grp', 'ty'), None, 'tx'), may hold values from -6 to 6
- amateur_hidden: bfloat16 [2, 64, 4096], P(None, None, 'ty'), may hold values from -400 to 400
- amateur_gain: bfloat16 [4096], P('ty'), may hold values from 0.5 to 1.5
- amateur_query: bfloat16 [4096, 4096], P('ty', 'tx'), may hold values from -0.09375 to 0.09375
- amateur_keys: bfloat16 [4096, 4096], P('ty', 'tx'), may hold values from -0.375 to 0.375
- amateur_values: bfloat16 [4096, 4096], P('ty', 'tx'), may hold values from -0.09375 to 0.09375
- amateur_output: bfloat16 [4096, 4096], P('tx', 'ty'), may hold values from -0.375 to 0.375
- amateur_final: bfloat16 [4096], P('ty'), may hold values from 0.5 to 1.5
- amateur_head: bfloat16 [32000, 4096], P(('grp', 'tx'), 'ty'), may hold values from -400 to 400
- amateur_keycache: bfloat16 [64, 1024, 4096], P(('grp', 'ty'), None, 'tx'), may hold values from -400 to 400
- amateur_valcache: bfloat16 [64, 1024, 4096], P(('grp', 'ty'), None, 'tx'), may hold values from -6 to 6
- lengths: int32 [64], P(('grp', 'ty')), may hold values from 1 to 1022, as said below
- tokens: int32 [2, 64], P(None, 'ty'), may hold values from 0 to 31999
Outputs:
- contrast: float32 [2, 64, 32000], P(None, 'ty', ('grp', 'tx'))
- token_score: float32 [2, 64], P(None, 'ty')
The draws below stay inside these ranges and needn't reach their ends.
Inputs may be any that keep to these rules, and one draw needn't show every extreme that they name: Row r's prompt fills cache positions 0 to lengths[r] - 1; the later cache positions hold no data.
All inputs are finite; a program needn't handle non-finite values.
Results may differ from the reference program's by a relative error of at most 0.012.
The reference program's roundings to bfloat16 on the way count: a program that leaves them out, or rounds other values in their place, can miss the bound.
Values may be sent and summed in bfloat16 or wider, within the bound.
A program may use at most 128 MiB of HBM per device.

```python
import math
import jax
import jax.numpy as jnp
import numpy as np
from jax import lax

D = 8192
HEADS = 64
KV_HEADS = 8
HEAD_DIM = 128
VOCAB = 32000
DA = 4096
HEADS_A = 32
CACHE = 1024
STEPS = 2
ROWS = 64


def scaled_states(key, shape):
    key_noise, key_rows = jax.random.split(key, 2)
    feature_count = shape[-1]
    noise = jnp.clip(jax.random.normal(key_noise, shape, jnp.float32), -6.0, 6.0)
    rising = 3.0 ** (jnp.arange(feature_count, dtype=jnp.float32) / (feature_count - 1))
    row_scale = 10.0 ** jax.random.uniform(key_rows, shape[:-1] + (1,), jnp.float32)
    return 0.3 * noise * rising * row_scale


def spiky_keys(key, shape, spread):
    key_noise, key_rows = jax.random.split(key)
    noise = jnp.clip(jax.random.normal(key_noise, shape, jnp.float32), -6.0, 6.0) * 2.0
    row_scale = 10.0 ** (jax.random.uniform(key_rows, (shape[0], shape[1], 1), jnp.float32) * spread)
    return noise * row_scale


def vocab_rows(key, shape, spread):
    key_noise, key_rows = jax.random.split(key)
    noise = jnp.clip(jax.random.normal(key_noise, shape, jnp.float32), -6.0, 6.0) * (4.0 / shape[1] ** 0.5)
    row_scale = 10.0 ** (jax.random.uniform(key_rows, (shape[0], 1), jnp.float32) * spread)
    return noise * row_scale


def draw_expert_hidden(key, part):
    key = jax.random.fold_in(key, 11)
    return scaled_states(key, (STEPS, ROWS, D)).astype(jnp.bfloat16)


def draw_amateur_hidden(key, part):
    key = jax.random.fold_in(key, 12)
    return scaled_states(key, (STEPS, ROWS, DA)).astype(jnp.bfloat16)


def draw_expert_keycache(key, part):
    key = jax.random.fold_in(key, 21)
    return spiky_keys(key, (ROWS, CACHE, KV_HEADS * HEAD_DIM), 0.0).astype(jnp.bfloat16)


def draw_amateur_keycache(key, part):
    key = jax.random.fold_in(key, 22)
    return spiky_keys(key, (ROWS, CACHE, HEADS_A * HEAD_DIM), 0.0).astype(jnp.bfloat16)


def draw_expert_head(key, part):
    key = jax.random.fold_in(key, 31)
    return vocab_rows(key, (VOCAB, D), 0.0).astype(jnp.bfloat16)


def draw_amateur_head(key, part):
    key = jax.random.fold_in(key, 32)
    return vocab_rows(key, (VOCAB, DA), 0.0).astype(jnp.bfloat16)


def draw_lengths(key, part):
    key = jax.random.fold_in(key, 5)
    key_draw, key_pick = jax.random.split(key)
    drawn = jax.random.randint(key_draw, (ROWS,), 1, CACHE - STEPS + 1, dtype=jnp.int32)
    chosen = jax.random.randint(key_pick, (), 0, ROWS, dtype=jnp.int32)
    return jnp.where(jnp.arange(ROWS, dtype=jnp.int32) == chosen, CACHE - STEPS, drawn).astype(jnp.int32)


def plant(result, key, least, high):
    shape = result.shape
    index_at = [jax.random.randint(jax.random.fold_in(key, axis), (), 0, shape[axis]) for axis in range(len(shape))]
    result = result.at[tuple(index_at)].set(least)
    longest = shape.index(max(shape))
    index_at[longest] = (index_at[longest] + 1) % shape[longest]
    return result.at[tuple(index_at)].set(high)


def level_of(rng, extent, pieces, least, high):
    def one(position, shards_of):
        steps = jax.random.uniform(jax.random.fold_in(jax.random.fold_in(rng, 6), position), (shards_of,), jnp.float32, least / len(pieces), high / len(pieces))
        return jnp.repeat(jnp.exp(steps), extent[position] // shards_of).reshape((-1,) + (1,) * (len(extent) - position - 1))

    level = one(*pieces[0])
    for cut in pieces[1:]:
        level = level * one(*cut)
    return level


def rank_table(amount, lean):
    weights = [(1 << 20) // math.isqrt(rank ** lean) + 1 for rank in range(1, amount + 1)]
    scale = 1 + sum(weights) // (1 << 30)
    return np.cumsum(np.array([max(1, weight // scale) for weight in weights]))


def skewed_ids(rng, extent, count, slope):
    table = rank_table(count, slope)
    lot = jax.random.randint(jax.random.fold_in(rng, 1), extent, 0, int(table[count - 1]))
    rank = jnp.searchsorted(jnp.asarray(table, jnp.int32), lot, side="right")
    return jax.random.permutation(jax.random.fold_in(rng, 2), count)[rank].astype(jnp.int32)


def bell_draw(rng, shape, deviation, bound, pieces=(), kind=jnp.bfloat16):
    factor_of = level_of(rng, shape, pieces, -0.22, 0.18) if pieces else 1.0
    array = jax.random.normal(rng, shape, jnp.float32) * deviation * factor_of
    return jnp.minimum(jnp.maximum(array, -bound), bound).astype(kind)


def setup_inputs(seed: int = 0) -> dict:
    splits = jax.random.split(jax.random.key(seed), 23)
    return {
        "expert_hidden": draw_expert_hidden(jax.random.fold_in(splits[22], 71), 0),
        "expert_gain": jnp.clip(1.0 + 0.1 * jax.random.normal(splits[1], (D,), jnp.float32), 0.5, 1.5).astype(jnp.bfloat16),
        "expert_query": bell_draw(splits[2], (D, HEADS * HEAD_DIM), D ** -0.5, 0.0625, ((0, 8), (1, 8))),
        "expert_keys": bell_draw(splits[3], (D, KV_HEADS * HEAD_DIM), (D // 16) ** -0.5, 0.25, ((0, 8), (1, 8))),
        "expert_values": bell_draw(splits[4], (D, KV_HEADS * HEAD_DIM), D ** -0.5, 0.0625, ((0, 8), (1, 8))),
        "expert_output": bell_draw(splits[5], (HEADS * HEAD_DIM, D), (HEADS * HEAD_DIM // 16) ** -0.5, 0.25, ((0, 8), (1, 8))),
        "expert_final": jnp.clip(1.0 + 0.1 * jax.random.normal(splits[6], (D,), jnp.float32), 0.5, 1.5).astype(jnp.bfloat16),
        "expert_head": draw_expert_head(jax.random.fold_in(splits[22], 71), 0),
        "expert_keycache": draw_expert_keycache(jax.random.fold_in(splits[22], 71), 0),
        "expert_valcache": bell_draw(splits[9], (ROWS, CACHE, KV_HEADS * HEAD_DIM), 1.0, 6.0, ((0, 16), (2, 8))),
        "amateur_hidden": draw_amateur_hidden(jax.random.fold_in(splits[22], 71), 0),
        "amateur_gain": jnp.clip(1.0 + 0.1 * jax.random.normal(splits[11], (DA,), jnp.float32), 0.5, 1.5).astype(jnp.bfloat16),
        "amateur_query": bell_draw(splits[12], (DA, HEADS_A * HEAD_DIM), DA ** -0.5, 0.09375, ((0, 8), (1, 8))),
        "amateur_keys": bell_draw(splits[13], (DA, HEADS_A * HEAD_DIM), (DA // 16) ** -0.5, 0.375, ((0, 8), (1, 8))),
        "amateur_values": bell_draw(splits[14], (DA, HEADS_A * HEAD_DIM), DA ** -0.5, 0.09375, ((0, 8), (1, 8))),
        "amateur_output": bell_draw(splits[15], (HEADS_A * HEAD_DIM, DA), (HEADS_A * HEAD_DIM // 16) ** -0.5, 0.375, ((0, 8), (1, 8))),
        "amateur_final": jnp.clip(1.0 + 0.1 * jax.random.normal(splits[16], (DA,), jnp.float32), 0.5, 1.5).astype(jnp.bfloat16),
        "amateur_head": draw_amateur_head(jax.random.fold_in(splits[22], 71), 0),
        "amateur_keycache": draw_amateur_keycache(jax.random.fold_in(splits[22], 71), 0),
        "amateur_valcache": bell_draw(splits[19], (ROWS, CACHE, HEADS_A * HEAD_DIM), 1.0, 6.0, ((0, 16), (2, 8))),
        "lengths": draw_lengths(jax.random.fold_in(splits[22], 71), 0),
        "tokens": plant(skewed_ids(splits[21], (STEPS, ROWS), VOCAB, 2), jax.random.fold_in(splits[21], 3), 0, VOCAB - 1).astype(jnp.int32),
    }


epsilon = 1e-05
rope_base = 10000.0
amateur_weight = 0.5

def rotary(values, positions):
    half_dim = values.shape[-1] // 2
    exponent = jnp.arange(half_dim, dtype=jnp.float32) * (2.0 / values.shape[-1])
    frequency = rope_base ** (-exponent)
    angles = positions.astype(jnp.float32)[..., None, None] * frequency
    cosine = jnp.cos(angles)
    sine_part = jnp.sin(angles)
    front_part = values[..., :half_dim]
    back_part = values[..., half_dim:]
    return jnp.concatenate([front_part * cosine - back_part * sine_part, back_part * cosine + front_part * sine_part], axis=-1)

def rms_scale(values, norm_gain):
    mean_square = lax.optimization_barrier(jnp.mean(values * values, axis=-1, keepdims=True))
    return values * lax.rsqrt(mean_square + epsilon) * norm_gain.astype(jnp.float32)

def log_probs(hidden, norm_gain, query_weight, key_weight, value_weight, output_weight, final_gain, head_weight, keycache, valcache, lengths):
    step_count, row_count, feature_count = hidden.shape
    head_count = query_weight.shape[1] // HEAD_DIM
    key_heads = key_weight.shape[1] // HEAD_DIM
    group_size = head_count // key_heads
    cache_size = keycache.shape[1]
    inputs = hidden.astype(jnp.float32)
    normed = rms_scale(inputs, norm_gain).astype(jnp.bfloat16).reshape(step_count * row_count, feature_count)
    queries = jnp.dot(normed, query_weight, preferred_element_type=jnp.float32).reshape(step_count, row_count, head_count, HEAD_DIM)
    fresh_keys = jnp.dot(normed, key_weight, preferred_element_type=jnp.float32).reshape(step_count, row_count, key_heads, HEAD_DIM)
    fresh_values = jnp.dot(normed, value_weight, preferred_element_type=jnp.float32).reshape(step_count, row_count, key_heads, HEAD_DIM)
    positions = lengths[None, :] + jnp.arange(step_count, dtype=jnp.int32)[:, None]
    queries = rotary(queries, positions).astype(jnp.bfloat16).reshape(step_count, row_count, key_heads, group_size, HEAD_DIM)
    fresh_keys = rotary(fresh_keys, positions).astype(jnp.bfloat16)
    fresh_values = fresh_values.astype(jnp.bfloat16)
    score_scale = HEAD_DIM ** (-0.5)
    query_float = queries.astype(jnp.float32)
    past_keys = keycache.reshape(row_count, cache_size, key_heads, HEAD_DIM).astype(jnp.float32)
    past_values = valcache.reshape(row_count, cache_size, key_heads, HEAD_DIM).astype(jnp.float32)
    cache_scores = jnp.einsum('srkgd,rckd->srkgc', query_float, past_keys) * score_scale
    fresh_scores = jnp.einsum('srkgd,trkd->srkgt', query_float, fresh_keys.astype(jnp.float32)) * score_scale
    visible = (jnp.arange(cache_size, dtype=jnp.int32)[None, :] < lengths[:, None])[None, :, None, None, :]
    causal = (jnp.arange(step_count, dtype=jnp.int32)[None, :] <= jnp.arange(step_count, dtype=jnp.int32)[:, None])[:, None, None, None, :]
    cache_scores = jnp.where(visible, cache_scores, -jnp.inf)
    fresh_scores = jnp.where(causal, fresh_scores, -jnp.inf)
    peak_score = jnp.maximum(lax.optimization_barrier(jnp.max(cache_scores, axis=-1)), lax.optimization_barrier(jnp.max(fresh_scores, axis=-1)))[..., None]
    cache_exp = jnp.exp(cache_scores - peak_score)
    fresh_exp = jnp.exp(fresh_scores - peak_score)
    weight_total = lax.optimization_barrier(jnp.sum(cache_exp, axis=-1)) + lax.optimization_barrier(jnp.sum(fresh_exp, axis=-1))
    cache_weights = lax.optimization_barrier(cache_exp.astype(jnp.bfloat16)).astype(jnp.float32)
    fresh_weights = lax.optimization_barrier(fresh_exp.astype(jnp.bfloat16)).astype(jnp.float32)
    mixture = jnp.einsum('srkgc,rckd->srkgd', cache_weights, past_values)
    mixture = mixture + jnp.einsum('srkgt,trkd->srkgd', fresh_weights, fresh_values.astype(jnp.float32))
    attended = (mixture / weight_total[..., None]).astype(jnp.bfloat16).reshape(step_count * row_count, head_count * HEAD_DIM)
    projected = jnp.dot(attended, output_weight, preferred_element_type=jnp.float32)
    residual = inputs.reshape(step_count * row_count, feature_count) + projected
    final_rows = rms_scale(residual, final_gain).astype(jnp.bfloat16)
    logits = lax.dot_general(final_rows, head_weight, (((1,), (1,)), ((), ())), preferred_element_type=jnp.float32)
    peak_logit = lax.optimization_barrier(jnp.max(logits, axis=-1, keepdims=True))
    log_total = peak_logit + jnp.log(lax.optimization_barrier(jnp.sum(jnp.exp(logits - peak_logit), axis=-1, keepdims=True)))
    return (logits - log_total).reshape(step_count, row_count, -1)

def reference(expert_hidden, expert_gain, expert_query, expert_keys, expert_values, expert_output, expert_final, expert_head, expert_keycache, expert_valcache, amateur_hidden, amateur_gain, amateur_query, amateur_keys, amateur_values, amateur_output, amateur_final, amateur_head, amateur_keycache, amateur_valcache, lengths, tokens):
    expert_logp = log_probs(expert_hidden, expert_gain, expert_query, expert_keys, expert_values, expert_output, expert_final, expert_head, expert_keycache, expert_valcache, lengths)
    amateur_logp = log_probs(amateur_hidden, amateur_gain, amateur_query, amateur_keys, amateur_values, amateur_output, amateur_final, amateur_head, amateur_keycache, amateur_valcache, lengths)
    contrast = expert_logp - amateur_weight * amateur_logp
    token_score = jnp.take_along_axis(contrast, tokens[..., None], axis=-1)[..., 0]
    return (contrast, token_score)
```

```python
import functools
import math

import jax
import jax.numpy as jnp
from jax import lax
from jax.experimental import pallas as pl
from jax.experimental.pallas import tpu as pltpu
from jax.sharding import PartitionSpec as P

HEAD = 128
EPS = 1e-05
BASE = 10000.0
AMATEUR = 0.5
SCALE = HEAD**-0.5
CHUNK = 512
F32 = jnp.float32
BF16 = jnp.bfloat16
MESH = pl.DeviceIdType.MESH


def iota(shape, axis):
    return lax.broadcasted_iota(jnp.int32, shape, axis)


def mm(a, b):
    return lax.dot_general(a, b, (((1,), (0,)), ((), ())), preferred_element_type=F32)


def mm_t(a, b):
    return lax.dot_general(a, b, (((1,), (1,)), ((), ())), preferred_element_type=F32)


def one_hot(size, source):
    out = iota((size, size), 0)
    return jnp.where(iota((size, size), 1) == source(out), 1.0, 0.0).astype(BF16)


def folded(values):
    half = values.shape[-1] // 2
    return jnp.concatenate([values[..., :half], values[..., half:]], axis=-2)


def unfolded(values):
    return jnp.concatenate([values[..., :8, :], values[..., 8:, :]], axis=-1)


def lane_fold(values):
    total = values[:, :HEAD]
    for start in range(HEAD, values.shape[1], HEAD):
        total = total + values[:, start : start + HEAD]
    return total


def widen(column, width):
    return jnp.concatenate([column] * (width // HEAD), axis=1)


def kernel(axes, dims, *refs):
    n_grp, n_tx, n_ty = axes
    (
        hid_e, gain_e, wq_e, wk_e, wv_e, wo_e, fin_e, head_e, kc_e, vc_e,
        hid_a, gain_a, wq_a, wk_a, wv_a, wo_a, fin_a, head_a, kc_a, vc_a,
        lengths, tokens,
        out_ref, score_ref,
        v_hid_e, v_wq_e, v_wk_e, v_wv_e, v_wo_e, v_head_e, v_kc_e, v_vc_e,
        v_hid_a, v_wq_a, v_wk_a, v_wv_a, v_wo_a, v_head_a, v_kc_a, v_vc_a,
        x_e, x_a, sq_send, sq_recv,
        p_send_e, p_recv_e, p_send_a, p_recv_a,
        g_e, g_a,
        o_send_e, o_recv_e, o_send_a, o_recv_a,
        s_send_e, s_recv_e, s_send_a, s_recv_a,
        f_e, f_a, rows_e, rows_a,
        l_send, l_recv, t_send, t_recv,
        local_sem, ty_send, ty_recv, tx_send, tx_recv, fw_send, fw_recv, l_ssem, l_rsem, t_ssem, t_rsem,
    ) = refs
    grp, tx, ty = lax.axis_index("grp"), lax.axis_index("tx"), lax.axis_index("ty")
    half_rows = v_hid_e.shape[1]
    width_e, width_a = v_hid_e.shape[2], v_hid_a.shape[2]
    heads_e, heads_a = v_wq_e.shape[1] // HEAD, v_wq_a.shape[1] // HEAD
    vocab = head_e.shape[0]

    first = pl.multiple_of(grp * half_rows, half_rows)
    pairs = [
        (hid_e.at[:, pl.ds(first, half_rows)], v_hid_e),
        (hid_a.at[:, pl.ds(first, half_rows)], v_hid_a),
        (wq_e, v_wq_e), (wk_e, v_wk_e), (wv_e, v_wv_e),
        (wq_a, v_wq_a), (wk_a, v_wk_a), (wv_a, v_wv_a),
        (kc_e, v_kc_e), (vc_e, v_vc_e), (kc_a, v_kc_a), (vc_a, v_vc_a),
        (wo_e, v_wo_e), (wo_a, v_wo_a),
        (head_e, v_head_e.at[pl.ds(0, vocab)]), (head_a, v_head_a.at[pl.ds(0, vocab)]),
    ]
    loads = [
        pltpu.make_async_copy(source, target, local_sem.at[number])
        for number, (source, target) in enumerate(pairs)
    ]
    for load in loads:
        load.start()
    (l_hid_e, l_hid_a, l_wq_e, l_wk_e, l_wv_e, l_wq_a, l_wk_a, l_wv_a,
     l_kc_e, l_vc_e, l_kc_a, l_vc_a, l_wo_e, l_wo_a, l_head_e, l_head_a) = loads

    def ty_peer(step):
        return lax.rem(ty + step, n_ty)

    def tx_peer(step):
        return lax.rem(tx + step, n_tx)

    flat = grp * n_tx + tx
    n_flat = n_grp * n_tx

    def flat_peer(step):
        peer = lax.rem(flat + step, n_flat)
        return {"grp": peer // n_tx, "tx": lax.rem(peer, n_tx)}

    barrier = pltpu.get_barrier_semaphore()
    for step in range(1, n_ty):
        pl.semaphore_signal(barrier, inc=1, device_id={"ty": ty_peer(step)}, device_id_type=MESH)
    for step in range(1, n_flat):
        pl.semaphore_signal(barrier, inc=1, device_id=flat_peer(step), device_id_type=MESH)

    sent = []

    def push(source, target, send_sem, recv_sem, device):
        copy = pltpu.make_async_remote_copy(
            src_ref=source, dst_ref=target, send_sem=send_sem, recv_sem=recv_sem,
            device_id=device, device_id_type=MESH,
        )
        copy.start()
        sent.append(copy)
        return copy

    n_rows = 2 * half_rows
    block = half_rows // n_ty
    order = one_hot(
        n_rows, lambda o: (o // block) % 2 * half_rows + o // (2 * block) * block + o % block
    )
    l_hid_e.wait()
    wide_e = mm(order, v_hid_e[...].reshape(n_rows, width_e))
    x_e[...] = wide_e.reshape(n_ty, 8, width_e)
    l_hid_a.wait()
    wide_a = mm(order, v_hid_a[...].reshape(n_rows, width_a))
    x_a[...] = wide_a.reshape(n_ty, 8, width_a)
    partial = jnp.concatenate([lane_fold(wide_e * wide_e), lane_fold(wide_a * wide_a)], axis=0)
    own = jnp.broadcast_to(jnp.sum(partial.T, axis=0, keepdims=True), (8, HEAD))
    sq_send[...] = own

    pl.semaphore_wait(barrier, n_ty - 1 + n_flat - 1)

    copies = [
        push(sq_send, sq_recv.at[step], ty_send.at[0, step], ty_recv.at[0, step], {"ty": ty_peer(step)})
        for step in range(1, n_ty)
    ]

    row8, lane8 = iota((8, HEAD), 0), iota((8, HEAD), 1)
    position = jnp.zeros((8, HEAD), jnp.int32)
    for i in range(block):
        position = jnp.where(row8 % block == i, lengths[i], position)
    position = (position + row8 // block).astype(F32)
    exponent = (lane8 % (HEAD // 2)).astype(F32) * (2.0 / HEAD)
    angle = position * jnp.exp(exponent * (-math.log(BASE)))
    cosine = jnp.cos(angle)
    sine = jnp.where(lane8 < HEAD // 2, -1.0, 1.0) * jnp.sin(angle)

    def rotated(values):
        turned = jnp.concatenate([values[:, HEAD // 2 :], values[:, : HEAD // 2]], axis=1)
        return values * cosine + turned * sine

    total = own
    for copy, step in zip(copies, range(1, n_ty)):
        copy.wait_recv()
        total = total + sq_recv[step]
    square = jnp.broadcast_to(total[0:1], (HEAD, HEAD)).T
    root_e = lax.rsqrt(square[:n_rows] / (width_e * n_ty) + EPS)
    root_a = lax.rsqrt(square[n_rows:] / (width_a * n_ty) + EPS)

    def project(x, root, gain, weights, send, recv, kind):
        width = x.shape[2]
        values = x[...].reshape(n_rows, width)
        normed = (values * widen(root, width) * gain[...].astype(F32).reshape(1, width)).astype(BF16)
        start = 0
        for load, weight in weights:
            load.wait()
            columns = weight.shape[1]
            for at in range(0, columns, CHUNK):
                size = min(CHUNK, columns - at)
                part = mm(normed, weight[:, at : at + size])
                send[:, :, start : start + size] = part.reshape(n_ty, 8, size)
                start += size
        return [
            push(send.at[ty_peer(step)], recv.at[step], ty_send.at[kind, step], ty_recv.at[kind, step],
                 {"ty": ty_peer(step)})
            for step in range(1, n_ty)
        ]

    sent_pe = project(x_e, root_e, gain_e, ((l_wq_e, v_wq_e), (l_wk_e, v_wk_e), (l_wv_e, v_wv_e)), p_send_e, p_recv_e, 1)
    sent_pa = project(x_a, root_a, gain_a, ((l_wq_a, v_wq_a), (l_wk_a, v_wk_a), (l_wv_a, v_wv_a)), p_send_a, p_recv_a, 2)

    def summed(copies, send, recv, me):
        total = send[me]
        for copy, step in zip(copies, range(1, n_ty)):
            copy.wait_recv()
            total = total + recv[step]
        return total

    def padded(rows, size):
        if rows.shape[0] == size:
            return rows
        return jnp.concatenate([rows, jnp.zeros((size - rows.shape[0], rows.shape[1]), F32)], axis=0)

    def attend(acc, heads, key_heads, k_load, keys, v_load, values):
        group = heads // key_heads
        n_query = heads * 8
        per_row = 2 * heads
        cache = keys.shape[1]
        wide = key_heads * HEAD
        query = jnp.concatenate([rotated(acc[:, h * HEAD : (h + 1) * HEAD]) for h in range(heads)], axis=0)
        at = heads * HEAD
        fresh_k = jnp.concatenate(
            [rotated(acc[:, at + h * HEAD : at + (h + 1) * HEAD]) for h in range(key_heads)], axis=0
        )
        at += wide
        fresh_v = jnp.concatenate(
            [acc[:, at + h * HEAD : at + (h + 1) * HEAD] for h in range(key_heads)], axis=0
        )
        fresh_k = padded(fresh_k, HEAD).astype(BF16)
        fresh_v = padded(fresh_v, HEAD).astype(BF16)
        forth = one_hot(n_query, lambda o: o % heads * 8 + o // heads % 2 * block + o // per_row)
        back = one_hot(n_query, lambda o: o % block * per_row + o // block % 2 * heads + o // 8)
        query = mm(forth, query.astype(BF16))
        owner = iota((n_query, HEAD), 0)
        lane = iota((n_query, HEAD), 1)
        fresh = mm_t(query.astype(BF16), fresh_k) * SCALE
        seen = (
            (lane < key_heads * 8)
            & (lane // 8 == owner % heads // group)
            & (lane % block == owner // per_row)
            & (lane // block % 2 <= owner // heads % 2)
        )
        fresh = jnp.where(seen, fresh, -jnp.inf)
        if key_heads > 1:
            spread = widen(query, wide)
            keep = iota((n_query, wide), 1) // HEAD == iota((n_query, wide), 0) % heads // group
            query = jnp.where(keep, spread, 0.0)
        k_load.wait()
        cached = []
        for i in range(block):
            part = query[i * per_row : (i + 1) * per_row].astype(BF16)
            score = mm_t(part, keys[i]) * SCALE
            cached.append(jnp.where(iota((per_row, cache), 1) < lengths[i], score, -jnp.inf))
        cached = jnp.concatenate(cached, axis=0)
        peak = jnp.maximum(jnp.max(cached, axis=1, keepdims=True), jnp.max(fresh, axis=1, keepdims=True))
        cached = jnp.exp(cached - peak)
        fresh = jnp.exp(fresh - peak)
        total = jnp.sum(cached, axis=1, keepdims=True) + jnp.sum(fresh, axis=1, keepdims=True)
        v_load.wait()
        mixture = jnp.concatenate(
            [mm(cached[i * per_row : (i + 1) * per_row].astype(BF16), values[i]) for i in range(block)], axis=0
        )
        if key_heads > 1:
            picked = jnp.zeros((n_query, HEAD), F32)
            for h in range(key_heads):
                picked = picked + jnp.where(owner % heads // group == h, mixture[:, h * HEAD : (h + 1) * HEAD], 0.0)
            mixture = picked
        mixture = mixture + mm(fresh.astype(BF16), fresh_v)
        ready = mm(back, (mixture / total).astype(BF16))
        return jnp.concatenate([ready[h * 8 : (h + 1) * 8] for h in range(heads)], axis=1)

    def gather(rows, buffer, kind):
        buffer[ty] = folded(rows).astype(BF16)
        return [
            push(buffer.at[ty], buffer.at[ty], ty_send.at[kind, step], ty_recv.at[kind, step], {"ty": ty_peer(step)})
            for step in range(1, n_ty)
        ]

    acc = summed(sent_pe, p_send_e, p_recv_e, ty)
    sent_ge = gather(attend(acc, heads_e, v_wk_e.shape[1] // HEAD, l_kc_e, v_kc_e, l_vc_e, v_vc_e), g_e, 3)
    acc = summed(sent_pa, p_send_a, p_recv_a, ty)
    sent_ga = gather(attend(acc, heads_a, v_wk_a.shape[1] // HEAD, l_kc_a, v_kc_a, l_vc_a, v_vc_a), g_a, 4)

    def output(copies, buffer, load, weight, send, recv, kind):
        for copy in copies:
            copy.wait_recv()
        rows = unfolded(buffer[...].astype(F32)).reshape(n_rows, weight.shape[0]).astype(BF16)
        load.wait()
        columns = weight.shape[1]
        for at in range(0, columns, CHUNK):
            part = mm(rows, weight[:, at : at + CHUNK])
            send[:, :, at : at + CHUNK] = part.reshape(n_tx, 8, CHUNK)
        return [
            push(send.at[tx_peer(step)], recv.at[step], tx_send.at[kind, step], tx_recv.at[kind, step],
                 {"tx": tx_peer(step)})
            for step in range(1, n_tx)
        ]

    sent_oe = output(sent_ge, g_e, l_wo_e, v_wo_e, o_send_e, o_recv_e, 0)
    sent_oa = output(sent_ga, g_a, l_wo_a, v_wo_a, o_send_a, o_recv_a, 1)

    def residual(copies, x, send, recv, s_send, s_recv, kind):
        values = x[tx] + summed(copies, send, recv, tx)
        part = lane_fold(values * values)
        s_send[...] = part
        return values, part, [
            push(s_send, s_recv.at[step], ty_send.at[kind, step], ty_recv.at[kind, step], {"ty": ty_peer(step)})
            for step in range(1, n_ty)
        ]

    res_e, part_e, sent_se = residual(sent_oe, x_e, o_send_e, o_recv_e, s_send_e, s_recv_e, 5)
    res_a, part_a, sent_sa = residual(sent_oa, x_a, o_send_a, o_recv_a, s_send_a, s_recv_a, 6)

    partner = {"grp": 1 - grp}

    def final(values, part, copies, s_recv, gain, buffer, kind):
        width = values.shape[1]
        for copy, step in zip(copies, range(1, n_ty)):
            copy.wait_recv()
            part = part + s_recv[step]
        mean = jnp.sum(part, axis=1, keepdims=True) / (width * n_ty)
        rows = values * lax.rsqrt(mean + EPS) * gain[...].astype(F32).reshape(1, width)
        buffer[flat] = folded(rows).astype(BF16)
        across = [
            push(buffer.at[flat], buffer.at[flat], tx_send.at[kind, step], tx_recv.at[kind, step], {"tx": tx_peer(step)})
            for step in range(1, n_tx)
        ]
        forward = [
            push(buffer.at[flat], buffer.at[flat], fw_send.at[kind - 2, 0], fw_recv.at[kind - 2, 0], partner)
        ]
        return across, forward

    def pass_on(across, forward, buffer, kind):
        for copy, step in zip(across, range(1, n_tx)):
            copy.wait_recv()
            source = grp * n_tx + lax.rem(tx + n_tx - step, n_tx)
            forward.append(
                push(buffer.at[source], buffer.at[source], fw_send.at[kind - 2, step], fw_recv.at[kind - 2, step], partner)
            )

    def collect(forward, buffer, rows):
        for copy in forward:
            copy.wait_recv()
        rows[...] = unfolded(buffer[...].astype(F32)).reshape(rows.shape).astype(BF16)

    across_e, forward_e = final(res_e, part_e, sent_se, s_recv_e, fin_e, f_e, 2)
    across_a, forward_a = final(res_a, part_a, sent_sa, s_recv_a, fin_a, f_a, 3)

    padding = v_head_e.shape[0] - vocab
    l_head_e.wait()
    v_head_e[pl.ds(vocab, padding), :] = jnp.zeros((padding, width_e), BF16)
    l_head_a.wait()
    v_head_a[pl.ds(vocab, padding), :] = jnp.zeros((padding, width_a), BF16)

    n_chunk = v_head_e.shape[0] // CHUNK
    logit_copies = []

    def logits(rows, head, base):
        for c in range(n_chunk):
            part = mm_t(rows[...], head[pl.ds(c * CHUNK, CHUNK), :])
            l_send[base + c] = part.reshape(n_ty, 16, CHUNK).astype(BF16)
            for step in range(1, n_ty):
                logit_copies.append(
                    push(l_send.at[base + c, ty_peer(step)], l_recv.at[base + c, step],
                         l_ssem.at[base + c, step], l_rsem.at[base + c, step], {"ty": ty_peer(step)})
                )

    pass_on(across_e, forward_e, f_e, 2)
    collect(forward_e, f_e, rows_e)
    logits(rows_e, v_head_e, 0)
    pass_on(across_a, forward_a, f_a, 3)
    collect(forward_a, f_a, rows_a)
    logits(rows_a, v_head_a, n_chunk)

    def chunk_sum(c):
        total = l_send[c, ty].astype(F32)
        for step in range(1, n_ty):
            logit_copies[c * (n_ty - 1) + step - 1].wait_recv()
            total = total + l_recv[c, step].astype(F32)
        return total

    lane_c = iota((16, CHUNK), 1)

    def peak_and_total(parts):
        masked = [jnp.where(lane_c + c * CHUNK < vocab, part, -jnp.inf) for c, part in enumerate(parts)]
        peak = masked[0]
        for part in masked[1:]:
            peak = jnp.maximum(peak, part)
        peak = jnp.max(peak, axis=1, keepdims=True)
        total = jnp.exp(masked[0] - peak)
        for part in masked[1:]:
            total = total + jnp.exp(part - peak)
        return peak, jnp.sum(total, axis=1, keepdims=True)

    row16 = iota((16, HEAD), 0)
    token = jnp.zeros((16, HEAD), jnp.int32)
    for s in range(2):
        for r in range(8):
            token = jnp.where(row16 == r // block * 8 + s * block + r % block, tokens[s, r], token)
    token = widen(token - flat * vocab, CHUNK)

    expert = [chunk_sum(c) for c in range(n_chunk)]
    peak_e, total_e = peak_and_total(expert)
    amateur = [chunk_sum(n_chunk + c) for c in range(n_chunk)]
    peak_a, total_a = peak_and_total(amateur)
    chosen = jnp.zeros((16, CHUNK), F32)
    mixed = []
    for c in range(n_chunk):
        mixed.append(expert[c] - AMATEUR * amateur[c])
        column = lane_c + c * CHUNK
        chosen = chosen + jnp.where((column == token) & (column < vocab), mixed[c], 0.0)
    chosen = jnp.sum(chosen, axis=1, keepdims=True)

    lane16 = iota((16, HEAD), 1) % 64
    tile = jnp.where(lane16 == 0, peak_e, jnp.where(lane16 == 1, total_e, 0.0))
    tile = jnp.where(lane16 == 2, peak_a, jnp.where(lane16 == 3, total_a, tile))
    tile = jnp.where(lane16 == 4, chosen, tile)
    tile = jnp.where(lane8 < 64, tile[:8], tile[8:])
    t_send[...] = tile
    copies = [
        push(t_send, t_recv.at[step], t_ssem.at[step], t_rsem.at[step], flat_peer(step)) for step in range(1, n_flat)
    ]
    for copy in copies:
        copy.wait_recv()
    tiles = [tile] + [t_recv[step] for step in range(1, n_flat)]
    highest = functools.reduce(jnp.maximum, tiles)
    picked = functools.reduce(jnp.add, tiles)

    def shifted(values):
        return jnp.concatenate([values[:, 1:], values[:, :1]], axis=1)

    summed_up = functools.reduce(jnp.add, [jnp.exp(t - highest) * shifted(t) for t in tiles])
    log_total = highest + jnp.log(summed_up)

    def column(values, lane):
        return jnp.concatenate([values[:, lane : lane + 1], values[:, lane + 64 : lane + 65]], axis=0)

    offset = column(log_total, 0) - AMATEUR * column(log_total, 2)
    for c in range(n_chunk):
        size = min(CHUNK, vocab - c * CHUNK)
        contrast = mixed[c] - offset
        for s in range(2):
            low = s * block
            out_ref[s, :, c * CHUNK : c * CHUNK + size] = jnp.concatenate(
                [contrast[low : low + block], contrast[8 + low : 8 + low + block]], axis=0
            )[:, :size]
    value = jnp.broadcast_to(column(picked, 4) - offset, (16, HEAD))
    lane_r = iota((16, HEAD), 1)
    for s in range(2):
        mine = row16 == lane_r // block * 8 + s * block + lane_r % block
        line = jnp.sum(jnp.where(mine & (lane_r < 8), value, 0.0), axis=0, keepdims=True)
        score_ref[s : s + 1, :] = line[:, :8]

    for copy in sent:
        copy.wait_send()


def on_device(axes, *args):
    (
        hid_e, gain_e, wq_e, wk_e, wv_e, wo_e, fin_e, head_e, kc_e, vc_e,
        hid_a, gain_a, wq_a, wk_a, wv_a, wo_a, fin_a, head_a, kc_a, vc_a,
        lengths, tokens,
    ) = args
    n_grp, n_tx, n_ty = axes
    n_flat = n_grp * n_tx
    half = hid_e.shape[1] // n_grp
    vocab = head_e.shape[0]
    padded = -(-vocab // CHUNK) * CHUNK
    n_chunk = padded // CHUNK
    n_rows = 2 * half
    width_e, width_a = hid_e.shape[2], hid_a.shape[2]
    cols_e = wq_e.shape[1] + wk_e.shape[1] + wv_e.shape[1]
    cols_a = wq_a.shape[1] + wk_a.shape[1] + wv_a.shape[1]
    inner_e, inner_a = wo_e.shape[0], wo_a.shape[0]

    def like(array):
        return pltpu.VMEM(array.shape, array.dtype)

    scratch = []
    for hid, wq, wk, wv, wo, head, kc, vc in (
        (hid_e, wq_e, wk_e, wv_e, wo_e, head_e, kc_e, vc_e),
        (hid_a, wq_a, wk_a, wv_a, wo_a, head_a, kc_a, vc_a),
    ):
        scratch += [
            pltpu.VMEM((2, half, hid.shape[2]), BF16), like(wq), like(wk), like(wv), like(wo),
            pltpu.VMEM((padded, head.shape[1]), BF16), like(kc), like(vc),
        ]
    scratch += [
        pltpu.VMEM((n_ty, 8, width_e), F32), pltpu.VMEM((n_ty, 8, width_a), F32),
        pltpu.VMEM((8, HEAD), F32), pltpu.VMEM((n_ty, 8, HEAD), F32),
        pltpu.VMEM((n_ty, 8, cols_e), F32), pltpu.VMEM((n_ty, 8, cols_e), F32),
        pltpu.VMEM((n_ty, 8, cols_a), F32), pltpu.VMEM((n_ty, 8, cols_a), F32),
        pltpu.VMEM((n_ty, 16, inner_e // 2), BF16), pltpu.VMEM((n_ty, 16, inner_a // 2), BF16),
        pltpu.VMEM((n_tx, 8, width_e), F32), pltpu.VMEM((n_tx, 8, width_e), F32),
        pltpu.VMEM((n_tx, 8, width_a), F32), pltpu.VMEM((n_tx, 8, width_a), F32),
        pltpu.VMEM((8, HEAD), F32), pltpu.VMEM((n_ty, 8, HEAD), F32),
        pltpu.VMEM((8, HEAD), F32), pltpu.VMEM((n_ty, 8, HEAD), F32),
        pltpu.VMEM((n_flat, 16, width_e // 2), BF16), pltpu.VMEM((n_flat, 16, width_a // 2), BF16),
        pltpu.VMEM((n_flat * 8, width_e), BF16), pltpu.VMEM((n_flat * 8, width_a), BF16),
        pltpu.VMEM((2 * n_chunk, n_ty, 16, CHUNK), BF16), pltpu.VMEM((2 * n_chunk, n_ty, 16, CHUNK), BF16),
        pltpu.VMEM((8, HEAD), F32), pltpu.VMEM((n_flat, 8, HEAD), F32),
        pltpu.SemaphoreType.DMA((16,)),
        pltpu.SemaphoreType.DMA((7, n_ty)), pltpu.SemaphoreType.DMA((7, n_ty)),
        pltpu.SemaphoreType.DMA((4, n_tx)), pltpu.SemaphoreType.DMA((4, n_tx)),
        pltpu.SemaphoreType.DMA((2, n_tx)), pltpu.SemaphoreType.DMA((2, n_tx)),
        pltpu.SemaphoreType.DMA((2 * n_chunk, n_ty)), pltpu.SemaphoreType.DMA((2 * n_chunk, n_ty)),
        pltpu.SemaphoreType.DMA((n_flat,)), pltpu.SemaphoreType.DMA((n_flat,)),
    ]
    hbm = pl.BlockSpec(memory_space=pl.ANY)
    vmem = pl.BlockSpec(memory_space=pltpu.VMEM)
    smem = pl.BlockSpec(memory_space=pltpu.SMEM)
    model = [hbm, vmem, hbm, hbm, hbm, hbm, vmem, hbm, hbm, hbm]
    macs = n_rows * (width_e * (cols_e + inner_e) + width_a * (cols_a + inner_a)) + 2 * n_rows * vocab * (width_e + width_a)
    read = sum(array.size * array.dtype.itemsize for array in args)
    return pl.pallas_call(
        functools.partial(kernel, axes, None),
        out_shape=(
            jax.ShapeDtypeStruct((2, hid_e.shape[1] // n_ty, vocab), F32),
            jax.ShapeDtypeStruct((2, hid_e.shape[1] // n_ty), F32),
        ),
        in_specs=model + model + [smem, smem],
        out_specs=(vmem, vmem),
        scratch_shapes=scratch,
        compiler_params=pltpu.CompilerParams(
            collective_id=0, has_side_effects=True, vmem_limit_bytes=56 * 1024 * 1024
        ),
        cost_estimate=pl.CostEstimate(flops=2 * macs, bytes_accessed=read, transcendentals=0),
        name="contrast",
    )(*args)


def solution(mesh):
    model = (
        P(None, None, "ty"), P("ty"), P("ty", "tx"), P("ty", "tx"), P("ty", "tx"), P("tx", "ty"), P("ty"),
        P(("grp", "tx"), "ty"), P(("grp", "ty"), None, "tx"), P(("grp", "ty"), None, "tx"),
    )
    axes = tuple(mesh.shape[name] for name in ("grp", "tx", "ty"))
    return jax.shard_map(
        functools.partial(on_device, axes),
        mesh=mesh,
        in_specs=model + model + (P(("grp", "ty")), P(None, "ty")),
        out_specs=(P(None, "ty", ("grp", "tx")), P(None, "ty")),
        check_vma=False,
    )
```

```python
import functools
import math

import jax
import jax.numpy as jnp
from jax import lax
from jax.experimental import pallas as pl
from jax.experimental.pallas import tpu as pltpu
from jax.sharding import PartitionSpec as P

HEAD = 128
EPS = 1e-05
BASE = 10000.0
AMATEUR = 0.5
SCALE = HEAD**-0.5
CHUNK = 512
F32 = jnp.float32
BF16 = jnp.bfloat16
MESH = pl.DeviceIdType.MESH


def iota(shape, axis):
    return lax.broadcasted_iota(jnp.int32, shape, axis)


def mm(a, b):
    return lax.dot_general(a, b, (((1,), (0,)), ((), ())), preferred_element_type=F32)


def mm_t(a, b):
    return lax.dot_general(a, b, (((1,), (1,)), ((), ())), preferred_element_type=F32)


def one_hot(size, source):
    out = iota((size, size), 0)
    return jnp.where(iota((size, size), 1) == source(out), 1.0, 0.0).astype(BF16)


def folded(values):
    half = values.shape[-1] // 2
    return jnp.concatenate([values[..., :half], values[..., half:]], axis=-2)


def unfolded(values):
    return jnp.concatenate([values[..., :8, :], values[..., 8:, :]], axis=-1)


def lane_fold(values):
    total = values[:, :HEAD]
    for start in range(HEAD, values.shape[1], HEAD):
        total = total + values[:, start : start + HEAD]
    return total


def widen(column, width):
    return jnp.concatenate([column] * (width // HEAD), axis=1)


def kernel(axes, dims, *refs):
    n_grp, n_tx, n_ty = axes
    (
        hid_e, gain_e, wq_e, wk_e, wv_e, wo_e, fin_e, head_e, kc_e, vc_e,
        hid_a, gain_a, wq_a, wk_a, wv_a, wo_a, fin_a, head_a, kc_a, vc_a,
        h_lengths, h_tokens,
        out_ref, score_ref,
        lengths, tokens, v_gain_e, v_fin_e, v_gain_a, v_fin_a,
        v_hid_e, v_wq_e, v_wk_e, v_wv_e, v_wo_e, v_head_e, v_kc_e, v_vc_e,
        v_hid_a, v_wq_a, v_wk_a, v_wv_a, v_wo_a, v_head_a, v_kc_a, v_vc_a,
        x_e, x_a, sq_send, sq_recv,
        p_send_e, p_recv_e, p_send_a, p_recv_a,
        g_e, g_a,
        o_send_e, o_recv_e, o_send_a, o_recv_a,
        s_send_e, s_recv_e, s_send_a, s_recv_a,
        f_e, f_a, rows_e, rows_a,
        l_send, l_recv, t_send, t_recv,
        local_sem, ty_send, ty_recv, tx_send, tx_recv, fw_send, fw_recv, l_ssem, l_rsem, t_ssem, t_rsem,
    ) = refs
    grp, tx, ty = lax.axis_index("grp"), lax.axis_index("tx"), lax.axis_index("ty")
    half_rows = v_hid_e.shape[1]
    width_e, width_a = v_hid_e.shape[2], v_hid_a.shape[2]
    heads_e, heads_a = v_wq_e.shape[1] // HEAD, v_wq_a.shape[1] // HEAD
    vocab = head_e.shape[0]

    first = pl.multiple_of(grp * half_rows, half_rows)
    pairs = [
        (hid_e.at[:, pl.ds(first, half_rows)], v_hid_e),
        (hid_a.at[:, pl.ds(first, half_rows)], v_hid_a),
        (h_lengths, lengths), (gain_e, v_gain_e), (gain_a, v_gain_a),
        (fin_e, v_fin_e), (fin_a, v_fin_a), (h_tokens, tokens),
        (wq_e, v_wq_e), (wk_e, v_wk_e), (wv_e, v_wv_e),
        (wq_a, v_wq_a), (wk_a, v_wk_a), (wv_a, v_wv_a),
        (kc_e, v_kc_e), (vc_e, v_vc_e), (kc_a, v_kc_a), (vc_a, v_vc_a),
        (wo_e, v_wo_e), (wo_a, v_wo_a),
        (head_e, v_head_e.at[pl.ds(0, vocab)]), (head_a, v_head_a.at[pl.ds(0, vocab)]),
    ]
    loads = [
        pltpu.make_async_copy(source, target, local_sem.at[number])
        for number, (source, target) in enumerate(pairs)
    ]
    for load in loads[:8]:
        load.start()
    (l_hid_e, l_hid_a, l_lengths, l_gain_e, l_gain_a, l_fin_e, l_fin_a, l_tokens, l_wq_e, l_wk_e, l_wv_e, l_wq_a, l_wk_a, l_wv_a,
     l_kc_e, l_vc_e, l_kc_a, l_vc_a, l_wo_e, l_wo_a, l_head_e, l_head_a) = loads

    def ty_peer(step):
        return lax.rem(ty + step, n_ty)

    def tx_peer(step):
        return lax.rem(tx + step, n_tx)

    flat = grp * n_tx + tx
    n_flat = n_grp * n_tx

    def flat_peer(step):
        peer = lax.rem(flat + step, n_flat)
        return {"grp": peer // n_tx, "tx": lax.rem(peer, n_tx)}

    barrier = pltpu.get_barrier_semaphore()
    for step in range(1, n_ty):
        pl.semaphore_signal(barrier, inc=1, device_id={"ty": ty_peer(step)}, device_id_type=MESH)
    for step in range(1, n_flat):
        pl.semaphore_signal(barrier, inc=1, device_id=flat_peer(step), device_id_type=MESH)

    for load in loads[8:14]:
        load.start()

    sent = []

    def push(source, target, send_sem, recv_sem, device):
        copy = pltpu.make_async_remote_copy(
            src_ref=source, dst_ref=target, send_sem=send_sem, recv_sem=recv_sem,
            device_id=device, device_id_type=MESH,
        )
        copy.start()
        sent.append(copy)
        return copy

    n_rows = 2 * half_rows
    block = half_rows // n_ty
    order = one_hot(
        n_rows, lambda o: (o // block) % 2 * half_rows + o // (2 * block) * block + o % block
    )
    l_hid_e.wait()
    wide_e = mm(order, v_hid_e[...].reshape(n_rows, width_e))
    x_e[...] = wide_e.reshape(n_ty, 8, width_e)
    l_hid_a.wait()
    wide_a = mm(order, v_hid_a[...].reshape(n_rows, width_a))
    x_a[...] = wide_a.reshape(n_ty, 8, width_a)
    partial = jnp.concatenate([lane_fold(wide_e * wide_e), lane_fold(wide_a * wide_a)], axis=0)
    own = jnp.broadcast_to(jnp.sum(partial.T, axis=0, keepdims=True), (8, HEAD))
    sq_send[...] = own

    pl.semaphore_wait(barrier, n_ty - 1 + n_flat - 1)

    copies = [
        push(sq_send, sq_recv.at[step], ty_send.at[0, step], ty_recv.at[0, step], {"ty": ty_peer(step)})
        for step in range(1, n_ty)
    ]

    for load in loads[14:18]:
        load.start()

    row8, lane8 = iota((8, HEAD), 0), iota((8, HEAD), 1)
    position = jnp.zeros((8, HEAD), jnp.int32)
    l_lengths.wait()
    for i in range(block):
        position = jnp.where(row8 % block == i, lengths[i], position)
    position = (position + row8 // block).astype(F32)
    exponent = (lane8 % (HEAD // 2)).astype(F32) * (2.0 / HEAD)
    angle = position * jnp.exp(exponent * (-math.log(BASE)))
    cosine = jnp.cos(angle)
    sine = jnp.where(lane8 < HEAD // 2, -1.0, 1.0) * jnp.sin(angle)

    def rotated(values):
        turned = jnp.concatenate([values[:, HEAD // 2 :], values[:, : HEAD // 2]], axis=1)
        return values * cosine + turned * sine

    total = own
    for copy, step in zip(copies, range(1, n_ty)):
        copy.wait_recv()
        total = total + sq_recv[step]
    square = jnp.broadcast_to(total[0:1], (HEAD, HEAD)).T
    root_e = lax.rsqrt(square[:n_rows] / (width_e * n_ty) + EPS)
    root_a = lax.rsqrt(square[n_rows:] / (width_a * n_ty) + EPS)

    def project(x, root, g_load, gain, weights, send, recv, kind):
        width = x.shape[2]
        g_load.wait()
        values = x[...].reshape(n_rows, width)
        normed = (values * widen(root, width) * gain[...].astype(F32).reshape(1, width)).astype(BF16)
        parts = []
        for load, weight in weights:
            load.wait()
            columns = weight.shape[1]
            for at in range(0, columns, CHUNK):
                parts.append(mm(normed, weight[:, at : at + min(CHUNK, columns - at)]))
        send[...] = folded(jnp.concatenate(parts, axis=1).reshape(n_ty, 8, 2 * send.shape[2])).astype(BF16)
        return [
            push(send.at[ty_peer(step)], recv.at[step], ty_send.at[kind, step], ty_recv.at[kind, step],
                 {"ty": ty_peer(step)})
            for step in range(1, n_ty)
        ]

    sent_pe = project(x_e, root_e, l_gain_e, v_gain_e, ((l_wq_e, v_wq_e), (l_wk_e, v_wk_e), (l_wv_e, v_wv_e)), p_send_e, p_recv_e, 1)
    sent_pa = project(x_a, root_a, l_gain_a, v_gain_a, ((l_wq_a, v_wq_a), (l_wk_a, v_wk_a), (l_wv_a, v_wv_a)), p_send_a, p_recv_a, 2)

    for load in loads[18:]:
        load.start()

    def summed(copies, send, recv, me):
        total = send[me].astype(F32)
        for copy, step in zip(copies, range(1, n_ty)):
            copy.wait_recv()
            total = total + recv[step].astype(F32)
        return unfolded(total)

    def padded(rows, size):
        if rows.shape[0] == size:
            return rows
        return jnp.concatenate([rows, jnp.zeros((size - rows.shape[0], rows.shape[1]), F32)], axis=0)

    def attend(acc, heads, key_heads, k_load, keys, v_load, values):
        group = heads // key_heads
        n_query = heads * 8
        per_row = 2 * heads
        cache = keys.shape[1]
        wide = key_heads * HEAD
        query = jnp.concatenate([rotated(acc[:, h * HEAD : (h + 1) * HEAD]) for h in range(heads)], axis=0)
        at = heads * HEAD
        fresh_k = jnp.concatenate(
            [rotated(acc[:, at + h * HEAD : at + (h + 1) * HEAD]) for h in range(key_heads)], axis=0
        )
        at += wide
        fresh_v = jnp.concatenate(
            [acc[:, at + h * HEAD : at + (h + 1) * HEAD] for h in range(key_heads)], axis=0
        )
        fresh_k = padded(fresh_k, HEAD).astype(BF16)
        fresh_v = padded(fresh_v, HEAD).astype(BF16)
        forth = one_hot(n_query, lambda o: o % heads * 8 + o // heads % 2 * block + o // per_row)
        back = one_hot(n_query, lambda o: o % block * per_row + o // block % 2 * heads + o // 8)
        query = mm(forth, query.astype(BF16))
        owner = iota((n_query, HEAD), 0)
        lane = iota((n_query, HEAD), 1)
        fresh = mm_t(query.astype(BF16), fresh_k) * SCALE
        seen = (
            (lane < key_heads * 8)
            & (lane // 8 == owner % heads // group)
            & (lane % block == owner // per_row)
            & (lane // block % 2 <= owner // heads % 2)
        )
        fresh = jnp.where(seen, fresh, -jnp.inf)
        if key_heads > 1:
            spread = widen(query, wide)
            keep = iota((n_query, wide), 1) // HEAD == iota((n_query, wide), 0) % heads // group
            query = jnp.where(keep, spread, 0.0)
        k_load.wait()
        cached = []
        for i in range(block):
            part = query[i * per_row : (i + 1) * per_row].astype(BF16)
            score = mm_t(part, keys[i]) * SCALE
            cached.append(jnp.where(iota((per_row, cache), 1) < lengths[i], score, -jnp.inf))
        cached = jnp.concatenate(cached, axis=0)
        peak = jnp.maximum(jnp.max(cached, axis=1, keepdims=True), jnp.max(fresh, axis=1, keepdims=True))
        cached = jnp.exp(cached - peak)
        fresh = jnp.exp(fresh - peak)
        total = jnp.sum(cached, axis=1, keepdims=True) + jnp.sum(fresh, axis=1, keepdims=True)
        v_load.wait()
        mixture = jnp.concatenate(
            [mm(cached[i * per_row : (i + 1) * per_row].astype(BF16), values[i]) for i in range(block)], axis=0
        )
        if key_heads > 1:
            picked = jnp.zeros((n_query, HEAD), F32)
            for h in range(key_heads):
                picked = picked + jnp.where(owner % heads // group == h, mixture[:, h * HEAD : (h + 1) * HEAD], 0.0)
            mixture = picked
        mixture = mixture + mm(fresh.astype(BF16), fresh_v)
        ready = mm(back, (mixture / total).astype(BF16))
        return jnp.concatenate([ready[h * 8 : (h + 1) * 8] for h in range(heads)], axis=1)

    def gather(rows, buffer, kind):
        buffer[ty] = folded(rows).astype(BF16)
        return [
            push(buffer.at[ty], buffer.at[ty], ty_send.at[kind, step], ty_recv.at[kind, step], {"ty": ty_peer(step)})
            for step in range(1, n_ty)
        ]

    acc = summed(sent_pe, p_send_e, p_recv_e, ty)
    sent_ge = gather(attend(acc, heads_e, v_wk_e.shape[1] // HEAD, l_kc_e, v_kc_e, l_vc_e, v_vc_e), g_e, 3)
    acc = summed(sent_pa, p_send_a, p_recv_a, ty)
    sent_ga = gather(attend(acc, heads_a, v_wk_a.shape[1] // HEAD, l_kc_a, v_kc_a, l_vc_a, v_vc_a), g_a, 4)

    def output(copies, buffer, load, weight, send, recv, kind):
        for copy in copies:
            copy.wait_recv()
        rows = unfolded(buffer[...].astype(F32)).reshape(n_rows, weight.shape[0]).astype(BF16)
        load.wait()
        columns = weight.shape[1]
        parts = [mm(rows, weight[:, at : at + CHUNK]) for at in range(0, columns, CHUNK)]
        send[...] = folded(jnp.concatenate(parts, axis=1).reshape(n_tx, 8, columns)).astype(BF16)
        return [
            push(send.at[tx_peer(step)], recv.at[step], tx_send.at[kind, step], tx_recv.at[kind, step],
                 {"tx": tx_peer(step)})
            for step in range(1, n_tx)
        ]

    sent_oe = output(sent_ge, g_e, l_wo_e, v_wo_e, o_send_e, o_recv_e, 0)
    sent_oa = output(sent_ga, g_a, l_wo_a, v_wo_a, o_send_a, o_recv_a, 1)

    def residual(copies, x, send, recv, s_send, s_recv, kind):
        values = x[tx] + summed(copies, send, recv, tx)
        part = lane_fold(values * values)
        s_send[...] = part
        return values, part, [
            push(s_send, s_recv.at[step], ty_send.at[kind, step], ty_recv.at[kind, step], {"ty": ty_peer(step)})
            for step in range(1, n_ty)
        ]

    res_e, part_e, sent_se = residual(sent_oe, x_e, o_send_e, o_recv_e, s_send_e, s_recv_e, 5)
    res_a, part_a, sent_sa = residual(sent_oa, x_a, o_send_a, o_recv_a, s_send_a, s_recv_a, 6)

    partner = {"grp": 1 - grp}

    def final(values, part, copies, s_recv, g_load, gain, buffer, kind):
        width = values.shape[1]
        g_load.wait()
        for copy, step in zip(copies, range(1, n_ty)):
            copy.wait_recv()
            part = part + s_recv[step]
        mean = jnp.sum(part, axis=1, keepdims=True) / (width * n_ty)
        rows = values * lax.rsqrt(mean + EPS) * gain[...].astype(F32).reshape(1, width)
        buffer[flat] = folded(rows).astype(BF16)
        across = [
            push(buffer.at[flat], buffer.at[flat], tx_send.at[kind, step], tx_recv.at[kind, step], {"tx": tx_peer(step)})
            for step in range(1, n_tx)
        ]
        forward = [
            push(buffer.at[flat], buffer.at[flat], fw_send.at[kind - 2, 0], fw_recv.at[kind - 2, 0], partner)
        ]
        return across, forward

    def pass_on(across, forward, buffer, kind):
        for copy, step in zip(across, range(1, n_tx)):
            copy.wait_recv()
            source = grp * n_tx + lax.rem(tx + n_tx - step, n_tx)
            forward.append(
                push(buffer.at[source], buffer.at[source], fw_send.at[kind - 2, step], fw_recv.at[kind - 2, step], partner)
            )

    def collect(forward, buffer, rows):
        for copy in forward:
            copy.wait_recv()
        rows[...] = unfolded(buffer[...].astype(F32)).reshape(rows.shape).astype(BF16)

    across_e, forward_e = final(res_e, part_e, sent_se, s_recv_e, l_fin_e, v_fin_e, f_e, 2)
    across_a, forward_a = final(res_a, part_a, sent_sa, s_recv_a, l_fin_a, v_fin_a, f_a, 3)

    padding = v_head_e.shape[0] - vocab
    l_head_e.wait()
    v_head_e[pl.ds(vocab, padding), :] = jnp.zeros((padding, width_e), BF16)
    l_head_a.wait()
    v_head_a[pl.ds(vocab, padding), :] = jnp.zeros((padding, width_a), BF16)

    n_chunk = v_head_e.shape[0] // CHUNK
    logit_copies = []

    def logits(rows, head, base):
        for c in range(n_chunk):
            part = mm_t(rows[...], head[pl.ds(c * CHUNK, CHUNK), :])
            l_send[base + c] = part.reshape(n_ty, 16, CHUNK).astype(BF16)
            for step in range(1, n_ty):
                logit_copies.append(
                    push(l_send.at[base + c, ty_peer(step)], l_recv.at[base + c, step],
                         l_ssem.at[base + c, step], l_rsem.at[base + c, step], {"ty": ty_peer(step)})
                )

    pass_on(across_e, forward_e, f_e, 2)
    collect(forward_e, f_e, rows_e)
    logits(rows_e, v_head_e, 0)
    pass_on(across_a, forward_a, f_a, 3)
    collect(forward_a, f_a, rows_a)
    logits(rows_a, v_head_a, n_chunk)

    def chunk_sum(c):
        total = l_send[c, ty].astype(F32)
        for step in range(1, n_ty):
            logit_copies[c * (n_ty - 1) + step - 1].wait_recv()
            total = total + l_recv[c, step].astype(F32)
        return total

    lane_c = iota((16, CHUNK), 1)

    def peak_and_total(parts):
        masked = [jnp.where(lane_c + c * CHUNK < vocab, part, -jnp.inf) for c, part in enumerate(parts)]
        peak = masked[0]
        for part in masked[1:]:
            peak = jnp.maximum(peak, part)
        peak = jnp.max(peak, axis=1, keepdims=True)
        total = jnp.exp(masked[0] - peak)
        for part in masked[1:]:
            total = total + jnp.exp(part - peak)
        return peak, jnp.sum(total, axis=1, keepdims=True)

    l_tokens.wait()
    row16 = iota((16, HEAD), 0)
    token = jnp.zeros((16, HEAD), jnp.int32)
    for s in range(2):
        for r in range(8):
            token = jnp.where(row16 == r // block * 8 + s * block + r % block, tokens[s, r], token)
    token = widen(token - flat * vocab, CHUNK)

    expert = [chunk_sum(c) for c in range(n_chunk)]
    peak_e, total_e = peak_and_total(expert)
    amateur = [chunk_sum(n_chunk + c) for c in range(n_chunk)]
    peak_a, total_a = peak_and_total(amateur)
    chosen = jnp.zeros((16, CHUNK), F32)
    mixed = []
    for c in range(n_chunk):
        mixed.append(expert[c] - AMATEUR * amateur[c])
        column = lane_c + c * CHUNK
        chosen = chosen + jnp.where((column == token) & (column < vocab), mixed[c], 0.0)
    chosen = jnp.sum(chosen, axis=1, keepdims=True)

    lane16 = iota((16, HEAD), 1) % 64
    tile = jnp.where(lane16 == 0, peak_e, jnp.where(lane16 == 1, total_e, 0.0))
    tile = jnp.where(lane16 == 2, peak_a, jnp.where(lane16 == 3, total_a, tile))
    tile = jnp.where(lane16 == 4, chosen, tile)
    tile = jnp.where(lane8 < 64, tile[:8], tile[8:])
    t_send[...] = tile
    copies = [
        push(t_send, t_recv.at[step], t_ssem.at[step], t_rsem.at[step], flat_peer(step)) for step in range(1, n_flat)
    ]
    for copy in copies:
        copy.wait_recv()
    tiles = [tile] + [t_recv[step] for step in range(1, n_flat)]
    highest = functools.reduce(jnp.maximum, tiles)
    picked = functools.reduce(jnp.add, tiles)

    def shifted(values):
        return jnp.concatenate([values[:, 1:], values[:, :1]], axis=1)

    summed_up = functools.reduce(jnp.add, [jnp.exp(t - highest) * shifted(t) for t in tiles])
    log_total = highest + jnp.log(summed_up)

    def column(values, lane):
        return jnp.concatenate([values[:, lane : lane + 1], values[:, lane + 64 : lane + 65]], axis=0)

    offset = column(log_total, 0) - AMATEUR * column(log_total, 2)
    for c in range(n_chunk):
        size = min(CHUNK, vocab - c * CHUNK)
        contrast = mixed[c] - offset
        for s in range(2):
            low = s * block
            out_ref[s, :, c * CHUNK : c * CHUNK + size] = jnp.concatenate(
                [contrast[low : low + block], contrast[8 + low : 8 + low + block]], axis=0
            )[:, :size]
    value = jnp.broadcast_to(column(picked, 4) - offset, (16, HEAD))
    lane_r = iota((16, HEAD), 1)
    for s in range(2):
        mine = row16 == lane_r // block * 8 + s * block + lane_r % block
        line = jnp.sum(jnp.where(mine & (lane_r < 8), value, 0.0), axis=0, keepdims=True)
        score_ref[s : s + 1, :] = line[:, :8]

    for copy in sent:
        copy.wait_send()


def on_device(axes, *args):
    (
        hid_e, gain_e, wq_e, wk_e, wv_e, wo_e, fin_e, head_e, kc_e, vc_e,
        hid_a, gain_a, wq_a, wk_a, wv_a, wo_a, fin_a, head_a, kc_a, vc_a,
        lengths, tokens,
    ) = args
    n_grp, n_tx, n_ty = axes
    n_flat = n_grp * n_tx
    half = hid_e.shape[1] // n_grp
    vocab = head_e.shape[0]
    padded = -(-vocab // CHUNK) * CHUNK
    n_chunk = padded // CHUNK
    n_rows = 2 * half
    width_e, width_a = hid_e.shape[2], hid_a.shape[2]
    cols_e = wq_e.shape[1] + wk_e.shape[1] + wv_e.shape[1]
    cols_a = wq_a.shape[1] + wk_a.shape[1] + wv_a.shape[1]
    inner_e, inner_a = wo_e.shape[0], wo_a.shape[0]

    def like(array):
        return pltpu.VMEM(array.shape, array.dtype)

    scratch = [
        pltpu.SMEM(lengths.shape, jnp.int32), pltpu.SMEM(tokens.shape, jnp.int32),
        like(gain_e), like(fin_e), like(gain_a), like(fin_a),
    ]
    for hid, wq, wk, wv, wo, head, kc, vc in (
        (hid_e, wq_e, wk_e, wv_e, wo_e, head_e, kc_e, vc_e),
        (hid_a, wq_a, wk_a, wv_a, wo_a, head_a, kc_a, vc_a),
    ):
        scratch += [
            pltpu.VMEM((2, half, hid.shape[2]), BF16), like(wq), like(wk), like(wv), like(wo),
            pltpu.VMEM((padded, head.shape[1]), BF16), like(kc), like(vc),
        ]
    scratch += [
        pltpu.VMEM((n_ty, 8, width_e), F32), pltpu.VMEM((n_ty, 8, width_a), F32),
        pltpu.VMEM((8, HEAD), F32), pltpu.VMEM((n_ty, 8, HEAD), F32),
        pltpu.VMEM((n_ty, 16, cols_e // 2), BF16), pltpu.VMEM((n_ty, 16, cols_e // 2), BF16),
        pltpu.VMEM((n_ty, 16, cols_a // 2), BF16), pltpu.VMEM((n_ty, 16, cols_a // 2), BF16),
        pltpu.VMEM((n_ty, 16, inner_e // 2), BF16), pltpu.VMEM((n_ty, 16, inner_a // 2), BF16),
        pltpu.VMEM((n_tx, 16, width_e // 2), BF16), pltpu.VMEM((n_tx, 16, width_e // 2), BF16),
        pltpu.VMEM((n_tx, 16, width_a // 2), BF16), pltpu.VMEM((n_tx, 16, width_a // 2), BF16),
        pltpu.VMEM((8, HEAD), F32), pltpu.VMEM((n_ty, 8, HEAD), F32),
        pltpu.VMEM((8, HEAD), F32), pltpu.VMEM((n_ty, 8, HEAD), F32),
        pltpu.VMEM((n_flat, 16, width_e // 2), BF16), pltpu.VMEM((n_flat, 16, width_a // 2), BF16),
        pltpu.VMEM((n_flat * 8, width_e), BF16), pltpu.VMEM((n_flat * 8, width_a), BF16),
        pltpu.VMEM((2 * n_chunk, n_ty, 16, CHUNK), BF16), pltpu.VMEM((2 * n_chunk, n_ty, 16, CHUNK), BF16),
        pltpu.VMEM((8, HEAD), F32), pltpu.VMEM((n_flat, 8, HEAD), F32),
        pltpu.SemaphoreType.DMA((22,)),
        pltpu.SemaphoreType.DMA((7, n_ty)), pltpu.SemaphoreType.DMA((7, n_ty)),
        pltpu.SemaphoreType.DMA((4, n_tx)), pltpu.SemaphoreType.DMA((4, n_tx)),
        pltpu.SemaphoreType.DMA((2, n_tx)), pltpu.SemaphoreType.DMA((2, n_tx)),
        pltpu.SemaphoreType.DMA((2 * n_chunk, n_ty)), pltpu.SemaphoreType.DMA((2 * n_chunk, n_ty)),
        pltpu.SemaphoreType.DMA((n_flat,)), pltpu.SemaphoreType.DMA((n_flat,)),
    ]
    hbm = pl.BlockSpec(memory_space=pl.ANY)
    vmem = pl.BlockSpec(memory_space=pltpu.VMEM)
    macs = n_rows * (width_e * (cols_e + inner_e) + width_a * (cols_a + inner_a)) + 2 * n_rows * vocab * (width_e + width_a)
    read = sum(array.size * array.dtype.itemsize for array in args)
    return pl.pallas_call(
        functools.partial(kernel, axes, None),
        out_shape=(
            jax.ShapeDtypeStruct((2, hid_e.shape[1] // n_ty, vocab), F32),
            jax.ShapeDtypeStruct((2, hid_e.shape[1] // n_ty), F32),
        ),
        in_specs=[hbm] * len(args),
        out_specs=(vmem, vmem),
        scratch_shapes=scratch,
        compiler_params=pltpu.CompilerParams(
            collective_id=0, has_side_effects=True, vmem_limit_bytes=56 * 1024 * 1024
        ),
        cost_estimate=pl.CostEstimate(flops=2 * macs, bytes_accessed=read, transcendentals=0),
        name="contrast",
    )(*args)


def solution(mesh):
    model = (
        P(None, None, "ty"), P("ty"), P("ty", "tx"), P("ty", "tx"), P("ty", "tx"), P("tx", "ty"), P("ty"),
        P(("grp", "tx"), "ty"), P(("grp", "ty"), None, "tx"), P(("grp", "ty"), None, "tx"),
    )
    axes = tuple(mesh.shape[name] for name in ("grp", "tx", "ty"))
    return jax.shard_map(
        functools.partial(on_device, axes),
        mesh=mesh,
        in_specs=model + model + (P(("grp", "ty")), P(None, "ty")),
        out_specs=(P(None, "ty", ("grp", "tx")), P(None, "ty")),
        check_vma=False,
    )
```

```python
import functools
import math

import jax
import jax.numpy as jnp
from jax import lax
from jax.experimental import pallas as pl
from jax.experimental.pallas import tpu as pltpu
from jax.sharding import PartitionSpec as P

HEAD = 128
EPS = 1e-05
BASE = 10000.0
AMATEUR = 0.5
SCALE = HEAD**-0.5
CHUNK = 512
SLAB = 1024
F32 = jnp.float32
BF16 = jnp.bfloat16
MESH = pl.DeviceIdType.MESH


def iota(shape, axis):
    return lax.broadcasted_iota(jnp.int32, shape, axis)


def mm(a, b):
    return lax.dot_general(a, b, (((1,), (0,)), ((), ())), preferred_element_type=F32)


def mm_t(a, b):
    return lax.dot_general(a, b, (((1,), (1,)), ((), ())), preferred_element_type=F32)


def one_hot(size, source):
    out = iota((size, size), 0)
    return jnp.where(iota((size, size), 1) == source(out), 1.0, 0.0).astype(BF16)


def folded(values):
    half = values.shape[-1] // 2
    return jnp.concatenate([values[..., :half], values[..., half:]], axis=-2)


def unfolded(values):
    return jnp.concatenate([values[..., :8, :], values[..., 8:, :]], axis=-1)


def packed(values, ref):
    return values if ref.dtype == F32 else folded(values).astype(ref.dtype)


def lane_fold(values):
    total = values[:, :HEAD]
    for start in range(HEAD, values.shape[1], HEAD):
        total = total + values[:, start : start + HEAD]
    return total


def widen(column, width):
    return jnp.concatenate([column] * (width // HEAD), axis=1)


def kernel(axes, dims, *refs):
    n_grp, n_tx, n_ty = axes
    (
        hid_e, gain_e, wq_e, wk_e, wv_e, wo_e, fin_e, head_e, kc_e, vc_e,
        hid_a, gain_a, wq_a, wk_a, wv_a, wo_a, fin_a, head_a, kc_a, vc_a,
        h_lengths, h_tokens,
        out_ref, score_ref,
        lengths, tokens, v_gain_e, v_fin_e, v_gain_a, v_fin_a,
        v_hid_e, v_wq_e, v_wk_e, v_wv_e, v_wo_e, v_head_e, v_kc_e, v_vc_e,
        v_hid_a, v_wq_a, v_wk_a, v_wv_a, v_wo_a, v_head_a, v_kc_a, v_vc_a,
        x_e, x_a, sq_send, sq_recv,
        p_send_e, p_recv_e, p_send_a, p_recv_a,
        g_e, g_a,
        o_send_e, o_recv_e, o_send_a, o_recv_a,
        s_send_e, s_recv_e, s_send_a, s_recv_a,
        f_e, f_a, rows_e, rows_a,
        l_send, l_recv, t_send, t_recv,
        local_sem, ty_send, ty_recv, tx_send, tx_recv, fw_send, fw_recv, l_ssem, l_rsem, t_ssem, t_rsem,
    ) = refs
    grp, tx, ty = lax.axis_index("grp"), lax.axis_index("tx"), lax.axis_index("ty")
    half_rows = v_hid_e.shape[1]
    width_e, width_a = v_hid_e.shape[2], v_hid_a.shape[2]
    heads_e, heads_a = v_wq_e.shape[1] // HEAD, v_wq_a.shape[1] // HEAD
    vocab = head_e.shape[0]

    first = pl.multiple_of(grp * half_rows, half_rows)
    pairs = [
        (hid_e.at[:, pl.ds(first, half_rows)], v_hid_e),
        (hid_a.at[:, pl.ds(first, half_rows)], v_hid_a),
        (h_lengths, lengths), (gain_e, v_gain_e), (gain_a, v_gain_a),
        (fin_e, v_fin_e), (fin_a, v_fin_a), (h_tokens, tokens),
        (wq_e, v_wq_e), (wk_e, v_wk_e), (wv_e, v_wv_e),
        (wq_a, v_wq_a), (wk_a, v_wk_a), (wv_a, v_wv_a),
        (kc_e, v_kc_e), (vc_e, v_vc_e), (kc_a, v_kc_a), (vc_a, v_vc_a),
        (wo_e, v_wo_e), (wo_a, v_wo_a),
        (head_e, v_head_e.at[pl.ds(0, vocab)]), (head_a, v_head_a.at[pl.ds(0, vocab)]),
    ]
    loads = [
        pltpu.make_async_copy(source, target, local_sem.at[number])
        for number, (source, target) in enumerate(pairs)
    ]
    for load in loads[:8]:
        load.start()
    (l_hid_e, l_hid_a, l_lengths, l_gain_e, l_gain_a, l_fin_e, l_fin_a, l_tokens, l_wq_e, l_wk_e, l_wv_e, l_wq_a, l_wk_a, l_wv_a,
     l_kc_e, l_vc_e, l_kc_a, l_vc_a, l_wo_e, l_wo_a, l_head_e, l_head_a) = loads

    def ty_peer(step):
        return lax.rem(ty // 4 + step // 4, n_ty // 4) * 4 + lax.rem(ty + step, 4)

    def tx_peer(step):
        return lax.rem(tx // 4 + step // 4, n_tx // 4) * 4 + lax.rem(tx + step, 4)

    flat = grp * n_tx + tx
    n_flat = n_grp * n_tx

    def flat_peer(step):
        return {"grp": lax.rem(grp + step // n_tx, n_grp), "tx": tx_peer(lax.rem(step, n_tx))}

    def to_ty(step):
        return {"ty": ty_peer(step)}

    def to_tx(step):
        return {"tx": tx_peer(step)}

    barrier = pltpu.get_barrier_semaphore()

    def greet(device):
        pl.semaphore_signal(barrier, inc=1, device_id=device, device_id_type=MESH)

    @pl.loop(1, n_ty)
    def _(step):
        greet(to_ty(n_ty - step))

    @pl.loop(1, n_flat)
    def _(step):
        greet(flat_peer(n_flat - step))

    for load in loads[8:14]:
        load.start()

    started = []

    class Exchange:
        def __init__(self, n, source, target, send_sems, recv_sems, device, begin=True):
            self.n = n
            self.make = lambda step: pltpu.make_async_remote_copy(
                src_ref=source(step), dst_ref=target(step), send_sem=send_sems.at[step], recv_sem=recv_sems.at[step],
                device_id=device(step), device_id_type=MESH,
            )
            started.append(self)
            if begin:
                self.begin()

        def begin(self):
            @pl.loop(1, self.n)
            def _(step):
                self.make(self.n - step).start()

        def arrive(self):
            @pl.loop(1, self.n)
            def _(step):
                self.make(step).wait_recv()

        def finish(self):
            @pl.loop(1, self.n)
            def _(step):
                self.make(step).wait_send()

    def add_up(exchange, first, recv):
        def body(step, total):
            exchange.make(step).wait_recv()
            return total + recv[step].astype(F32)

        return lax.fori_loop(1, exchange.n, body, first)

    n_rows = 2 * half_rows
    block = half_rows // n_ty
    order = one_hot(
        n_rows, lambda o: (o // block) % 2 * half_rows + o // (2 * block) * block + o % block
    )
    l_hid_e.wait()
    wide_e = mm(order, v_hid_e[...].reshape(n_rows, width_e))
    x_e[...] = wide_e.reshape(n_ty, 8, width_e)
    l_hid_a.wait()
    wide_a = mm(order, v_hid_a[...].reshape(n_rows, width_a))
    x_a[...] = wide_a.reshape(n_ty, 8, width_a)
    partial = jnp.concatenate([lane_fold(wide_e * wide_e), lane_fold(wide_a * wide_a)], axis=0)
    own = jnp.broadcast_to(jnp.sum(partial.T, axis=0, keepdims=True), (8, HEAD))
    sq_send[...] = own

    pl.semaphore_wait(barrier, n_ty - 1 + n_flat - 1)

    squares = Exchange(n_ty, lambda d: sq_send, lambda d: sq_recv.at[d], ty_send.at[0], ty_recv.at[0], to_ty)
    for load in loads[14:18]:
        load.start()

    row8, lane8 = iota((8, HEAD), 0), iota((8, HEAD), 1)
    position = jnp.zeros((8, HEAD), jnp.int32)
    l_lengths.wait()
    for i in range(block):
        position = jnp.where(row8 % block == i, lengths[i], position)
    position = (position + row8 // block).astype(F32)
    exponent = (lane8 % (HEAD // 2)).astype(F32) * (2.0 / HEAD)
    angle = position * jnp.exp(exponent * (-math.log(BASE)))
    cosine = jnp.cos(angle)
    sine = jnp.where(lane8 < HEAD // 2, -1.0, 1.0) * jnp.sin(angle)

    def rotated(values):
        turned = jnp.concatenate([values[:, HEAD // 2 :], values[:, : HEAD // 2]], axis=1)
        return values * cosine + turned * sine

    total = add_up(squares, own, sq_recv)
    square = jnp.broadcast_to(total[0:1], (HEAD, HEAD)).T
    root_e = lax.rsqrt(square[:n_rows] / (width_e * n_ty) + EPS)
    root_a = lax.rsqrt(square[n_rows:] / (width_a * n_ty) + EPS)

    def project(x, root, g_load, gain, weights, send, recv, kind):
        width = x.shape[2]
        g_load.wait()
        values = x[...].reshape(n_rows, width)
        normed = (values * widen(root, width) * gain[...].astype(F32).reshape(1, width)).astype(BF16)
        parts = []
        for load, weight in weights:
            load.wait()
            columns = weight.shape[1]
            for at in range(0, columns, CHUNK):
                parts.append(mm(normed, weight[:, at : at + min(CHUNK, columns - at)]))
        send[...] = packed(jnp.concatenate(parts, axis=1).reshape(n_ty, 8, -1), send)
        return Exchange(n_ty, lambda d: send.at[ty_peer(d)], lambda d: recv.at[d], ty_send.at[kind], ty_recv.at[kind], to_ty)

    sent_pe = project(x_e, root_e, l_gain_e, v_gain_e, ((l_wq_e, v_wq_e), (l_wk_e, v_wk_e), (l_wv_e, v_wv_e)), p_send_e, p_recv_e, 1)
    sent_pa = project(x_a, root_a, l_gain_a, v_gain_a, ((l_wq_a, v_wq_a), (l_wk_a, v_wk_a), (l_wv_a, v_wv_a)), p_send_a, p_recv_a, 2)

    for load in loads[18:]:
        load.start()

    def summed(exchange, send, recv, me):
        total = add_up(exchange, send[me].astype(F32), recv)
        return total if send.dtype == F32 else unfolded(total)

    def padded(rows, size):
        if rows.shape[0] == size:
            return rows
        return jnp.concatenate([rows, jnp.zeros((size - rows.shape[0], rows.shape[1]), F32)], axis=0)

    def attend(acc, heads, key_heads, k_load, keys, v_load, values):
        group = heads // key_heads
        n_query = heads * 8
        per_row = 2 * heads
        cache = keys.shape[1]
        wide = key_heads * HEAD
        query = jnp.concatenate([rotated(acc[:, h * HEAD : (h + 1) * HEAD]) for h in range(heads)], axis=0)
        at = heads * HEAD
        fresh_k = jnp.concatenate(
            [rotated(acc[:, at + h * HEAD : at + (h + 1) * HEAD]) for h in range(key_heads)], axis=0
        )
        at += wide
        fresh_v = jnp.concatenate(
            [acc[:, at + h * HEAD : at + (h + 1) * HEAD] for h in range(key_heads)], axis=0
        )
        fresh_k = padded(fresh_k, HEAD).astype(BF16)
        fresh_v = padded(fresh_v, HEAD).astype(BF16)
        forth = one_hot(n_query, lambda o: o % heads * 8 + o // heads % 2 * block + o // per_row)
        back = one_hot(n_query, lambda o: o % block * per_row + o // block % 2 * heads + o // 8)
        query = mm(forth, query.astype(BF16))
        owner = iota((n_query, HEAD), 0)
        lane = iota((n_query, HEAD), 1)
        fresh = mm_t(query.astype(BF16), fresh_k) * SCALE
        seen = (
            (lane < key_heads * 8)
            & (lane // 8 == owner % heads // group)
            & (lane % block == owner // per_row)
            & (lane // block % 2 <= owner // heads % 2)
        )
        fresh = jnp.where(seen, fresh, -jnp.inf)
        if key_heads > 1:
            spread = widen(query, wide)
            keep = iota((n_query, wide), 1) // HEAD == iota((n_query, wide), 0) % heads // group
            query = jnp.where(keep, spread, 0.0)
        k_load.wait()
        cached = []
        for i in range(block):
            part = query[i * per_row : (i + 1) * per_row].astype(BF16)
            score = mm_t(part, keys[i]) * SCALE
            cached.append(jnp.where(iota((per_row, cache), 1) < lengths[i], score, -jnp.inf))
        cached = jnp.concatenate(cached, axis=0)
        peak = jnp.maximum(jnp.max(cached, axis=1, keepdims=True), jnp.max(fresh, axis=1, keepdims=True))
        cached = jnp.exp(cached - peak)
        fresh = jnp.exp(fresh - peak)
        total = jnp.sum(cached, axis=1, keepdims=True) + jnp.sum(fresh, axis=1, keepdims=True)
        v_load.wait()
        mixture = jnp.concatenate(
            [mm(cached[i * per_row : (i + 1) * per_row].astype(BF16), values[i]) for i in range(block)], axis=0
        )
        if key_heads > 1:
            picked = jnp.zeros((n_query, HEAD), F32)
            for h in range(key_heads):
                picked = picked + jnp.where(owner % heads // group == h, mixture[:, h * HEAD : (h + 1) * HEAD], 0.0)
            mixture = picked
        mixture = mixture + mm(fresh.astype(BF16), fresh_v)
        ready = mm(back, (mixture / total).astype(BF16))
        return jnp.concatenate([ready[h * 8 : (h + 1) * 8] for h in range(heads)], axis=1)

    def gather(rows, buffer, kind):
        buffer[ty] = folded(rows).astype(BF16)
        return Exchange(n_ty, lambda d: buffer.at[ty], lambda d: buffer.at[ty], ty_send.at[kind], ty_recv.at[kind], to_ty)

    acc = summed(sent_pe, p_send_e, p_recv_e, ty)
    sent_ge = gather(attend(acc, heads_e, v_wk_e.shape[1] // HEAD, l_kc_e, v_kc_e, l_vc_e, v_vc_e), g_e, 3)
    acc = summed(sent_pa, p_send_a, p_recv_a, ty)
    sent_ga = gather(attend(acc, heads_a, v_wk_a.shape[1] // HEAD, l_kc_a, v_kc_a, l_vc_a, v_vc_a), g_a, 4)

    def output(exchange, buffer, load, weight, send, recv, kind):
        exchange.arrive()
        rows = unfolded(buffer[...].astype(F32)).reshape(n_rows, weight.shape[0]).astype(BF16)
        load.wait()
        columns = weight.shape[1]
        parts = [mm(rows, weight[:, at : at + CHUNK]) for at in range(0, columns, CHUNK)]
        send[...] = packed(jnp.concatenate(parts, axis=1).reshape(n_tx, 8, columns), send)
        return Exchange(n_tx, lambda d: send.at[tx_peer(d)], lambda d: recv.at[d], tx_send.at[kind], tx_recv.at[kind], to_tx)

    sent_oe = output(sent_ge, g_e, l_wo_e, v_wo_e, o_send_e, o_recv_e, 0)
    sent_oa = output(sent_ga, g_a, l_wo_a, v_wo_a, o_send_a, o_recv_a, 1)

    def residual(exchange, x, send, recv, s_send, s_recv, kind):
        values = x[tx] + summed(exchange, send, recv, tx)
        part = lane_fold(values * values)
        s_send[...] = part
        return values, part, Exchange(
            n_ty, lambda d: s_send, lambda d: s_recv.at[d], ty_send.at[kind], ty_recv.at[kind], to_ty
        )

    res_e, part_e, sent_se = residual(sent_oe, x_e, o_send_e, o_recv_e, s_send_e, s_recv_e, 5)
    res_a, part_a, sent_sa = residual(sent_oa, x_a, o_send_a, o_recv_a, s_send_a, s_recv_a, 6)

    def final(values, part, exchange, s_recv, g_load, gain, buffer, kind):
        width = values.shape[1]
        g_load.wait()
        part = add_up(exchange, part, s_recv)
        mean = jnp.sum(part, axis=1, keepdims=True) / (width * n_ty)
        rows = values * lax.rsqrt(mean + EPS) * gain[...].astype(F32).reshape(1, width)
        buffer[flat] = folded(rows).astype(BF16)
        across = Exchange(
            n_tx, lambda d: buffer.at[flat], lambda d: buffer.at[flat], tx_send.at[kind], tx_recv.at[kind], to_tx
        )

        def from_tx(step):
            return grp * n_tx + lax.rem(tx // 4 + n_tx // 4 - step // 4, n_tx // 4) * 4 + lax.rem(tx + 4 - lax.rem(step, 4), 4)

        forward = Exchange(
            n_tx, lambda d: buffer.at[from_tx(d)], lambda d: buffer.at[from_tx(d)], fw_send.at[kind - 2],
            fw_recv.at[kind - 2], lambda d: {"grp": 1 - grp}, begin=False,
        )
        forward.make(0).start()
        return across, forward

    def collect(pair, buffer, rows):
        across, forward = pair

        @pl.loop(1, n_tx)
        def _(step):
            across.make(step).wait_recv()
            forward.make(step).start()

        forward.make(0).wait_recv()
        forward.arrive()
        rows[...] = unfolded(buffer[...].astype(F32)).reshape(rows.shape).astype(BF16)

    pair_e = final(res_e, part_e, sent_se, s_recv_e, l_fin_e, v_fin_e, f_e, 2)
    pair_a = final(res_a, part_a, sent_sa, s_recv_a, l_fin_a, v_fin_a, f_a, 3)

    padding = v_head_e.shape[0] - vocab
    l_head_e.wait()
    v_head_e[pl.ds(vocab, padding), :] = jnp.zeros((padding, width_e), BF16)
    l_head_a.wait()
    v_head_a[pl.ds(vocab, padding), :] = jnp.zeros((padding, width_a), BF16)

    n_slab = v_head_e.shape[0] // SLAB

    def logit_exchange(slab, begin=True):
        return Exchange(
            n_ty, lambda d: l_send.at[slab, ty_peer(d)], lambda d: l_recv.at[slab, d], l_ssem.at[slab], l_rsem.at[slab],
            to_ty, begin,
        )

    def logits(rows, head, base):
        @pl.loop(0, n_slab)
        def _(slab):
            for at in range(0, SLAB, CHUNK):
                part = mm_t(rows[...], head[pl.ds(pl.multiple_of(slab * SLAB + at, CHUNK), CHUNK), :])
                l_send[base + slab, :, :, at : at + CHUNK] = part.reshape(n_ty, 16, CHUNK).astype(BF16)
            logit_exchange(base + slab)
            started.pop()

    collect(pair_e, f_e, rows_e)
    logits(rows_e, v_head_e, 0)
    collect(pair_a, f_a, rows_a)
    logits(rows_a, v_head_a, n_slab)

    def slab_sum(slab):
        exchange = logit_exchange(slab, False)
        started.pop()
        return add_up(exchange, l_send[slab, ty].astype(F32), l_recv.at[slab])

    lane_c = iota((16, SLAB), 1)

    def peak_and_total(parts):
        masked = [jnp.where(lane_c + c * SLAB < vocab, part, -jnp.inf) for c, part in enumerate(parts)]
        peak = masked[0]
        for part in masked[1:]:
            peak = jnp.maximum(peak, part)
        peak = jnp.max(peak, axis=1, keepdims=True)
        total = jnp.exp(masked[0] - peak)
        for part in masked[1:]:
            total = total + jnp.exp(part - peak)
        return peak, jnp.sum(total, axis=1, keepdims=True)

    l_tokens.wait()
    row16 = iota((16, HEAD), 0)
    token = jnp.zeros((16, HEAD), jnp.int32)
    for s in range(2):
        for r in range(8):
            token = jnp.where(row16 == r // block * 8 + s * block + r % block, tokens[s, r], token)
    token = widen(token - flat * vocab, SLAB)

    expert = [slab_sum(c) for c in range(n_slab)]
    peak_e, total_e = peak_and_total(expert)
    amateur = [slab_sum(n_slab + c) for c in range(n_slab)]
    peak_a, total_a = peak_and_total(amateur)
    chosen = jnp.zeros((16, SLAB), F32)
    mixed = []
    for c in range(n_slab):
        mixed.append(expert[c] - AMATEUR * amateur[c])
        column = lane_c + c * SLAB
        chosen = chosen + jnp.where((column == token) & (column < vocab), mixed[c], 0.0)
    chosen = jnp.sum(chosen, axis=1, keepdims=True)

    lane16 = iota((16, HEAD), 1) % 64
    tile = jnp.where(lane16 == 0, peak_e, jnp.where(lane16 == 1, total_e, 0.0))
    tile = jnp.where(lane16 == 2, peak_a, jnp.where(lane16 == 3, total_a, tile))
    tile = jnp.where(lane16 == 4, chosen, tile)
    tile = jnp.where(lane8 < 64, tile[:8], tile[8:])
    t_send[...] = tile
    Exchange(n_flat, lambda d: t_send, lambda d: t_recv.at[d], t_ssem, t_rsem, flat_peer).arrive()
    tiles = [tile] + [t_recv[step] for step in range(1, n_flat)]
    highest = functools.reduce(jnp.maximum, tiles)
    picked = functools.reduce(jnp.add, tiles)

    def shifted(values):
        return jnp.concatenate([values[:, 1:], values[:, :1]], axis=1)

    summed_up = functools.reduce(jnp.add, [jnp.exp(t - highest) * shifted(t) for t in tiles])
    log_total = highest + jnp.log(summed_up)

    def column(values, lane):
        return jnp.concatenate([values[:, lane : lane + 1], values[:, lane + 64 : lane + 65]], axis=0)

    offset = column(log_total, 0) - AMATEUR * column(log_total, 2)
    for c in range(n_slab):
        size = min(SLAB, vocab - c * SLAB)
        contrast = mixed[c] - offset
        for s in range(2):
            low = s * block
            out_ref[s, :, c * SLAB : c * SLAB + size] = jnp.concatenate(
                [contrast[low : low + block], contrast[8 + low : 8 + low + block]], axis=0
            )[:, :size]
    value = jnp.broadcast_to(column(picked, 4) - offset, (16, HEAD))
    lane_r = iota((16, HEAD), 1)
    for s in range(2):
        mine = row16 == lane_r // block * 8 + s * block + lane_r % block
        line = jnp.sum(jnp.where(mine & (lane_r < 8), value, 0.0), axis=0, keepdims=True)
        score_ref[s : s + 1, :] = line[:, :8]

    for exchange in started:
        exchange.finish()
    pair_e[1].make(0).wait_send()
    pair_a[1].make(0).wait_send()

    @pl.loop(0, 2 * n_slab)
    def _(slab):
        logit_exchange(slab, False).finish()
        started.pop()


def hand_over(a_in, b_in, a_out, b_out, sems):
    copies = [pltpu.make_async_copy(a_in, a_out, sems.at[0]), pltpu.make_async_copy(b_in, b_out, sems.at[1])]
    for copy in copies:
        copy.start()
    for copy in copies:
        copy.wait()


def on_device(axes, *args):
    (
        hid_e, gain_e, wq_e, wk_e, wv_e, wo_e, fin_e, head_e, kc_e, vc_e,
        hid_a, gain_a, wq_a, wk_a, wv_a, wo_a, fin_a, head_a, kc_a, vc_a,
        lengths, tokens,
    ) = args
    n_grp, n_tx, n_ty = axes
    n_flat = n_grp * n_tx
    half = hid_e.shape[1] // n_grp
    vocab = head_e.shape[0]
    padded = -(-vocab // SLAB) * SLAB
    n_slab = padded // SLAB
    n_rows = 2 * half
    width_e, width_a = hid_e.shape[2], hid_a.shape[2]
    cols_e = wq_e.shape[1] + wk_e.shape[1] + wv_e.shape[1]
    cols_a = wq_a.shape[1] + wk_a.shape[1] + wv_a.shape[1]
    inner_e, inner_a = wo_e.shape[0], wo_a.shape[0]

    def like(array):
        return pltpu.VMEM(array.shape, array.dtype)

    scratch = [
        pltpu.SMEM(lengths.shape, jnp.int32), pltpu.SMEM(tokens.shape, jnp.int32),
        like(gain_e), like(fin_e), like(gain_a), like(fin_a),
    ]
    for hid, wq, wk, wv, wo, head, kc, vc in (
        (hid_e, wq_e, wk_e, wv_e, wo_e, head_e, kc_e, vc_e),
        (hid_a, wq_a, wk_a, wv_a, wo_a, head_a, kc_a, vc_a),
    ):
        scratch += [
            pltpu.VMEM((2, half, hid.shape[2]), BF16), like(wq), like(wk), like(wv), like(wo),
            pltpu.VMEM((padded, head.shape[1]), BF16), like(kc), like(vc),
        ]
    scratch += [
        pltpu.VMEM((n_ty, 8, width_e), F32), pltpu.VMEM((n_ty, 8, width_a), F32),
        pltpu.VMEM((8, HEAD), F32), pltpu.VMEM((n_ty, 8, HEAD), F32),
        pltpu.VMEM((n_ty, 8, cols_e), F32), pltpu.VMEM((n_ty, 8, cols_e), F32),
        pltpu.VMEM((n_ty, 16, cols_a // 2), BF16), pltpu.VMEM((n_ty, 16, cols_a // 2), BF16),
        pltpu.VMEM((n_ty, 16, inner_e // 2), BF16), pltpu.VMEM((n_ty, 16, inner_a // 2), BF16),
        pltpu.VMEM((n_tx, 16, width_e // 2), BF16), pltpu.VMEM((n_tx, 16, width_e // 2), BF16),
        pltpu.VMEM((n_tx, 16, width_a // 2), BF16), pltpu.VMEM((n_tx, 16, width_a // 2), BF16),
        pltpu.VMEM((8, HEAD), F32), pltpu.VMEM((n_ty, 8, HEAD), F32),
        pltpu.VMEM((8, HEAD), F32), pltpu.VMEM((n_ty, 8, HEAD), F32),
        pltpu.VMEM((n_flat, 16, width_e // 2), BF16), pltpu.VMEM((n_flat, 16, width_a // 2), BF16),
        pltpu.VMEM((n_flat * 8, width_e), BF16), pltpu.VMEM((n_flat * 8, width_a), BF16),
        pltpu.VMEM((2 * n_slab, n_ty, 16, SLAB), BF16), pltpu.VMEM((2 * n_slab, n_ty, 16, SLAB), BF16),
        pltpu.VMEM((8, HEAD), F32), pltpu.VMEM((n_flat, 8, HEAD), F32),
        pltpu.SemaphoreType.DMA((22,)),
        pltpu.SemaphoreType.DMA((7, n_ty)), pltpu.SemaphoreType.DMA((7, n_ty)),
        pltpu.SemaphoreType.DMA((4, n_tx)), pltpu.SemaphoreType.DMA((4, n_tx)),
        pltpu.SemaphoreType.DMA((2, n_tx)), pltpu.SemaphoreType.DMA((2, n_tx)),
        pltpu.SemaphoreType.DMA((2 * n_slab, n_ty)), pltpu.SemaphoreType.DMA((2 * n_slab, n_ty)),
        pltpu.SemaphoreType.DMA((n_flat,)), pltpu.SemaphoreType.DMA((n_flat,)),
    ]
    hbm = pl.BlockSpec(memory_space=pl.ANY)
    vmem = pl.BlockSpec(memory_space=pltpu.VMEM)
    macs = n_rows * (width_e * (cols_e + inner_e) + width_a * (cols_a + inner_a)) + 2 * n_rows * vocab * (width_e + width_a)
    read = sum(array.size * array.dtype.itemsize for array in args)
    outs = pl.pallas_call(
        functools.partial(kernel, axes, None),
        out_shape=(
            jax.ShapeDtypeStruct((2, hid_e.shape[1] // n_ty, vocab), F32),
            jax.ShapeDtypeStruct((2, hid_e.shape[1] // n_ty), F32),
        ),
        in_specs=[hbm] * len(args),
        out_specs=(vmem, vmem),
        scratch_shapes=scratch,
        compiler_params=pltpu.CompilerParams(
            collective_id=0, has_side_effects=True, vmem_limit_bytes=56 * 1024 * 1024
        ),
        cost_estimate=pl.CostEstimate(flops=2 * macs, bytes_accessed=read, transcendentals=0),
        name="contrast",
    )(*args)
    return pl.pallas_call(
        hand_over,
        out_shape=tuple(jax.ShapeDtypeStruct(out.shape, out.dtype) for out in outs),
        in_specs=[hbm, hbm],
        out_specs=(hbm, hbm),
        scratch_shapes=[pltpu.SemaphoreType.DMA((2,))],
        name="hand_over",
    )(*outs)


def solution(mesh):
    model = (
        P(None, None, "ty"), P("ty"), P("ty", "tx"), P("ty", "tx"), P("ty", "tx"), P("tx", "ty"), P("ty"),
        P(("grp", "tx"), "ty"), P(("grp", "ty"), None, "tx"), P(("grp", "ty"), None, "tx"),
    )
    axes = tuple(mesh.shape[name] for name in ("grp", "tx", "ty"))
    return jax.shard_map(
        functools.partial(on_device, axes),
        mesh=mesh,
        in_specs=model + model + (P(("grp", "ty")), P(None, "ty")),
        out_specs=(P(None, "ty", ("grp", "tx")), P(None, "ty")),
        check_vma=False,
    )
```

```python
import functools
import math

import jax
import jax.numpy as jnp
from jax import lax
from jax.experimental import pallas as pl
from jax.experimental.pallas import tpu as pltpu
from jax.sharding import PartitionSpec as P

HEAD = 128
EPS = 1e-05
BASE = 10000.0
AMATEUR = 0.5
SCALE = HEAD**-0.5
CHUNK = 512
SLAB = 1024
F32 = jnp.float32
BF16 = jnp.bfloat16
MESH = pl.DeviceIdType.MESH


def iota(shape, axis):
    return lax.broadcasted_iota(jnp.int32, shape, axis)


def mm(a, b):
    return lax.dot_general(a, b, (((1,), (0,)), ((), ())), preferred_element_type=F32)


def mm_t(a, b):
    return lax.dot_general(a, b, (((1,), (1,)), ((), ())), preferred_element_type=F32)


def one_hot(size, source):
    out = iota((size, size), 0)
    return jnp.where(iota((size, size), 1) == source(out), 1.0, 0.0).astype(BF16)


def folded(values):
    half = values.shape[-1] // 2
    return jnp.concatenate([values[..., :half], values[..., half:]], axis=-2)


def unfolded(values):
    return jnp.concatenate([values[..., :8, :], values[..., 8:, :]], axis=-1)


def packed(values, ref):
    return values if ref.dtype == F32 else folded(values).astype(ref.dtype)


def lane_fold(values):
    total = values[:, :HEAD]
    for start in range(HEAD, values.shape[1], HEAD):
        total = total + values[:, start : start + HEAD]
    return total


def widen(column, width):
    return jnp.concatenate([column] * (width // HEAD), axis=1)


def kernel(axes, dims, *refs):
    n_grp, n_tx, n_ty = axes
    (
        hid_e, gain_e, wq_e, wk_e, wv_e, wo_e, fin_e, head_e, kc_e, vc_e,
        hid_a, gain_a, wq_a, wk_a, wv_a, wo_a, fin_a, head_a, kc_a, vc_a,
        h_lengths, h_tokens,
        out_ref, score_ref,
        lengths, tokens, v_gain_e, v_fin_e, v_gain_a, v_fin_a,
        v_hid_e, v_wq_e, v_wk_e, v_wv_e, v_wo_e, v_head_e, v_kc_e, v_vc_e,
        v_hid_a, v_wq_a, v_wk_a, v_wv_a, v_wo_a, v_head_a, v_kc_a, v_vc_a,
        x_e, x_a, sq_send, sq_recv,
        p_send_e, p_recv_e, p_send_a, p_recv_a,
        g_e, g_a,
        o_send_e, o_recv_e, o_send_a, o_recv_a,
        s_send_e, s_recv_e, s_send_a, s_recv_a,
        f_e, f_a,
        l_send, l_recv, t_send, t_recv,
        local_sem, ty_send, ty_recv, tx_send, tx_recv, fw_send, fw_recv, l_ssem, l_rsem, t_ssem, t_rsem,
    ) = refs
    grp, tx, ty = lax.axis_index("grp"), lax.axis_index("tx"), lax.axis_index("ty")
    half_rows = v_hid_e.shape[1]
    width_e, width_a = v_hid_e.shape[2], v_hid_a.shape[2]
    heads_e, heads_a = v_wq_e.shape[1] // HEAD, v_wq_a.shape[1] // HEAD
    vocab = head_e.shape[0]

    first = pl.multiple_of(grp * half_rows, half_rows)
    pairs = [
        (hid_e.at[:, pl.ds(first, half_rows)], v_hid_e),
        (hid_a.at[:, pl.ds(first, half_rows)], v_hid_a),
        (h_lengths, lengths), (gain_e, v_gain_e), (gain_a, v_gain_a),
        (fin_e, v_fin_e), (fin_a, v_fin_a), (h_tokens, tokens),
        (wq_a, v_wq_a), (wk_a, v_wk_a), (wv_a, v_wv_a),
        (wq_e, v_wq_e), (wk_e, v_wk_e), (wv_e, v_wv_e),
        (kc_a, v_kc_a), (vc_a, v_vc_a), (kc_e, v_kc_e), (vc_e, v_vc_e),
        (wo_a, v_wo_a), (wo_e, v_wo_e),
        (head_a, v_head_a.at[pl.ds(0, vocab)]), (head_e, v_head_e.at[pl.ds(0, vocab)]),
    ]
    loads = [
        pltpu.make_async_copy(source, target, local_sem.at[number])
        for number, (source, target) in enumerate(pairs)
    ]
    for load in loads[:8]:
        load.start()
    (l_hid_e, l_hid_a, l_lengths, l_gain_e, l_gain_a, l_fin_e, l_fin_a, l_tokens, l_wq_a, l_wk_a, l_wv_a, l_wq_e, l_wk_e, l_wv_e,
     l_kc_a, l_vc_a, l_kc_e, l_vc_e, l_wo_a, l_wo_e, l_head_a, l_head_e) = loads

    def ty_peer(step):
        return lax.rem(ty // 4 + step // 4, n_ty // 4) * 4 + lax.rem(ty + step, 4)

    def tx_peer(step):
        return lax.rem(tx // 4 + step // 4, n_tx // 4) * 4 + lax.rem(tx + step, 4)

    flat = grp * n_tx + tx
    n_flat = n_grp * n_tx

    def flat_peer(step):
        return {"grp": lax.rem(grp + step // n_tx, n_grp), "tx": tx_peer(lax.rem(step, n_tx))}

    def to_ty(step):
        return {"ty": ty_peer(step)}

    def to_tx(step):
        return {"tx": tx_peer(step)}

    def near(step):
        return {"tx": lax.rem(tx // 4 + step // 4, n_tx // 4) * 4 + lax.rem(tx, 4), "ty": ty_peer(step)}

    barrier = pltpu.get_barrier_semaphore()

    def greet(device):
        pl.semaphore_signal(barrier, inc=1, device_id=device, device_id_type=MESH)

    @pl.loop(1, n_ty)
    def _(step):
        greet(to_ty(n_ty - step))

    @pl.loop(4, n_ty)
    def _(step):
        greet(near(step))

    @pl.loop(1, n_flat)
    def _(step):
        greet(flat_peer(n_flat - step))

    for load in loads[8:14]:
        load.start()

    started = []

    class Exchange:
        def __init__(self, n, source, target, send_sems, recv_sems, device, begin=True):
            self.n = n
            self.make = lambda step: pltpu.make_async_remote_copy(
                src_ref=source(step), dst_ref=target(step), send_sem=send_sems.at[step], recv_sem=recv_sems.at[step],
                device_id=device(step), device_id_type=MESH,
            )
            started.append(self)
            if begin:
                self.begin()

        def begin(self):
            @pl.loop(1, self.n)
            def _(step):
                self.make(self.n - step).start()

        def arrive(self):
            @pl.loop(1, self.n)
            def _(step):
                self.make(step).wait_recv()

        def finish(self):
            @pl.loop(1, self.n)
            def _(step):
                self.make(step).wait_send()

    def add_up(exchange, first, recv):
        def body(step, total):
            exchange.make(step).wait_recv()
            return total + recv[step].astype(F32)

        return lax.fori_loop(1, exchange.n, body, first)

    n_rows = 2 * half_rows
    block = half_rows // n_ty
    order = one_hot(
        n_rows, lambda o: (o // block) % 2 * half_rows + o // (2 * block) * block + o % block
    )
    l_hid_e.wait()
    wide_e = mm(order, v_hid_e[...].reshape(n_rows, width_e))
    x_e[...] = wide_e.reshape(n_ty, 8, width_e)
    l_hid_a.wait()
    wide_a = mm(order, v_hid_a[...].reshape(n_rows, width_a))
    x_a[...] = wide_a.reshape(n_ty, 8, width_a)
    partial = jnp.concatenate([lane_fold(wide_e * wide_e), lane_fold(wide_a * wide_a)], axis=0)
    own = jnp.broadcast_to(jnp.sum(partial.T, axis=0, keepdims=True), (8, HEAD))
    sq_send[...] = own

    pl.semaphore_wait(barrier, n_ty - 1 + n_ty - 4 + n_flat - 1)

    squares = Exchange(n_ty, lambda d: sq_send, lambda d: sq_recv.at[d], ty_send.at[0], ty_recv.at[0], near)
    for load in loads[14:18]:
        load.start()

    row8, lane8 = iota((8, HEAD), 0), iota((8, HEAD), 1)
    position = jnp.zeros((8, HEAD), jnp.int32)
    l_lengths.wait()
    for i in range(block):
        position = jnp.where(row8 % block == i, lengths[i], position)
    position = (position + row8 // block).astype(F32)
    exponent = (lane8 % (HEAD // 2)).astype(F32) * (2.0 / HEAD)
    angle = position * jnp.exp(exponent * (-math.log(BASE)))
    cosine = jnp.cos(angle)
    sine = jnp.where(lane8 < HEAD // 2, -1.0, 1.0) * jnp.sin(angle)

    def rotated(values):
        turned = jnp.concatenate([values[:, HEAD // 2 :], values[:, : HEAD // 2]], axis=1)
        return values * cosine + turned * sine

    total = add_up(squares, own, sq_recv)
    square = jnp.broadcast_to(total[0:1], (HEAD, HEAD)).T
    root_e = lax.rsqrt(square[:n_rows] / (width_e * n_ty) + EPS)
    root_a = lax.rsqrt(square[n_rows:] / (width_a * n_ty) + EPS)

    def project(x, root, g_load, gain, weights, send, recv, kind):
        width = x.shape[2]
        g_load.wait()
        values = x[...].reshape(n_rows, width)
        normed = (values * widen(root, width) * gain[...].astype(F32).reshape(1, width)).astype(BF16)
        parts = []
        for load, weight in weights:
            load.wait()
            columns = weight.shape[1]
            for at in range(0, columns, CHUNK):
                parts.append(mm(normed, weight[:, at : at + min(CHUNK, columns - at)]))
        send[...] = packed(jnp.concatenate(parts, axis=1).reshape(n_ty, 8, -1), send)
        return Exchange(n_ty, lambda d: send.at[ty_peer(d)], lambda d: recv.at[d], ty_send.at[kind], ty_recv.at[kind], to_ty)

    sent_pa = project(x_a, root_a, l_gain_a, v_gain_a, ((l_wq_a, v_wq_a), (l_wk_a, v_wk_a), (l_wv_a, v_wv_a)), p_send_a, p_recv_a, 2)
    sent_pe = project(x_e, root_e, l_gain_e, v_gain_e, ((l_wq_e, v_wq_e), (l_wk_e, v_wk_e), (l_wv_e, v_wv_e)), p_send_e, p_recv_e, 1)

    for load in loads[18:]:
        load.start()

    def summed(exchange, send, recv, me):
        total = add_up(exchange, send[me].astype(F32), recv)
        return total if send.dtype == F32 else unfolded(total)

    def padded(rows, size):
        if rows.shape[0] == size:
            return rows
        return jnp.concatenate([rows, jnp.zeros((size - rows.shape[0], rows.shape[1]), F32)], axis=0)

    def attend(acc, heads, key_heads, k_load, keys, v_load, values):
        group = heads // key_heads
        n_query = heads * 8
        per_row = 2 * heads
        cache = keys.shape[1]
        wide = key_heads * HEAD
        query = jnp.concatenate([rotated(acc[:, h * HEAD : (h + 1) * HEAD]) for h in range(heads)], axis=0)
        at = heads * HEAD
        fresh_k = jnp.concatenate(
            [rotated(acc[:, at + h * HEAD : at + (h + 1) * HEAD]) for h in range(key_heads)], axis=0
        )
        at += wide
        fresh_v = jnp.concatenate(
            [acc[:, at + h * HEAD : at + (h + 1) * HEAD] for h in range(key_heads)], axis=0
        )
        fresh_k = padded(fresh_k, HEAD).astype(BF16)
        fresh_v = padded(fresh_v, HEAD).astype(BF16)
        forth = one_hot(n_query, lambda o: o % heads * 8 + o // heads % 2 * block + o // per_row)
        back = one_hot(n_query, lambda o: o % block * per_row + o // block % 2 * heads + o // 8)
        query = mm(forth, query.astype(BF16))
        owner = iota((n_query, HEAD), 0)
        lane = iota((n_query, HEAD), 1)
        fresh = mm_t(query.astype(BF16), fresh_k) * SCALE
        seen = (
            (lane < key_heads * 8)
            & (lane // 8 == owner % heads // group)
            & (lane % block == owner // per_row)
            & (lane // block % 2 <= owner // heads % 2)
        )
        fresh = jnp.where(seen, fresh, -jnp.inf)
        if key_heads > 1:
            spread = widen(query, wide)
            keep = iota((n_query, wide), 1) // HEAD == iota((n_query, wide), 0) % heads // group
            query = jnp.where(keep, spread, 0.0)
        k_load.wait()
        cached = []
        for i in range(block):
            part = query[i * per_row : (i + 1) * per_row].astype(BF16)
            score = mm_t(part, keys[i]) * SCALE
            cached.append(jnp.where(iota((per_row, cache), 1) < lengths[i], score, -jnp.inf))
        cached = jnp.concatenate(cached, axis=0)
        peak = jnp.maximum(jnp.max(cached, axis=1, keepdims=True), jnp.max(fresh, axis=1, keepdims=True))
        cached = jnp.exp(cached - peak)
        fresh = jnp.exp(fresh - peak)
        total = jnp.sum(cached, axis=1, keepdims=True) + jnp.sum(fresh, axis=1, keepdims=True)
        v_load.wait()
        mixture = jnp.concatenate(
            [mm(cached[i * per_row : (i + 1) * per_row].astype(BF16), values[i]) for i in range(block)], axis=0
        )
        if key_heads > 1:
            picked = jnp.zeros((n_query, HEAD), F32)
            for h in range(key_heads):
                picked = picked + jnp.where(owner % heads // group == h, mixture[:, h * HEAD : (h + 1) * HEAD], 0.0)
            mixture = picked
        mixture = mixture + mm(fresh.astype(BF16), fresh_v)
        ready = mm(back, (mixture / total).astype(BF16))
        return jnp.concatenate([ready[h * 8 : (h + 1) * 8] for h in range(heads)], axis=1)

    def gather(rows, buffer, kind):
        buffer[ty] = folded(rows).astype(BF16)
        return Exchange(n_ty, lambda d: buffer.at[ty], lambda d: buffer.at[ty], ty_send.at[kind], ty_recv.at[kind], to_ty)

    acc = summed(sent_pa, p_send_a, p_recv_a, ty)
    sent_ga = gather(attend(acc, heads_a, v_wk_a.shape[1] // HEAD, l_kc_a, v_kc_a, l_vc_a, v_vc_a), g_a, 4)
    acc = summed(sent_pe, p_send_e, p_recv_e, ty)
    sent_ge = gather(attend(acc, heads_e, v_wk_e.shape[1] // HEAD, l_kc_e, v_kc_e, l_vc_e, v_vc_e), g_e, 3)

    def output(exchange, buffer, load, weight, send, recv, kind):
        exchange.arrive()
        rows = unfolded(buffer[...].astype(F32)).reshape(n_rows, weight.shape[0]).astype(BF16)
        load.wait()
        columns = weight.shape[1]
        parts = [mm(rows, weight[:, at : at + CHUNK]) for at in range(0, columns, CHUNK)]
        send[...] = packed(jnp.concatenate(parts, axis=1).reshape(n_tx, 8, columns), send)
        return Exchange(n_tx, lambda d: send.at[tx_peer(d)], lambda d: recv.at[d], tx_send.at[kind], tx_recv.at[kind], to_tx)

    sent_oa = output(sent_ga, g_a, l_wo_a, v_wo_a, o_send_a, o_recv_a, 1)
    sent_oe = output(sent_ge, g_e, l_wo_e, v_wo_e, o_send_e, o_recv_e, 0)

    def residual(exchange, x, send, recv, s_send, s_recv, kind):
        values = x[tx] + summed(exchange, send, recv, tx)
        part = lane_fold(values * values)
        s_send[...] = part
        return values, part, Exchange(
            n_ty, lambda d: s_send, lambda d: s_recv.at[d], ty_send.at[kind], ty_recv.at[kind], to_ty
        )

    res_a, part_a, sent_sa = residual(sent_oa, x_a, o_send_a, o_recv_a, s_send_a, s_recv_a, 6)
    res_e, part_e, sent_se = residual(sent_oe, x_e, o_send_e, o_recv_e, s_send_e, s_recv_e, 5)

    def final(values, part, exchange, s_recv, g_load, gain, buffer, kind):
        width = values.shape[1]
        g_load.wait()
        part = add_up(exchange, part, s_recv)
        mean = jnp.sum(part, axis=1, keepdims=True) / (width * n_ty)
        rows = values * lax.rsqrt(mean + EPS) * gain[...].astype(F32).reshape(1, width)
        buffer[flat] = folded(rows).astype(BF16)
        across = Exchange(
            n_tx, lambda d: buffer.at[flat], lambda d: buffer.at[flat], tx_send.at[kind], tx_recv.at[kind], to_tx
        )

        def from_tx(step):
            return grp * n_tx + lax.rem(tx // 4 + n_tx // 4 - step // 4, n_tx // 4) * 4 + lax.rem(tx + 4 - lax.rem(step, 4), 4)

        forward = Exchange(
            n_tx, lambda d: buffer.at[from_tx(d)], lambda d: buffer.at[from_tx(d)], fw_send.at[kind - 2],
            fw_recv.at[kind - 2], lambda d: {"grp": 1 - grp}, begin=False,
        )
        forward.make(0).start()
        return across, forward

    def pass_on(pair):
        across, forward = pair

        @pl.loop(1, n_tx)
        def _(step):
            across.make(step).wait_recv()
            forward.make(step).start()

    def passed_on(pair):
        pair[1].make(0).wait_recv()
        pair[1].arrive()

    pair_a = final(res_a, part_a, sent_sa, s_recv_a, l_fin_a, v_fin_a, f_a, 3)
    pair_e = final(res_e, part_e, sent_se, s_recv_e, l_fin_e, v_fin_e, f_e, 2)

    padding = v_head_e.shape[0] - vocab
    l_head_a.wait()
    v_head_a[pl.ds(vocab, padding), :] = jnp.zeros((padding, width_a), BF16)
    l_head_e.wait()
    v_head_e[pl.ds(vocab, padding), :] = jnp.zeros((padding, width_e), BF16)

    n_slab = v_head_e.shape[0] // SLAB

    def logit_exchange(slab, begin=True):
        return Exchange(
            n_ty, lambda d: l_send.at[slab, ty_peer(d)], lambda d: l_recv.at[slab, d], l_ssem.at[slab], l_rsem.at[slab],
            to_ty, begin,
        )

    own_coarse = ty // 4 == grp
    first_from, first_to = jnp.where(own_coarse, 1, 4), jnp.where(own_coarse, 4, n_ty)
    second_from, second_to = jnp.where(own_coarse, 4, 1), jnp.where(own_coarse, n_ty, 4)

    def logits(buffer, half, head, base, low, high):
        rows = unfolded(buffer[pl.ds(half * n_tx, n_tx)].astype(F32)).reshape(n_rows, head.shape[1]).astype(BF16)
        for slab in range(n_slab):
            for at in range(0, SLAB, CHUNK):
                part = mm_t(rows, head[slab * SLAB + at : slab * SLAB + at + CHUNK, :])
                part = part.reshape(n_ty // n_grp, 16, CHUNK).astype(BF16)
                l_send[base + slab, pl.ds(half * (n_ty // n_grp), n_ty // n_grp), :, at : at + CHUNK] = part
            exchange = logit_exchange(base + slab, False)
            started.pop()

            @pl.loop(low, high)
            def _(step):
                exchange.make(step).start()

    pass_on(pair_a)
    logits(f_a, grp, v_head_a, n_slab, first_from, first_to)
    passed_on(pair_a)
    logits(f_a, 1 - grp, v_head_a, n_slab, second_from, second_to)
    pass_on(pair_e)
    logits(f_e, grp, v_head_e, 0, first_from, first_to)
    passed_on(pair_e)
    logits(f_e, 1 - grp, v_head_e, 0, second_from, second_to)

    def slab_sum(slab):
        exchange = logit_exchange(slab, False)
        started.pop()
        return add_up(exchange, l_send[slab, ty].astype(F32), l_recv.at[slab])

    lane_c = iota((16, SLAB), 1)

    def peak_and_total(parts):
        masked = [jnp.where(lane_c + c * SLAB < vocab, part, -jnp.inf) for c, part in enumerate(parts)]
        peak = masked[0]
        for part in masked[1:]:
            peak = jnp.maximum(peak, part)
        peak = jnp.max(peak, axis=1, keepdims=True)
        total = jnp.exp(masked[0] - peak)
        for part in masked[1:]:
            total = total + jnp.exp(part - peak)
        return peak, jnp.sum(total, axis=1, keepdims=True)

    l_tokens.wait()
    row16 = iota((16, HEAD), 0)
    token = jnp.zeros((16, HEAD), jnp.int32)
    for s in range(2):
        for r in range(8):
            token = jnp.where(row16 == r // block * 8 + s * block + r % block, tokens[s, r], token)
    token = widen(token - flat * vocab, SLAB)

    amateur = [slab_sum(n_slab + c) for c in range(n_slab)]
    peak_a, total_a = peak_and_total(amateur)
    expert = [slab_sum(c) for c in range(n_slab)]
    peak_e, total_e = peak_and_total(expert)
    chosen = jnp.zeros((16, SLAB), F32)
    mixed = []
    for c in range(n_slab):
        mixed.append(expert[c] - AMATEUR * amateur[c])
        column = lane_c + c * SLAB
        chosen = chosen + jnp.where((column == token) & (column < vocab), mixed[c], 0.0)
    chosen = jnp.sum(chosen, axis=1, keepdims=True)

    lane16 = iota((16, HEAD), 1) % 64
    tile = jnp.where(lane16 == 0, peak_e, jnp.where(lane16 == 1, total_e, 0.0))
    tile = jnp.where(lane16 == 2, peak_a, jnp.where(lane16 == 3, total_a, tile))
    tile = jnp.where(lane16 == 4, chosen, tile)
    tile = jnp.where(lane8 < 64, tile[:8], tile[8:])
    t_send[...] = tile
    Exchange(n_flat, lambda d: t_send, lambda d: t_recv.at[d], t_ssem, t_rsem, flat_peer).arrive()
    tiles = [tile] + [t_recv[step] for step in range(1, n_flat)]
    highest = functools.reduce(jnp.maximum, tiles)
    picked = functools.reduce(jnp.add, tiles)

    def shifted(values):
        return jnp.concatenate([values[:, 1:], values[:, :1]], axis=1)

    summed_up = functools.reduce(jnp.add, [jnp.exp(t - highest) * shifted(t) for t in tiles])
    log_total = highest + jnp.log(summed_up)

    def column(values, lane):
        return jnp.concatenate([values[:, lane : lane + 1], values[:, lane + 64 : lane + 65]], axis=0)

    offset = column(log_total, 0) - AMATEUR * column(log_total, 2)
    for c in range(n_slab):
        size = min(SLAB, vocab - c * SLAB)
        contrast = mixed[c] - offset
        for s in range(2):
            low = s * block
            out_ref[s, :, c * SLAB : c * SLAB + size] = jnp.concatenate(
                [contrast[low : low + block], contrast[8 + low : 8 + low + block]], axis=0
            )[:, :size]
    value = jnp.broadcast_to(column(picked, 4) - offset, (16, HEAD))
    lane_r = iota((16, HEAD), 1)
    for s in range(2):
        mine = row16 == lane_r // block * 8 + s * block + lane_r % block
        line = jnp.sum(jnp.where(mine & (lane_r < 8), value, 0.0), axis=0, keepdims=True)
        score_ref[s : s + 1, :] = line[:, :8]

    for exchange in started:
        exchange.finish()
    pair_e[1].make(0).wait_send()
    pair_a[1].make(0).wait_send()

    @pl.loop(0, 2 * n_slab)
    def _(slab):
        logit_exchange(slab, False).finish()
        started.pop()


def on_device(axes, *args):
    (
        hid_e, gain_e, wq_e, wk_e, wv_e, wo_e, fin_e, head_e, kc_e, vc_e,
        hid_a, gain_a, wq_a, wk_a, wv_a, wo_a, fin_a, head_a, kc_a, vc_a,
        lengths, tokens,
    ) = args
    n_grp, n_tx, n_ty = axes
    n_flat = n_grp * n_tx
    half = hid_e.shape[1] // n_grp
    vocab = head_e.shape[0]
    padded = -(-vocab // SLAB) * SLAB
    n_slab = padded // SLAB
    n_rows = 2 * half
    width_e, width_a = hid_e.shape[2], hid_a.shape[2]
    cols_e = wq_e.shape[1] + wk_e.shape[1] + wv_e.shape[1]
    cols_a = wq_a.shape[1] + wk_a.shape[1] + wv_a.shape[1]
    inner_e, inner_a = wo_e.shape[0], wo_a.shape[0]

    def like(array):
        return pltpu.VMEM(array.shape, array.dtype)

    scratch = [
        pltpu.SMEM(lengths.shape, jnp.int32), pltpu.SMEM(tokens.shape, jnp.int32),
        like(gain_e), like(fin_e), like(gain_a), like(fin_a),
    ]
    for hid, wq, wk, wv, wo, head, kc, vc in (
        (hid_e, wq_e, wk_e, wv_e, wo_e, head_e, kc_e, vc_e),
        (hid_a, wq_a, wk_a, wv_a, wo_a, head_a, kc_a, vc_a),
    ):
        scratch += [
            pltpu.VMEM((2, half, hid.shape[2]), BF16), like(wq), like(wk), like(wv), like(wo),
            pltpu.VMEM((padded, head.shape[1]), BF16), like(kc), like(vc),
        ]
    scratch += [
        pltpu.VMEM((n_ty, 8, width_e), F32), pltpu.VMEM((n_ty, 8, width_a), F32),
        pltpu.VMEM((8, HEAD), F32), pltpu.VMEM((n_ty, 8, HEAD), F32),
        pltpu.VMEM((n_ty, 8, cols_e), F32), pltpu.VMEM((n_ty, 8, cols_e), F32),
        pltpu.VMEM((n_ty, 16, cols_a // 2), BF16), pltpu.VMEM((n_ty, 16, cols_a // 2), BF16),
        pltpu.VMEM((n_ty, 16, inner_e // 2), BF16), pltpu.VMEM((n_ty, 16, inner_a // 2), BF16),
        pltpu.VMEM((n_tx, 16, width_e // 2), BF16), pltpu.VMEM((n_tx, 16, width_e // 2), BF16),
        pltpu.VMEM((n_tx, 16, width_a // 2), BF16), pltpu.VMEM((n_tx, 16, width_a // 2), BF16),
        pltpu.VMEM((8, HEAD), F32), pltpu.VMEM((n_ty, 8, HEAD), F32),
        pltpu.VMEM((8, HEAD), F32), pltpu.VMEM((n_ty, 8, HEAD), F32),
        pltpu.VMEM((n_flat, 16, width_e // 2), BF16), pltpu.VMEM((n_flat, 16, width_a // 2), BF16),
        pltpu.VMEM((2 * n_slab, n_ty, 16, SLAB), BF16), pltpu.VMEM((2 * n_slab, n_ty, 16, SLAB), BF16),
        pltpu.VMEM((8, HEAD), F32), pltpu.VMEM((n_flat, 8, HEAD), F32),
        pltpu.SemaphoreType.DMA((22,)),
        pltpu.SemaphoreType.DMA((7, n_ty)), pltpu.SemaphoreType.DMA((7, n_ty)),
        pltpu.SemaphoreType.DMA((4, n_tx)), pltpu.SemaphoreType.DMA((4, n_tx)),
        pltpu.SemaphoreType.DMA((2, n_tx)), pltpu.SemaphoreType.DMA((2, n_tx)),
        pltpu.SemaphoreType.DMA((2 * n_slab, n_ty)), pltpu.SemaphoreType.DMA((2 * n_slab, n_ty)),
        pltpu.SemaphoreType.DMA((n_flat,)), pltpu.SemaphoreType.DMA((n_flat,)),
    ]
    hbm = pl.BlockSpec(memory_space=pl.ANY)
    vmem = pl.BlockSpec(memory_space=pltpu.VMEM)
    macs = n_rows * (width_e * (cols_e + inner_e) + width_a * (cols_a + inner_a)) + 2 * n_rows * vocab * (width_e + width_a)
    read = sum(array.size * array.dtype.itemsize for array in args)
    return pl.pallas_call(
        functools.partial(kernel, axes, None),
        out_shape=(
            jax.ShapeDtypeStruct((2, hid_e.shape[1] // n_ty, vocab), F32),
            jax.ShapeDtypeStruct((2, hid_e.shape[1] // n_ty), F32),
        ),
        in_specs=[hbm] * len(args),
        out_specs=(vmem, vmem),
        scratch_shapes=scratch,
        compiler_params=pltpu.CompilerParams(
            collective_id=0, has_side_effects=True, vmem_limit_bytes=56 * 1024 * 1024
        ),
        cost_estimate=pl.CostEstimate(flops=2 * macs, bytes_accessed=read, transcendentals=0),
        name="contrast",
    )(*args)


def solution(mesh):
    model = (
        P(None, None, "ty"), P("ty"), P("ty", "tx"), P("ty", "tx"), P("ty", "tx"), P("tx", "ty"), P("ty"),
        P(("grp", "tx"), "ty"), P(("grp", "ty"), None, "tx"), P(("grp", "ty"), None, "tx"),
    )
    axes = tuple(mesh.shape[name] for name in ("grp", "tx", "ty"))
    return jax.shard_map(
        functools.partial(on_device, axes),
        mesh=mesh,
        in_specs=model + model + (P(("grp", "ty")), P(None, "ty")),
        out_specs=(P(None, "ty", ("grp", "tx")), P(None, "ty")),
        check_vma=False,
    )
```

```python
import functools
import math

import jax
import jax.numpy as jnp
from jax import lax
from jax.experimental import pallas as pl
from jax.experimental.pallas import tpu as pltpu
from jax.sharding import PartitionSpec as P

HEAD = 128
EPS = 1e-05
BASE = 10000.0
AMATEUR = 0.5
SCALE = HEAD**-0.5
CHUNK = 512
SLAB = 1024
F32 = jnp.float32
BF16 = jnp.bfloat16
MESH = pl.DeviceIdType.MESH


def iota(shape, axis):
    return lax.broadcasted_iota(jnp.int32, shape, axis)


def mm(a, b):
    return lax.dot_general(a, b, (((1,), (0,)), ((), ())), preferred_element_type=F32)


def mm_t(a, b):
    return lax.dot_general(a, b, (((1,), (1,)), ((), ())), preferred_element_type=F32)


def one_hot(size, source):
    out = iota((size, size), 0)
    return jnp.where(iota((size, size), 1) == source(out), 1.0, 0.0).astype(BF16)


def folded(values):
    half = values.shape[-1] // 2
    return jnp.concatenate([values[..., :half], values[..., half:]], axis=-2)


def unfolded(values):
    return jnp.concatenate([values[..., :8, :], values[..., 8:, :]], axis=-1)


def packed(values, ref):
    return values if ref.dtype == F32 else folded(values).astype(ref.dtype)


def lane_fold(values):
    total = values[:, :HEAD]
    for start in range(HEAD, values.shape[1], HEAD):
        total = total + values[:, start : start + HEAD]
    return total


def widen(column, width):
    return jnp.concatenate([column] * (width // HEAD), axis=1)


def kernel(axes, dims, *refs):
    n_grp, n_tx, n_ty = axes
    (
        hid_e, gain_e, wq_e, wk_e, wv_e, wo_e, fin_e, head_e, kc_e, vc_e,
        hid_a, gain_a, wq_a, wk_a, wv_a, wo_a, fin_a, head_a, kc_a, vc_a,
        h_lengths, h_tokens,
        out_ref, score_ref,
        lengths, tokens, v_gain_e, v_fin_e, v_gain_a, v_fin_a,
        v_hid_e, v_wq_e, v_wk_e, v_wv_e, v_wo_e, v_head_e, v_kc_e, v_vc_e,
        v_hid_a, v_wq_a, v_wk_a, v_wv_a, v_wo_a, v_head_a, v_kc_a, v_vc_a,
        x_e, x_a, sq_send, sq_recv,
        p_send_e, p_recv_e, p_send_a, p_recv_a,
        g_e, g_a,
        o_send_e, o_recv_e, o_send_a, o_recv_a,
        s_send_e, s_recv_e, s_send_a, s_recv_a,
        f_e, f_a,
        l_send, l_own, a_recv, b_recv, c_send, c_recv, x_keep, x_send, x_recv, t_send, t_recv,
        local_sem, ty_send, ty_recv, tx_send, tx_recv, fw_send, fw_recv, l_ssem, l_rsem, t_ssem, t_rsem,
    ) = refs
    grp, tx, ty = lax.axis_index("grp"), lax.axis_index("tx"), lax.axis_index("ty")
    half_rows = v_hid_e.shape[1]
    width_e, width_a = v_hid_e.shape[2], v_hid_a.shape[2]
    heads_e, heads_a = v_wq_e.shape[1] // HEAD, v_wq_a.shape[1] // HEAD
    vocab = head_e.shape[0]

    first = pl.multiple_of(grp * half_rows, half_rows)
    pairs = [
        (hid_e.at[:, pl.ds(first, half_rows)], v_hid_e),
        (hid_a.at[:, pl.ds(first, half_rows)], v_hid_a),
        (h_lengths, lengths), (gain_e, v_gain_e), (gain_a, v_gain_a),
        (fin_e, v_fin_e), (fin_a, v_fin_a), (h_tokens, tokens),
        (wq_a, v_wq_a), (wk_a, v_wk_a), (wv_a, v_wv_a),
        (wq_e, v_wq_e), (wk_e, v_wk_e), (wv_e, v_wv_e),
        (kc_a, v_kc_a), (vc_a, v_vc_a), (kc_e, v_kc_e), (vc_e, v_vc_e),
        (wo_a, v_wo_a), (wo_e, v_wo_e),
        (head_a, v_head_a.at[pl.ds(0, vocab)]), (head_e, v_head_e.at[pl.ds(0, vocab)]),
    ]
    loads = [
        pltpu.make_async_copy(source, target, local_sem.at[number])
        for number, (source, target) in enumerate(pairs)
    ]
    for load in loads[:8]:
        load.start()
    (l_hid_e, l_hid_a, l_lengths, l_gain_e, l_gain_a, l_fin_e, l_fin_a, l_tokens, l_wq_a, l_wk_a, l_wv_a, l_wq_e, l_wk_e, l_wv_e,
     l_kc_a, l_vc_a, l_kc_e, l_vc_e, l_wo_a, l_wo_e, l_head_a, l_head_e) = loads

    def ty_peer(step):
        return lax.rem(ty // 4 + step // 4, n_ty // 4) * 4 + lax.rem(ty + step, 4)

    def tx_peer(step):
        return lax.rem(tx // 4 + step // 4, n_tx // 4) * 4 + lax.rem(tx + step, 4)

    flat = grp * n_tx + tx
    n_flat = n_grp * n_tx

    def flat_peer(step):
        return {"grp": lax.rem(grp + step // n_tx, n_grp), "tx": tx_peer(lax.rem(step, n_tx))}

    def to_ty(step):
        return {"ty": ty_peer(step)}

    def to_tx(step):
        return {"tx": tx_peer(step)}

    def near(step):
        return {"tx": lax.rem(tx // 4 + step // 4, n_tx // 4) * 4 + lax.rem(tx, 4), "ty": ty_peer(step)}

    barrier = pltpu.get_barrier_semaphore()

    def greet(device):
        pl.semaphore_signal(barrier, inc=1, device_id=device, device_id_type=MESH)

    @pl.loop(1, n_ty)
    def _(step):
        greet(to_ty(n_ty - step))

    @pl.loop(4, n_ty)
    def _(step):
        greet(near(step))

    @pl.loop(1, n_flat)
    def _(step):
        greet(flat_peer(n_flat - step))

    for load in loads[8:14]:
        load.start()

    started = []

    class Exchange:
        def __init__(self, n, source, target, send_sems, recv_sems, device, begin=True):
            self.n = n
            self.make = lambda step: pltpu.make_async_remote_copy(
                src_ref=source(step), dst_ref=target(step), send_sem=send_sems.at[step], recv_sem=recv_sems.at[step],
                device_id=device(step), device_id_type=MESH,
            )
            started.append(self)
            if begin:
                self.begin()

        def begin(self):
            @pl.loop(1, self.n)
            def _(step):
                self.make(self.n - step).start()

        def arrive(self):
            @pl.loop(1, self.n)
            def _(step):
                self.make(step).wait_recv()

        def finish(self):
            @pl.loop(1, self.n)
            def _(step):
                self.make(step).wait_send()

    def add_up(exchange, first, recv):
        def body(step, total):
            exchange.make(step).wait_recv()
            return total + recv[step].astype(F32)

        return lax.fori_loop(1, exchange.n, body, first)

    n_rows = 2 * half_rows
    block = half_rows // n_ty
    order = one_hot(
        n_rows, lambda o: (o // block) % 2 * half_rows + o // (2 * block) * block + o % block
    )
    l_hid_e.wait()
    wide_e = mm(order, v_hid_e[...].reshape(n_rows, width_e))
    x_e[...] = wide_e.reshape(n_ty, 8, width_e)
    l_hid_a.wait()
    wide_a = mm(order, v_hid_a[...].reshape(n_rows, width_a))
    x_a[...] = wide_a.reshape(n_ty, 8, width_a)
    partial = jnp.concatenate([lane_fold(wide_e * wide_e), lane_fold(wide_a * wide_a)], axis=0)
    own = jnp.broadcast_to(jnp.sum(partial.T, axis=0, keepdims=True), (8, HEAD))
    sq_send[...] = own

    pl.semaphore_wait(barrier, n_ty - 1 + n_ty - 4 + n_flat - 1)

    squares = Exchange(n_ty, lambda d: sq_send, lambda d: sq_recv.at[d], ty_send.at[0], ty_recv.at[0], near)
    for load in loads[14:18]:
        load.start()

    row8, lane8 = iota((8, HEAD), 0), iota((8, HEAD), 1)
    position = jnp.zeros((8, HEAD), jnp.int32)
    l_lengths.wait()
    for i in range(block):
        position = jnp.where(row8 % block == i, lengths[i], position)
    position = (position + row8 // block).astype(F32)
    exponent = (lane8 % (HEAD // 2)).astype(F32) * (2.0 / HEAD)
    angle = position * jnp.exp(exponent * (-math.log(BASE)))
    cosine = jnp.cos(angle)
    sine = jnp.where(lane8 < HEAD // 2, -1.0, 1.0) * jnp.sin(angle)

    def rotated(values):
        turned = jnp.concatenate([values[:, HEAD // 2 :], values[:, : HEAD // 2]], axis=1)
        return values * cosine + turned * sine

    total = add_up(squares, own, sq_recv)
    square = jnp.broadcast_to(total[0:1], (HEAD, HEAD)).T
    root_e = lax.rsqrt(square[:n_rows] / (width_e * n_ty) + EPS)
    root_a = lax.rsqrt(square[n_rows:] / (width_a * n_ty) + EPS)

    def project(x, root, g_load, gain, weights, send, recv, kind):
        width = x.shape[2]
        g_load.wait()
        values = x[...].reshape(n_rows, width)
        normed = (values * widen(root, width) * gain[...].astype(F32).reshape(1, width)).astype(BF16)
        parts = []
        for load, weight in weights:
            load.wait()
            columns = weight.shape[1]
            for at in range(0, columns, CHUNK):
                parts.append(mm(normed, weight[:, at : at + min(CHUNK, columns - at)]))
        send[...] = packed(jnp.concatenate(parts, axis=1).reshape(n_ty, 8, -1), send)
        return Exchange(n_ty, lambda d: send.at[ty_peer(d)], lambda d: recv.at[d], ty_send.at[kind], ty_recv.at[kind], to_ty)

    sent_pa = project(x_a, root_a, l_gain_a, v_gain_a, ((l_wq_a, v_wq_a), (l_wk_a, v_wk_a), (l_wv_a, v_wv_a)), p_send_a, p_recv_a, 2)
    sent_pe = project(x_e, root_e, l_gain_e, v_gain_e, ((l_wq_e, v_wq_e), (l_wk_e, v_wk_e), (l_wv_e, v_wv_e)), p_send_e, p_recv_e, 1)

    for load in loads[18:]:
        load.start()

    def summed(exchange, send, recv, me):
        total = add_up(exchange, send[me].astype(F32), recv)
        return total if send.dtype == F32 else unfolded(total)

    def padded(rows, size):
        if rows.shape[0] == size:
            return rows
        return jnp.concatenate([rows, jnp.zeros((size - rows.shape[0], rows.shape[1]), F32)], axis=0)

    def attend(acc, heads, key_heads, k_load, keys, v_load, values):
        group = heads // key_heads
        n_query = heads * 8
        per_row = 2 * heads
        cache = keys.shape[1]
        wide = key_heads * HEAD
        query = jnp.concatenate([rotated(acc[:, h * HEAD : (h + 1) * HEAD]) for h in range(heads)], axis=0)
        at = heads * HEAD
        fresh_k = jnp.concatenate(
            [rotated(acc[:, at + h * HEAD : at + (h + 1) * HEAD]) for h in range(key_heads)], axis=0
        )
        at += wide
        fresh_v = jnp.concatenate(
            [acc[:, at + h * HEAD : at + (h + 1) * HEAD] for h in range(key_heads)], axis=0
        )
        fresh_k = padded(fresh_k, HEAD).astype(BF16)
        fresh_v = padded(fresh_v, HEAD).astype(BF16)
        forth = one_hot(n_query, lambda o: o % heads * 8 + o // heads % 2 * block + o // per_row)
        back = one_hot(n_query, lambda o: o % block * per_row + o // block % 2 * heads + o // 8)
        query = mm(forth, query.astype(BF16))
        owner = iota((n_query, HEAD), 0)
        lane = iota((n_query, HEAD), 1)
        fresh = mm_t(query.astype(BF16), fresh_k) * SCALE
        seen = (
            (lane < key_heads * 8)
            & (lane // 8 == owner % heads // group)
            & (lane % block == owner // per_row)
            & (lane // block % 2 <= owner // heads % 2)
        )
        fresh = jnp.where(seen, fresh, -jnp.inf)
        if key_heads > 1:
            spread = widen(query, wide)
            keep = iota((n_query, wide), 1) // HEAD == iota((n_query, wide), 0) % heads // group
            query = jnp.where(keep, spread, 0.0)
        k_load.wait()
        cached = []
        for i in range(block):
            part = query[i * per_row : (i + 1) * per_row].astype(BF16)
            score = mm_t(part, keys[i]) * SCALE
            cached.append(jnp.where(iota((per_row, cache), 1) < lengths[i], score, -jnp.inf))
        cached = jnp.concatenate(cached, axis=0)
        peak = jnp.maximum(jnp.max(cached, axis=1, keepdims=True), jnp.max(fresh, axis=1, keepdims=True))
        cached = jnp.exp(cached - peak)
        fresh = jnp.exp(fresh - peak)
        total = jnp.sum(cached, axis=1, keepdims=True) + jnp.sum(fresh, axis=1, keepdims=True)
        v_load.wait()
        mixture = jnp.concatenate(
            [mm(cached[i * per_row : (i + 1) * per_row].astype(BF16), values[i]) for i in range(block)], axis=0
        )
        if key_heads > 1:
            picked = jnp.zeros((n_query, HEAD), F32)
            for h in range(key_heads):
                picked = picked + jnp.where(owner % heads // group == h, mixture[:, h * HEAD : (h + 1) * HEAD], 0.0)
            mixture = picked
        mixture = mixture + mm(fresh.astype(BF16), fresh_v)
        ready = mm(back, (mixture / total).astype(BF16))
        return jnp.concatenate([ready[h * 8 : (h + 1) * 8] for h in range(heads)], axis=1)

    def gather(rows, buffer, kind):
        buffer[ty] = folded(rows).astype(BF16)
        return Exchange(n_ty, lambda d: buffer.at[ty], lambda d: buffer.at[ty], ty_send.at[kind], ty_recv.at[kind], to_ty)

    acc = summed(sent_pa, p_send_a, p_recv_a, ty)
    sent_ga = gather(attend(acc, heads_a, v_wk_a.shape[1] // HEAD, l_kc_a, v_kc_a, l_vc_a, v_vc_a), g_a, 4)
    acc = summed(sent_pe, p_send_e, p_recv_e, ty)
    sent_ge = gather(attend(acc, heads_e, v_wk_e.shape[1] // HEAD, l_kc_e, v_kc_e, l_vc_e, v_vc_e), g_e, 3)

    def output(exchange, buffer, load, weight, send, recv, kind):
        exchange.arrive()
        rows = unfolded(buffer[...].astype(F32)).reshape(n_rows, weight.shape[0]).astype(BF16)
        load.wait()
        columns = weight.shape[1]
        parts = [mm(rows, weight[:, at : at + CHUNK]) for at in range(0, columns, CHUNK)]
        send[...] = packed(jnp.concatenate(parts, axis=1).reshape(n_tx, 8, columns), send)
        return Exchange(n_tx, lambda d: send.at[tx_peer(d)], lambda d: recv.at[d], tx_send.at[kind], tx_recv.at[kind], to_tx)

    sent_oa = output(sent_ga, g_a, l_wo_a, v_wo_a, o_send_a, o_recv_a, 1)
    sent_oe = output(sent_ge, g_e, l_wo_e, v_wo_e, o_send_e, o_recv_e, 0)

    def residual(exchange, x, send, recv, s_send, s_recv, kind):
        values = x[tx] + summed(exchange, send, recv, tx)
        part = lane_fold(values * values)
        s_send[...] = part
        return values, part, Exchange(
            n_ty, lambda d: s_send, lambda d: s_recv.at[d], ty_send.at[kind], ty_recv.at[kind], to_ty
        )

    res_a, part_a, sent_sa = residual(sent_oa, x_a, o_send_a, o_recv_a, s_send_a, s_recv_a, 6)
    res_e, part_e, sent_se = residual(sent_oe, x_e, o_send_e, o_recv_e, s_send_e, s_recv_e, 5)

    def final(values, part, exchange, s_recv, g_load, gain, buffer, kind):
        width = values.shape[1]
        g_load.wait()
        part = add_up(exchange, part, s_recv)
        mean = jnp.sum(part, axis=1, keepdims=True) / (width * n_ty)
        rows = values * lax.rsqrt(mean + EPS) * gain[...].astype(F32).reshape(1, width)
        buffer[flat] = folded(rows).astype(BF16)
        across = Exchange(
            n_tx, lambda d: buffer.at[flat], lambda d: buffer.at[flat], tx_send.at[kind], tx_recv.at[kind], to_tx
        )

        def from_tx(step):
            return grp * n_tx + lax.rem(tx // 4 + n_tx // 4 - step // 4, n_tx // 4) * 4 + lax.rem(tx + 4 - lax.rem(step, 4), 4)

        forward = Exchange(
            n_tx, lambda d: buffer.at[from_tx(d)], lambda d: buffer.at[from_tx(d)], fw_send.at[kind - 2],
            fw_recv.at[kind - 2], lambda d: {"grp": 1 - grp}, begin=False,
        )
        forward.make(0).start()
        return across, forward

    def pass_on(pair):
        across, forward = pair

        @pl.loop(1, n_tx)
        def _(step):
            across.make(step).wait_recv()
            forward.make(step).start()

    def passed_on(pair):
        pair[1].make(0).wait_recv()
        pair[1].arrive()

    pair_a = final(res_a, part_a, sent_sa, s_recv_a, l_fin_a, v_fin_a, f_a, 3)
    pair_e = final(res_e, part_e, sent_se, s_recv_e, l_fin_e, v_fin_e, f_e, 2)

    padding = v_head_e.shape[0] - vocab
    l_head_a.wait()
    v_head_a[pl.ds(vocab, padding), :] = jnp.zeros((padding, width_a), BF16)
    l_head_e.wait()
    v_head_e[pl.ds(vocab, padding), :] = jnp.zeros((padding, width_e), BF16)

    n_slab = v_head_e.shape[0] // SLAB

    ring, coarse = lax.rem(ty, 4), ty // 4
    n_unit = 4 * n_slab

    def along(turn):
        return lax.rem(ring + turn + 4, 4)

    def remote(kind, unit, source, target, device):
        return pltpu.make_async_remote_copy(
            src_ref=source, dst_ref=target, send_sem=l_ssem.at[kind, unit], recv_sem=l_rsem.at[kind, unit],
            device_id={"ty": device}, device_id_type=MESH,
        )

    def turn_of(unit):
        return 1 - 2 * (unit % 2)

    def opposite(unit):
        turn = turn_of(unit)
        return remote(0, unit, l_send.at[unit, along(2)], a_recv.at[unit], coarse * 4 + along(turn))

    def straight(unit):
        turn = turn_of(unit)
        return remote(1, unit, l_send.at[unit, along(-turn)], b_recv.at[unit], coarse * 4 + along(-turn))

    def joined(unit):
        turn = turn_of(unit)
        return remote(2, unit, c_send.at[unit], c_recv.at[unit], coarse * 4 + along(turn))

    def across_x(slab):
        return remote(3, slab, x_send.at[slab, 1 - coarse], x_recv.at[slab], (1 - coarse) * 4 + ring)

    def relay(unit):
        opposite(unit).wait_recv()
        c_send[unit] = (l_own[unit, along(turn_of(unit))] + a_recv[unit].astype(F32)).astype(BF16)
        joined(unit).start()

    def settle(unit):
        model, second, slab = unit // (2 * n_slab), unit // n_slab % 2, unit % n_slab
        half = 1 - grp if second else grp
        place = model * n_slab + slab
        straight(unit).wait_recv()
        joined(unit).wait_recv()
        total = l_own[unit, ring] + b_recv[unit].astype(F32) + c_recv[unit].astype(F32)
        x_keep[place, half] = total
        x_send[place, half] = total.astype(BF16)
        if second:
            across_x(place).start()

    def half_rows_of(buffer, half, width):
        return unfolded(buffer[pl.ds(half * n_tx, n_tx)].astype(F32)).reshape(n_rows, width).astype(BF16)

    def logits(rows, head, unit):
        slab = unit % n_slab
        for at in range(0, SLAB, CHUNK):
            part = mm_t(rows, head[slab * SLAB + at : slab * SLAB + at + CHUNK, :]).reshape(4, 16, CHUNK)
            l_own[unit, :, :, at : at + CHUNK] = part
            l_send[unit, :, :, at : at + CHUNK] = part.astype(BF16)
        opposite(unit).start()
        straight(unit).start()

    pass_on(pair_a)
    rows = half_rows_of(f_a, grp, width_a)
    logits(rows, v_head_a, 0)
    logits(rows, v_head_a, 1)
    passed_on(pair_a)
    rows = half_rows_of(f_a, 1 - grp, width_a)
    logits(rows, v_head_a, 2)
    relay(0)
    logits(rows, v_head_a, 3)
    relay(1)
    pass_on(pair_e)
    rows = half_rows_of(f_e, grp, width_e)
    logits(rows, v_head_e, 4)
    relay(2)
    settle(0)
    logits(rows, v_head_e, 5)
    relay(3)
    settle(1)
    passed_on(pair_e)
    rows = half_rows_of(f_e, 1 - grp, width_e)
    logits(rows, v_head_e, 6)
    relay(4)
    settle(2)
    logits(rows, v_head_e, 7)
    relay(5)
    settle(3)
    relay(6)
    settle(4)
    relay(7)
    settle(5)
    settle(6)
    settle(7)

    def slab_sum(slab):
        across_x(slab).wait_recv()
        return x_keep[slab, coarse] + x_recv[slab].astype(F32)

    lane_c = iota((16, SLAB), 1)

    def peak_and_total(parts):
        masked = [jnp.where(lane_c + c * SLAB < vocab, part, -jnp.inf) for c, part in enumerate(parts)]
        peak = masked[0]
        for part in masked[1:]:
            peak = jnp.maximum(peak, part)
        peak = jnp.max(peak, axis=1, keepdims=True)
        total = jnp.exp(masked[0] - peak)
        for part in masked[1:]:
            total = total + jnp.exp(part - peak)
        return peak, jnp.sum(total, axis=1, keepdims=True)

    l_tokens.wait()
    row16 = iota((16, HEAD), 0)
    token = jnp.zeros((16, HEAD), jnp.int32)
    for s in range(2):
        for r in range(8):
            token = jnp.where(row16 == r // block * 8 + s * block + r % block, tokens[s, r], token)
    token = widen(token - flat * vocab, SLAB)

    amateur = [slab_sum(c) for c in range(n_slab)]
    peak_a, total_a = peak_and_total(amateur)
    expert = [slab_sum(n_slab + c) for c in range(n_slab)]
    peak_e, total_e = peak_and_total(expert)
    chosen = jnp.zeros((16, SLAB), F32)
    mixed = []
    for c in range(n_slab):
        mixed.append(expert[c] - AMATEUR * amateur[c])
        column = lane_c + c * SLAB
        chosen = chosen + jnp.where((column == token) & (column < vocab), mixed[c], 0.0)
    chosen = jnp.sum(chosen, axis=1, keepdims=True)

    lane16 = iota((16, HEAD), 1) % 64
    tile = jnp.where(lane16 == 0, peak_e, jnp.where(lane16 == 1, total_e, 0.0))
    tile = jnp.where(lane16 == 2, peak_a, jnp.where(lane16 == 3, total_a, tile))
    tile = jnp.where(lane16 == 4, chosen, tile)
    tile = jnp.where(lane8 < 64, tile[:8], tile[8:])
    t_send[...] = tile
    Exchange(n_flat, lambda d: t_send, lambda d: t_recv.at[d], t_ssem, t_rsem, flat_peer).arrive()
    tiles = [tile] + [t_recv[step] for step in range(1, n_flat)]
    highest = functools.reduce(jnp.maximum, tiles)
    picked = functools.reduce(jnp.add, tiles)

    def shifted(values):
        return jnp.concatenate([values[:, 1:], values[:, :1]], axis=1)

    summed_up = functools.reduce(jnp.add, [jnp.exp(t - highest) * shifted(t) for t in tiles])
    log_total = highest + jnp.log(summed_up)

    def column(values, lane):
        return jnp.concatenate([values[:, lane : lane + 1], values[:, lane + 64 : lane + 65]], axis=0)

    offset = column(log_total, 0) - AMATEUR * column(log_total, 2)
    for c in range(n_slab):
        size = min(SLAB, vocab - c * SLAB)
        contrast = mixed[c] - offset
        for s in range(2):
            low = s * block
            out_ref[s, :, c * SLAB : c * SLAB + size] = jnp.concatenate(
                [contrast[low : low + block], contrast[8 + low : 8 + low + block]], axis=0
            )[:, :size]
    value = jnp.broadcast_to(column(picked, 4) - offset, (16, HEAD))
    lane_r = iota((16, HEAD), 1)
    for s in range(2):
        mine = row16 == lane_r // block * 8 + s * block + lane_r % block
        line = jnp.sum(jnp.where(mine & (lane_r < 8), value, 0.0), axis=0, keepdims=True)
        score_ref[s : s + 1, :] = line[:, :8]

    for exchange in started:
        exchange.finish()
    pair_e[1].make(0).wait_send()
    pair_a[1].make(0).wait_send()

    for unit in range(n_unit):
        opposite(unit).wait_send()
        straight(unit).wait_send()
        joined(unit).wait_send()
    for slab in range(2 * n_slab):
        across_x(slab).wait_send()


def on_device(axes, *args):
    (
        hid_e, gain_e, wq_e, wk_e, wv_e, wo_e, fin_e, head_e, kc_e, vc_e,
        hid_a, gain_a, wq_a, wk_a, wv_a, wo_a, fin_a, head_a, kc_a, vc_a,
        lengths, tokens,
    ) = args
    n_grp, n_tx, n_ty = axes
    n_flat = n_grp * n_tx
    half = hid_e.shape[1] // n_grp
    vocab = head_e.shape[0]
    padded = -(-vocab // SLAB) * SLAB
    n_slab = padded // SLAB
    n_rows = 2 * half
    width_e, width_a = hid_e.shape[2], hid_a.shape[2]
    cols_e = wq_e.shape[1] + wk_e.shape[1] + wv_e.shape[1]
    cols_a = wq_a.shape[1] + wk_a.shape[1] + wv_a.shape[1]
    inner_e, inner_a = wo_e.shape[0], wo_a.shape[0]

    def like(array):
        return pltpu.VMEM(array.shape, array.dtype)

    scratch = [
        pltpu.SMEM(lengths.shape, jnp.int32), pltpu.SMEM(tokens.shape, jnp.int32),
        like(gain_e), like(fin_e), like(gain_a), like(fin_a),
    ]
    for hid, wq, wk, wv, wo, head, kc, vc in (
        (hid_e, wq_e, wk_e, wv_e, wo_e, head_e, kc_e, vc_e),
        (hid_a, wq_a, wk_a, wv_a, wo_a, head_a, kc_a, vc_a),
    ):
        scratch += [
            pltpu.VMEM((2, half, hid.shape[2]), BF16), like(wq), like(wk), like(wv), like(wo),
            pltpu.VMEM((padded, head.shape[1]), BF16), like(kc), like(vc),
        ]
    scratch += [
        pltpu.VMEM((n_ty, 8, width_e), F32), pltpu.VMEM((n_ty, 8, width_a), F32),
        pltpu.VMEM((8, HEAD), F32), pltpu.VMEM((n_ty, 8, HEAD), F32),
        pltpu.VMEM((n_ty, 8, cols_e), F32), pltpu.VMEM((n_ty, 8, cols_e), F32),
        pltpu.VMEM((n_ty, 16, cols_a // 2), BF16), pltpu.VMEM((n_ty, 16, cols_a // 2), BF16),
        pltpu.VMEM((n_ty, 16, inner_e // 2), BF16), pltpu.VMEM((n_ty, 16, inner_a // 2), BF16),
        pltpu.VMEM((n_tx, 16, width_e // 2), BF16), pltpu.VMEM((n_tx, 16, width_e // 2), BF16),
        pltpu.VMEM((n_tx, 16, width_a // 2), BF16), pltpu.VMEM((n_tx, 16, width_a // 2), BF16),
        pltpu.VMEM((8, HEAD), F32), pltpu.VMEM((n_ty, 8, HEAD), F32),
        pltpu.VMEM((8, HEAD), F32), pltpu.VMEM((n_ty, 8, HEAD), F32),
        pltpu.VMEM((n_flat, 16, width_e // 2), BF16), pltpu.VMEM((n_flat, 16, width_a // 2), BF16),
        pltpu.VMEM((4 * n_slab, 4, 16, SLAB), BF16), pltpu.VMEM((4 * n_slab, 4, 16, SLAB), F32),
        pltpu.VMEM((4 * n_slab, 16, SLAB), BF16), pltpu.VMEM((4 * n_slab, 16, SLAB), BF16),
        pltpu.VMEM((4 * n_slab, 16, SLAB), BF16), pltpu.VMEM((4 * n_slab, 16, SLAB), BF16),
        pltpu.VMEM((2 * n_slab, 2, 16, SLAB), F32), pltpu.VMEM((2 * n_slab, 2, 16, SLAB), BF16),
        pltpu.VMEM((2 * n_slab, 16, SLAB), BF16),
        pltpu.VMEM((8, HEAD), F32), pltpu.VMEM((n_flat, 8, HEAD), F32),
        pltpu.SemaphoreType.DMA((22,)),
        pltpu.SemaphoreType.DMA((7, n_ty)), pltpu.SemaphoreType.DMA((7, n_ty)),
        pltpu.SemaphoreType.DMA((4, n_tx)), pltpu.SemaphoreType.DMA((4, n_tx)),
        pltpu.SemaphoreType.DMA((2, n_tx)), pltpu.SemaphoreType.DMA((2, n_tx)),
        pltpu.SemaphoreType.DMA((4, 4 * n_slab)), pltpu.SemaphoreType.DMA((4, 4 * n_slab)),
        pltpu.SemaphoreType.DMA((n_flat,)), pltpu.SemaphoreType.DMA((n_flat,)),
    ]
    hbm = pl.BlockSpec(memory_space=pl.ANY)
    vmem = pl.BlockSpec(memory_space=pltpu.VMEM)
    macs = n_rows * (width_e * (cols_e + inner_e) + width_a * (cols_a + inner_a)) + 2 * n_rows * vocab * (width_e + width_a)
    read = sum(array.size * array.dtype.itemsize for array in args)
    return pl.pallas_call(
        functools.partial(kernel, axes, None),
        out_shape=(
            jax.ShapeDtypeStruct((2, hid_e.shape[1] // n_ty, vocab), F32),
            jax.ShapeDtypeStruct((2, hid_e.shape[1] // n_ty), F32),
        ),
        in_specs=[hbm] * len(args),
        out_specs=(vmem, vmem),
        scratch_shapes=scratch,
        compiler_params=pltpu.CompilerParams(
            collective_id=0, has_side_effects=True, vmem_limit_bytes=56 * 1024 * 1024
        ),
        cost_estimate=pl.CostEstimate(flops=2 * macs, bytes_accessed=read, transcendentals=0),
        name="contrast",
    )(*args)


def solution(mesh):
    model = (
        P(None, None, "ty"), P("ty"), P("ty", "tx"), P("ty", "tx"), P("ty", "tx"), P("tx", "ty"), P("ty"),
        P(("grp", "tx"), "ty"), P(("grp", "ty"), None, "tx"), P(("grp", "ty"), None, "tx"),
    )
    axes = tuple(mesh.shape[name] for name in ("grp", "tx", "ty"))
    return jax.shard_map(
        functools.partial(on_device, axes),
        mesh=mesh,
        in_specs=model + model + (P(("grp", "ty")), P(None, "ty")),
        out_specs=(P(None, "ty", ("grp", "tx")), P(None, "ty")),
        check_vma=False,
    )
```

```python
import functools
import math

import jax
import jax.numpy as jnp
from jax import lax
from jax.experimental import pallas as pl
from jax.experimental.pallas import tpu as pltpu
from jax.sharding import PartitionSpec as P

HEAD = 128
EPS = 1e-05
BASE = 10000.0
AMATEUR = 0.5
SCALE = HEAD**-0.5
CHUNK = 512
SLAB = 1024
F32 = jnp.float32
BF16 = jnp.bfloat16
MESH = pl.DeviceIdType.MESH


def iota(shape, axis):
    return lax.broadcasted_iota(jnp.int32, shape, axis)


def mm(a, b):
    return lax.dot_general(a, b, (((1,), (0,)), ((), ())), preferred_element_type=F32)


def mm_t(a, b):
    return lax.dot_general(a, b, (((1,), (1,)), ((), ())), preferred_element_type=F32)


def one_hot(size, source):
    out = iota((size, size), 0)
    return jnp.where(iota((size, size), 1) == source(out), 1.0, 0.0).astype(BF16)


def folded(values):
    half = values.shape[-1] // 2
    return jnp.concatenate([values[..., :half], values[..., half:]], axis=-2)


def unfolded(values):
    return jnp.concatenate([values[..., :8, :], values[..., 8:, :]], axis=-1)


def packed(values, ref):
    return values if ref.dtype == F32 else folded(values).astype(ref.dtype)


def lane_fold(values):
    total = values[:, :HEAD]
    for start in range(HEAD, values.shape[1], HEAD):
        total = total + values[:, start : start + HEAD]
    return total


def widen(column, width):
    return jnp.concatenate([column] * (width // HEAD), axis=1)


def kernel(axes, dims, *refs):
    n_grp, n_tx, n_ty = axes
    (
        hid_e, gain_e, wq_e, wk_e, wv_e, wo_e, fin_e, head_e, kc_e, vc_e,
        hid_a, gain_a, wq_a, wk_a, wv_a, wo_a, fin_a, head_a, kc_a, vc_a,
        h_lengths, h_tokens,
        out_ref, score_ref,
        lengths, tokens, v_gain_e, v_fin_e, v_gain_a, v_fin_a,
        v_hid_e, v_wq_e, v_wk_e, v_wv_e, v_wo_e, v_head_e, v_kc_e, v_vc_e,
        v_hid_a, v_wq_a, v_wk_a, v_wv_a, v_wo_a, v_head_a, v_kc_a, v_vc_a,
        x_e, x_a, sq_send, sq_recv,
        p_send_e, p_recv_e, p_send_a, p_recv_a,
        g_e, g_a,
        o_send_e, o_recv_e, o_send_a, o_recv_a,
        s_send_e, s_recv_e, s_send_a, s_recv_a,
        f_e, f_a,
        l_send, l_recv, t_send, t_recv,
        local_sem, ty_send, ty_recv, tx_send, tx_recv, f_ssem, f_rsem, l_ssem, l_rsem, t_ssem, t_rsem,
    ) = refs
    grp, tx, ty = lax.axis_index("grp"), lax.axis_index("tx"), lax.axis_index("ty")
    half_rows = v_hid_e.shape[1]
    width_e, width_a = v_hid_e.shape[2], v_hid_a.shape[2]
    heads_e, heads_a = v_wq_e.shape[1] // HEAD, v_wq_a.shape[1] // HEAD
    vocab = head_e.shape[0]

    first = pl.multiple_of(grp * half_rows, half_rows)
    pairs = [
        (hid_e.at[:, pl.ds(first, half_rows)], v_hid_e),
        (hid_a.at[:, pl.ds(first, half_rows)], v_hid_a),
        (h_lengths, lengths), (gain_e, v_gain_e), (gain_a, v_gain_a),
        (fin_e, v_fin_e), (fin_a, v_fin_a), (h_tokens, tokens),
        (wq_a, v_wq_a), (wk_a, v_wk_a), (wv_a, v_wv_a),
        (wq_e, v_wq_e), (wk_e, v_wk_e), (wv_e, v_wv_e),
        (kc_a, v_kc_a), (vc_a, v_vc_a), (kc_e, v_kc_e), (vc_e, v_vc_e),
        (wo_a, v_wo_a), (wo_e, v_wo_e),
        (head_a, v_head_a.at[pl.ds(0, vocab)]), (head_e, v_head_e.at[pl.ds(0, vocab)]),
    ]
    loads = [
        pltpu.make_async_copy(source, target, local_sem.at[number])
        for number, (source, target) in enumerate(pairs)
    ]
    for load in loads[:8]:
        load.start()
    (l_hid_e, l_hid_a, l_lengths, l_gain_e, l_gain_a, l_fin_e, l_fin_a, l_tokens, l_wq_a, l_wk_a, l_wv_a, l_wq_e, l_wk_e, l_wv_e,
     l_kc_a, l_vc_a, l_kc_e, l_vc_e, l_wo_a, l_wo_e, l_head_a, l_head_e) = loads

    def ty_peer(step):
        return lax.rem(ty // 4 + step // 4, n_ty // 4) * 4 + lax.rem(ty + step, 4)

    def tx_peer(step):
        return lax.rem(tx // 4 + step // 4, n_tx // 4) * 4 + lax.rem(tx + step, 4)

    flat = grp * n_tx + tx
    n_flat = n_grp * n_tx

    def flat_peer(step):
        return {"grp": lax.rem(grp + step // n_tx, n_grp), "tx": tx_peer(lax.rem(step, n_tx))}

    def to_ty(step):
        return {"ty": ty_peer(step)}

    def to_tx(step):
        return {"tx": tx_peer(step)}

    def near(step):
        return {"tx": lax.rem(tx // 4 + step // 4, n_tx // 4) * 4 + lax.rem(tx, 4), "ty": ty_peer(step)}

    barrier = pltpu.get_barrier_semaphore()

    def greet(device):
        pl.semaphore_signal(barrier, inc=1, device_id=device, device_id_type=MESH)

    @pl.loop(1, n_ty)
    def _(step):
        greet(to_ty(n_ty - step))

    @pl.loop(4, n_ty)
    def _(step):
        greet(near(step))

    @pl.loop(1, n_flat)
    def _(step):
        greet(flat_peer(n_flat - step))

    for load in loads[8:14]:
        load.start()

    started = []

    class Exchange:
        def __init__(self, n, source, target, send_sems, recv_sems, device, begin=True):
            self.n = n
            self.make = lambda step: pltpu.make_async_remote_copy(
                src_ref=source(step), dst_ref=target(step), send_sem=send_sems.at[step], recv_sem=recv_sems.at[step],
                device_id=device(step), device_id_type=MESH,
            )
            started.append(self)
            if begin:
                self.begin()

        def begin(self):
            @pl.loop(1, self.n)
            def _(step):
                self.make(self.n - step).start()

        def arrive(self):
            @pl.loop(1, self.n)
            def _(step):
                self.make(step).wait_recv()

        def finish(self):
            @pl.loop(1, self.n)
            def _(step):
                self.make(step).wait_send()

    def add_up(exchange, first, recv):
        def body(step, total):
            exchange.make(step).wait_recv()
            return total + recv[step].astype(F32)

        return lax.fori_loop(1, exchange.n, body, first)

    n_rows = 2 * half_rows
    block = half_rows // n_ty
    order = one_hot(
        n_rows, lambda o: (o // block) % 2 * half_rows + o // (2 * block) * block + o % block
    )
    l_hid_e.wait()
    wide_e = mm(order, v_hid_e[...].reshape(n_rows, width_e))
    x_e[...] = wide_e.reshape(n_ty, 8, width_e)
    l_hid_a.wait()
    wide_a = mm(order, v_hid_a[...].reshape(n_rows, width_a))
    x_a[...] = wide_a.reshape(n_ty, 8, width_a)
    partial = jnp.concatenate([lane_fold(wide_e * wide_e), lane_fold(wide_a * wide_a)], axis=0)
    own = jnp.broadcast_to(jnp.sum(partial.T, axis=0, keepdims=True), (8, HEAD))
    sq_send[...] = own

    pl.semaphore_wait(barrier, n_ty - 1 + n_ty - 4 + n_flat - 1)

    squares = Exchange(n_ty, lambda d: sq_send, lambda d: sq_recv.at[d], ty_send.at[0], ty_recv.at[0], near)
    for load in loads[14:18]:
        load.start()

    row8, lane8 = iota((8, HEAD), 0), iota((8, HEAD), 1)
    position = jnp.zeros((8, HEAD), jnp.int32)
    l_lengths.wait()
    for i in range(block):
        position = jnp.where(row8 % block == i, lengths[i], position)
    position = (position + row8 // block).astype(F32)
    exponent = (lane8 % (HEAD // 2)).astype(F32) * (2.0 / HEAD)
    angle = position * jnp.exp(exponent * (-math.log(BASE)))
    cosine = jnp.cos(angle)
    sine = jnp.where(lane8 < HEAD // 2, -1.0, 1.0) * jnp.sin(angle)

    def rotated(values):
        turned = jnp.concatenate([values[:, HEAD // 2 :], values[:, : HEAD // 2]], axis=1)
        return values * cosine + turned * sine

    total = add_up(squares, own, sq_recv)
    square = jnp.broadcast_to(total[0:1], (HEAD, HEAD)).T
    root_e = lax.rsqrt(square[:n_rows] / (width_e * n_ty) + EPS)
    root_a = lax.rsqrt(square[n_rows:] / (width_a * n_ty) + EPS)

    def project(x, root, g_load, gain, weights, send, recv, kind):
        width = x.shape[2]
        g_load.wait()
        values = x[...].reshape(n_rows, width)
        normed = (values * widen(root, width) * gain[...].astype(F32).reshape(1, width)).astype(BF16)
        parts = []
        for load, weight in weights:
            load.wait()
            columns = weight.shape[1]
            for at in range(0, columns, CHUNK):
                parts.append(mm(normed, weight[:, at : at + min(CHUNK, columns - at)]))
        send[...] = packed(jnp.concatenate(parts, axis=1).reshape(n_ty, 8, -1), send)
        return Exchange(n_ty, lambda d: send.at[ty_peer(d)], lambda d: recv.at[d], ty_send.at[kind], ty_recv.at[kind], to_ty)

    sent_pa = project(x_a, root_a, l_gain_a, v_gain_a, ((l_wq_a, v_wq_a), (l_wk_a, v_wk_a), (l_wv_a, v_wv_a)), p_send_a, p_recv_a, 2)
    sent_pe = project(x_e, root_e, l_gain_e, v_gain_e, ((l_wq_e, v_wq_e), (l_wk_e, v_wk_e), (l_wv_e, v_wv_e)), p_send_e, p_recv_e, 1)

    for load in loads[18:]:
        load.start()

    def summed(exchange, send, recv, me):
        total = add_up(exchange, send[me].astype(F32), recv)
        return total if send.dtype == F32 else unfolded(total)

    def padded(rows, size):
        if rows.shape[0] == size:
            return rows
        return jnp.concatenate([rows, jnp.zeros((size - rows.shape[0], rows.shape[1]), F32)], axis=0)

    def attend(acc, heads, key_heads, k_load, keys, v_load, values):
        group = heads // key_heads
        n_query = heads * 8
        per_row = 2 * heads
        cache = keys.shape[1]
        wide = key_heads * HEAD
        query = jnp.concatenate([rotated(acc[:, h * HEAD : (h + 1) * HEAD]) for h in range(heads)], axis=0)
        at = heads * HEAD
        fresh_k = jnp.concatenate(
            [rotated(acc[:, at + h * HEAD : at + (h + 1) * HEAD]) for h in range(key_heads)], axis=0
        )
        at += wide
        fresh_v = jnp.concatenate(
            [acc[:, at + h * HEAD : at + (h + 1) * HEAD] for h in range(key_heads)], axis=0
        )
        fresh_k = padded(fresh_k, HEAD).astype(BF16)
        fresh_v = padded(fresh_v, HEAD).astype(BF16)
        forth = one_hot(n_query, lambda o: o % heads * 8 + o // heads % 2 * block + o // per_row)
        back = one_hot(n_query, lambda o: o % block * per_row + o // block % 2 * heads + o // 8)
        query = mm(forth, query.astype(BF16))
        owner = iota((n_query, HEAD), 0)
        lane = iota((n_query, HEAD), 1)
        fresh = mm_t(query.astype(BF16), fresh_k) * SCALE
        seen = (
            (lane < key_heads * 8)
            & (lane // 8 == owner % heads // group)
            & (lane % block == owner // per_row)
            & (lane // block % 2 <= owner // heads % 2)
        )
        fresh = jnp.where(seen, fresh, -jnp.inf)
        if key_heads > 1:
            spread = widen(query, wide)
            keep = iota((n_query, wide), 1) // HEAD == iota((n_query, wide), 0) % heads // group
            query = jnp.where(keep, spread, 0.0)
        k_load.wait()
        cached = []
        for i in range(block):
            part = query[i * per_row : (i + 1) * per_row].astype(BF16)
            score = mm_t(part, keys[i]) * SCALE
            cached.append(jnp.where(iota((per_row, cache), 1) < lengths[i], score, -jnp.inf))
        cached = jnp.concatenate(cached, axis=0)
        peak = jnp.maximum(jnp.max(cached, axis=1, keepdims=True), jnp.max(fresh, axis=1, keepdims=True))
        cached = jnp.exp(cached - peak)
        fresh = jnp.exp(fresh - peak)
        total = jnp.sum(cached, axis=1, keepdims=True) + jnp.sum(fresh, axis=1, keepdims=True)
        v_load.wait()
        mixture = jnp.concatenate(
            [mm(cached[i * per_row : (i + 1) * per_row].astype(BF16), values[i]) for i in range(block)], axis=0
        )
        if key_heads > 1:
            picked = jnp.zeros((n_query, HEAD), F32)
            for h in range(key_heads):
                picked = picked + jnp.where(owner % heads // group == h, mixture[:, h * HEAD : (h + 1) * HEAD], 0.0)
            mixture = picked
        mixture = mixture + mm(fresh.astype(BF16), fresh_v)
        ready = mm(back, (mixture / total).astype(BF16))
        return jnp.concatenate([ready[h * 8 : (h + 1) * 8] for h in range(heads)], axis=1)

    def gather(rows, buffer, kind):
        buffer[ty] = folded(rows).astype(BF16)
        return Exchange(n_ty, lambda d: buffer.at[ty], lambda d: buffer.at[ty], ty_send.at[kind], ty_recv.at[kind], to_ty)

    acc = summed(sent_pa, p_send_a, p_recv_a, ty)
    sent_ga = gather(attend(acc, heads_a, v_wk_a.shape[1] // HEAD, l_kc_a, v_kc_a, l_vc_a, v_vc_a), g_a, 4)
    acc = summed(sent_pe, p_send_e, p_recv_e, ty)
    sent_ge = gather(attend(acc, heads_e, v_wk_e.shape[1] // HEAD, l_kc_e, v_kc_e, l_vc_e, v_vc_e), g_e, 3)

    def output(exchange, buffer, load, weight, send, recv, kind):
        exchange.arrive()
        rows = unfolded(buffer[...].astype(F32)).reshape(n_rows, weight.shape[0]).astype(BF16)
        load.wait()
        columns = weight.shape[1]
        parts = [mm(rows, weight[:, at : at + CHUNK]) for at in range(0, columns, CHUNK)]
        send[...] = packed(jnp.concatenate(parts, axis=1).reshape(n_tx, 8, columns), send)
        return Exchange(n_tx, lambda d: send.at[tx_peer(d)], lambda d: recv.at[d], tx_send.at[kind], tx_recv.at[kind], to_tx)

    sent_oa = output(sent_ga, g_a, l_wo_a, v_wo_a, o_send_a, o_recv_a, 1)
    sent_oe = output(sent_ge, g_e, l_wo_e, v_wo_e, o_send_e, o_recv_e, 0)

    def residual(exchange, x, send, recv, s_send, s_recv, kind):
        values = x[tx] + summed(exchange, send, recv, tx)
        part = lane_fold(values * values)
        s_send[...] = part
        return values, part, Exchange(
            n_ty, lambda d: s_send, lambda d: s_recv.at[d], ty_send.at[kind], ty_recv.at[kind], to_ty
        )

    def final(values, part, exchange, s_recv, g_load, gain, buffer, kind):
        width = values.shape[1]
        g_load.wait()
        part = add_up(exchange, part, s_recv)
        mean = jnp.sum(part, axis=1, keepdims=True) / (width * n_ty)
        rows = values * lax.rsqrt(mean + EPS) * gain[...].astype(F32).reshape(1, width)
        buffer[flat] = folded(rows).astype(BF16)
        return Exchange(
            n_flat, lambda d: buffer.at[flat], lambda d: buffer.at[flat], f_ssem.at[kind], f_rsem.at[kind], flat_peer
        )

    res_a, part_a, sent_sa = residual(sent_oa, x_a, o_send_a, o_recv_a, s_send_a, s_recv_a, 6)
    sent_fa = final(res_a, part_a, sent_sa, s_recv_a, l_fin_a, v_fin_a, f_a, 0)
    res_e, part_e, sent_se = residual(sent_oe, x_e, o_send_e, o_recv_e, s_send_e, s_recv_e, 5)

    padding = v_head_e.shape[0] - vocab
    l_head_a.wait()
    v_head_a[pl.ds(vocab, padding), :] = jnp.zeros((padding, width_a), BF16)
    l_head_e.wait()
    v_head_e[pl.ds(vocab, padding), :] = jnp.zeros((padding, width_e), BF16)

    n_slab = v_head_e.shape[0] // SLAB

    def logit_exchange(slab, begin=True):
        return Exchange(
            n_ty, lambda d: l_send.at[slab, ty_peer(d)], lambda d: l_recv.at[slab, d], l_ssem.at[slab], l_rsem.at[slab],
            to_ty, begin,
        )

    def all_rows(exchange, buffer, width):
        exchange.arrive()
        return unfolded(buffer[...].astype(F32)).reshape(n_flat * 8, width).astype(BF16)

    def logits(rows, head, base, slab):
        for at in range(0, SLAB, CHUNK):
            part = mm_t(rows, head[slab * SLAB + at : slab * SLAB + at + CHUNK, :])
            l_send[base + slab, :, :, at : at + CHUNK] = part.reshape(n_ty, 16, CHUNK).astype(BF16)
        logit_exchange(base + slab)
        started.pop()

    rows = all_rows(sent_fa, f_a, width_a)
    logits(rows, v_head_a, n_slab, 0)
    sent_fe = final(res_e, part_e, sent_se, s_recv_e, l_fin_e, v_fin_e, f_e, 1)
    for slab in range(1, n_slab):
        logits(rows, v_head_a, n_slab, slab)
    rows = all_rows(sent_fe, f_e, width_e)
    for slab in range(n_slab):
        logits(rows, v_head_e, 0, slab)

    def slab_sum(slab):
        exchange = logit_exchange(slab, False)
        started.pop()
        return add_up(exchange, l_send[slab, ty].astype(F32), l_recv.at[slab])

    lane_c = iota((16, SLAB), 1)

    def peak_and_total(parts):
        masked = [jnp.where(lane_c + c * SLAB < vocab, part, -jnp.inf) for c, part in enumerate(parts)]
        peak = masked[0]
        for part in masked[1:]:
            peak = jnp.maximum(peak, part)
        peak = jnp.max(peak, axis=1, keepdims=True)
        total = jnp.exp(masked[0] - peak)
        for part in masked[1:]:
            total = total + jnp.exp(part - peak)
        return peak, jnp.sum(total, axis=1, keepdims=True)

    l_tokens.wait()
    row16 = iota((16, HEAD), 0)
    token = jnp.zeros((16, HEAD), jnp.int32)
    for s in range(2):
        for r in range(8):
            token = jnp.where(row16 == r // block * 8 + s * block + r % block, tokens[s, r], token)
    token = widen(token - flat * vocab, SLAB)

    amateur = [slab_sum(n_slab + c) for c in range(n_slab)]
    peak_a, total_a = peak_and_total(amateur)
    expert = [slab_sum(c) for c in range(n_slab)]
    peak_e, total_e = peak_and_total(expert)
    chosen = jnp.zeros((16, SLAB), F32)
    mixed = []
    for c in range(n_slab):
        mixed.append(expert[c] - AMATEUR * amateur[c])
        column = lane_c + c * SLAB
        chosen = chosen + jnp.where((column == token) & (column < vocab), mixed[c], 0.0)
    chosen = jnp.sum(chosen, axis=1, keepdims=True)

    lane16 = iota((16, HEAD), 1) % 64
    tile = jnp.where(lane16 == 0, peak_e, jnp.where(lane16 == 1, total_e, 0.0))
    tile = jnp.where(lane16 == 2, peak_a, jnp.where(lane16 == 3, total_a, tile))
    tile = jnp.where(lane16 == 4, chosen, tile)
    tile = jnp.where(lane8 < 64, tile[:8], tile[8:])
    t_send[...] = tile
    Exchange(n_flat, lambda d: t_send, lambda d: t_recv.at[d], t_ssem, t_rsem, flat_peer).arrive()
    tiles = [tile] + [t_recv[step] for step in range(1, n_flat)]
    highest = functools.reduce(jnp.maximum, tiles)
    picked = functools.reduce(jnp.add, tiles)

    def shifted(values):
        return jnp.concatenate([values[:, 1:], values[:, :1]], axis=1)

    summed_up = functools.reduce(jnp.add, [jnp.exp(t - highest) * shifted(t) for t in tiles])
    log_total = highest + jnp.log(summed_up)

    def column(values, lane):
        return jnp.concatenate([values[:, lane : lane + 1], values[:, lane + 64 : lane + 65]], axis=0)

    offset = column(log_total, 0) - AMATEUR * column(log_total, 2)
    for c in range(n_slab):
        size = min(SLAB, vocab - c * SLAB)
        contrast = mixed[c] - offset
        for s in range(2):
            low = s * block
            out_ref[s, :, c * SLAB : c * SLAB + size] = jnp.concatenate(
                [contrast[low : low + block], contrast[8 + low : 8 + low + block]], axis=0
            )[:, :size]
    value = jnp.broadcast_to(column(picked, 4) - offset, (16, HEAD))
    lane_r = iota((16, HEAD), 1)
    for s in range(2):
        mine = row16 == lane_r // block * 8 + s * block + lane_r % block
        line = jnp.sum(jnp.where(mine & (lane_r < 8), value, 0.0), axis=0, keepdims=True)
        score_ref[s : s + 1, :] = line[:, :8]

    for exchange in started:
        exchange.finish()

    @pl.loop(0, 2 * n_slab)
    def _(slab):
        logit_exchange(slab, False).finish()
        started.pop()


def on_device(axes, *args):
    (
        hid_e, gain_e, wq_e, wk_e, wv_e, wo_e, fin_e, head_e, kc_e, vc_e,
        hid_a, gain_a, wq_a, wk_a, wv_a, wo_a, fin_a, head_a, kc_a, vc_a,
        lengths, tokens,
    ) = args
    n_grp, n_tx, n_ty = axes
    n_flat = n_grp * n_tx
    half = hid_e.shape[1] // n_grp
    vocab = head_e.shape[0]
    padded = -(-vocab // SLAB) * SLAB
    n_slab = padded // SLAB
    n_rows = 2 * half
    width_e, width_a = hid_e.shape[2], hid_a.shape[2]
    cols_e = wq_e.shape[1] + wk_e.shape[1] + wv_e.shape[1]
    cols_a = wq_a.shape[1] + wk_a.shape[1] + wv_a.shape[1]
    inner_e, inner_a = wo_e.shape[0], wo_a.shape[0]

    def like(array):
        return pltpu.VMEM(array.shape, array.dtype)

    scratch = [
        pltpu.SMEM(lengths.shape, jnp.int32), pltpu.SMEM(tokens.shape, jnp.int32),
        like(gain_e), like(fin_e), like(gain_a), like(fin_a),
    ]
    for hid, wq, wk, wv, wo, head, kc, vc in (
        (hid_e, wq_e, wk_e, wv_e, wo_e, head_e, kc_e, vc_e),
        (hid_a, wq_a, wk_a, wv_a, wo_a, head_a, kc_a, vc_a),
    ):
        scratch += [
            pltpu.VMEM((2, half, hid.shape[2]), BF16), like(wq), like(wk), like(wv), like(wo),
            pltpu.VMEM((padded, head.shape[1]), BF16), like(kc), like(vc),
        ]
    scratch += [
        pltpu.VMEM((n_ty, 8, width_e), F32), pltpu.VMEM((n_ty, 8, width_a), F32),
        pltpu.VMEM((8, HEAD), F32), pltpu.VMEM((n_ty, 8, HEAD), F32),
        pltpu.VMEM((n_ty, 8, cols_e), F32), pltpu.VMEM((n_ty, 8, cols_e), F32),
        pltpu.VMEM((n_ty, 16, cols_a // 2), BF16), pltpu.VMEM((n_ty, 16, cols_a // 2), BF16),
        pltpu.VMEM((n_ty, 16, inner_e // 2), BF16), pltpu.VMEM((n_ty, 16, inner_a // 2), BF16),
        pltpu.VMEM((n_tx, 16, width_e // 2), BF16), pltpu.VMEM((n_tx, 16, width_e // 2), BF16),
        pltpu.VMEM((n_tx, 16, width_a // 2), BF16), pltpu.VMEM((n_tx, 16, width_a // 2), BF16),
        pltpu.VMEM((8, HEAD), F32), pltpu.VMEM((n_ty, 8, HEAD), F32),
        pltpu.VMEM((8, HEAD), F32), pltpu.VMEM((n_ty, 8, HEAD), F32),
        pltpu.VMEM((n_flat, 16, width_e // 2), BF16), pltpu.VMEM((n_flat, 16, width_a // 2), BF16),
        pltpu.VMEM((2 * n_slab, n_ty, 16, SLAB), BF16), pltpu.VMEM((2 * n_slab, n_ty, 16, SLAB), BF16),
        pltpu.VMEM((8, HEAD), F32), pltpu.VMEM((n_flat, 8, HEAD), F32),
        pltpu.SemaphoreType.DMA((22,)),
        pltpu.SemaphoreType.DMA((7, n_ty)), pltpu.SemaphoreType.DMA((7, n_ty)),
        pltpu.SemaphoreType.DMA((2, n_tx)), pltpu.SemaphoreType.DMA((2, n_tx)),
        pltpu.SemaphoreType.DMA((2, n_flat)), pltpu.SemaphoreType.DMA((2, n_flat)),
        pltpu.SemaphoreType.DMA((2 * n_slab, n_ty)), pltpu.SemaphoreType.DMA((2 * n_slab, n_ty)),
        pltpu.SemaphoreType.DMA((n_flat,)), pltpu.SemaphoreType.DMA((n_flat,)),
    ]
    hbm = pl.BlockSpec(memory_space=pl.ANY)
    vmem = pl.BlockSpec(memory_space=pltpu.VMEM)
    macs = n_rows * (width_e * (cols_e + inner_e) + width_a * (cols_a + inner_a)) + 2 * n_rows * vocab * (width_e + width_a)
    read = sum(array.size * array.dtype.itemsize for array in args)
    return pl.pallas_call(
        functools.partial(kernel, axes, None),
        out_shape=(
            jax.ShapeDtypeStruct((2, hid_e.shape[1] // n_ty, vocab), F32),
            jax.ShapeDtypeStruct((2, hid_e.shape[1] // n_ty), F32),
        ),
        in_specs=[hbm] * len(args),
        out_specs=(vmem, vmem),
        scratch_shapes=scratch,
        compiler_params=pltpu.CompilerParams(
            collective_id=0, has_side_effects=True, vmem_limit_bytes=56 * 1024 * 1024
        ),
        cost_estimate=pl.CostEstimate(flops=2 * macs, bytes_accessed=read, transcendentals=0),
        name="contrast",
    )(*args)


def solution(mesh):
    model = (
        P(None, None, "ty"), P("ty"), P("ty", "tx"), P("ty", "tx"), P("ty", "tx"), P("tx", "ty"), P("ty"),
        P(("grp", "tx"), "ty"), P(("grp", "ty"), None, "tx"), P(("grp", "ty"), None, "tx"),
    )
    axes = tuple(mesh.shape[name] for name in ("grp", "tx", "ty"))
    return jax.shard_map(
        functools.partial(on_device, axes),
        mesh=mesh,
        in_specs=model + model + (P(("grp", "ty")), P(None, "ty")),
        out_specs=(P(None, "ty", ("grp", "tx")), P(None, "ty")),
        check_vma=False,
    )
```

```python
import functools
import math

import jax
import jax.numpy as jnp
from jax import lax
from jax.experimental import pallas as pl
from jax.experimental.pallas import tpu as pltpu
from jax.sharding import PartitionSpec as P

HEAD = 128
EPS = 1e-05
BASE = 10000.0
AMATEUR = 0.5
SCALE = HEAD**-0.5
CHUNK = 512
SLAB = 1024
F32 = jnp.float32
BF16 = jnp.bfloat16
MESH = pl.DeviceIdType.MESH


def iota(shape, axis):
    return lax.broadcasted_iota(jnp.int32, shape, axis)


def mm(a, b):
    return lax.dot_general(a, b, (((1,), (0,)), ((), ())), preferred_element_type=F32)


def mm_t(a, b):
    return lax.dot_general(a, b, (((1,), (1,)), ((), ())), preferred_element_type=F32)


def one_hot(size, source):
    out = iota((size, size), 0)
    return jnp.where(iota((size, size), 1) == source(out), 1.0, 0.0).astype(BF16)


def folded(values):
    half = values.shape[-1] // 2
    return jnp.concatenate([values[..., :half], values[..., half:]], axis=-2)


def unfolded(values):
    return jnp.concatenate([values[..., :8, :], values[..., 8:, :]], axis=-1)


def packed(values, ref):
    return values if ref.dtype == F32 else folded(values).astype(ref.dtype)


def lane_fold(values):
    total = values[:, :HEAD]
    for start in range(HEAD, values.shape[1], HEAD):
        total = total + values[:, start : start + HEAD]
    return total


def widen(column, width):
    return jnp.concatenate([column] * (width // HEAD), axis=1)


def kernel(axes, dims, *refs):
    n_grp, n_tx, n_ty = axes
    (
        hid_e, gain_e, wq_e, wk_e, wv_e, wo_e, fin_e, head_e, kc_e, vc_e,
        hid_a, gain_a, wq_a, wk_a, wv_a, wo_a, fin_a, head_a, kc_a, vc_a,
        h_lengths, h_tokens,
        out_ref, score_ref,
        lengths, tokens, v_gain_e, v_fin_e, v_gain_a, v_fin_a,
        v_hid_e, v_wq_e, v_wk_e, v_wv_e, v_wo_e, v_head_e, v_kc_e, v_vc_e,
        v_hid_a, v_wq_a, v_wk_a, v_wv_a, v_wo_a, v_head_a, v_kc_a, v_vc_a,
        x_e, x_a, sq_send, sq_recv,
        p_send_e, p_recv_e, p_send_a, p_recv_a,
        g_e, g_a,
        o_send_e, o_recv_e, o_send_a, o_recv_a,
        s_send_e, s_recv_e, s_send_a, s_recv_a,
        f_e, f_a,
        l_send, l_own, xa_recv, yb_send, yb_recv, kept, ya_recv, summed_y, xb_send, xb_recv, t_send, t_recv,
        local_sem, ty_send, ty_recv, tx_send, tx_recv, fw_send, fw_recv, l_ssem, l_rsem, t_ssem, t_rsem,
    ) = refs
    grp, tx, ty = lax.axis_index("grp"), lax.axis_index("tx"), lax.axis_index("ty")
    half_rows = v_hid_e.shape[1]
    width_e, width_a = v_hid_e.shape[2], v_hid_a.shape[2]
    heads_e, heads_a = v_wq_e.shape[1] // HEAD, v_wq_a.shape[1] // HEAD
    vocab = head_e.shape[0]

    first = pl.multiple_of(grp * half_rows, half_rows)
    pairs = [
        (hid_e.at[:, pl.ds(first, half_rows)], v_hid_e),
        (hid_a.at[:, pl.ds(first, half_rows)], v_hid_a),
        (h_lengths, lengths), (gain_e, v_gain_e), (gain_a, v_gain_a),
        (fin_e, v_fin_e), (fin_a, v_fin_a), (h_tokens, tokens),
        (wq_a, v_wq_a), (wk_a, v_wk_a), (wv_a, v_wv_a),
        (wq_e, v_wq_e), (wk_e, v_wk_e), (wv_e, v_wv_e),
        (kc_a, v_kc_a), (vc_a, v_vc_a), (kc_e, v_kc_e), (vc_e, v_vc_e),
        (wo_a, v_wo_a), (wo_e, v_wo_e),
        (head_a, v_head_a.at[pl.ds(0, vocab)]), (head_e, v_head_e.at[pl.ds(0, vocab)]),
    ]
    loads = [
        pltpu.make_async_copy(source, target, local_sem.at[number])
        for number, (source, target) in enumerate(pairs)
    ]
    for load in loads[:8]:
        load.start()
    (l_hid_e, l_hid_a, l_lengths, l_gain_e, l_gain_a, l_fin_e, l_fin_a, l_tokens, l_wq_a, l_wk_a, l_wv_a, l_wq_e, l_wk_e, l_wv_e,
     l_kc_a, l_vc_a, l_kc_e, l_vc_e, l_wo_a, l_wo_e, l_head_a, l_head_e) = loads

    def ty_peer(step):
        return lax.rem(ty // 4 + step // 4, n_ty // 4) * 4 + lax.rem(ty + step, 4)

    def tx_peer(step):
        return lax.rem(tx // 4 + step // 4, n_tx // 4) * 4 + lax.rem(tx + step, 4)

    flat = grp * n_tx + tx
    n_flat = n_grp * n_tx

    def flat_peer(step):
        return {"grp": lax.rem(grp + step // n_tx, n_grp), "tx": tx_peer(lax.rem(step, n_tx))}

    def to_ty(step):
        return {"ty": ty_peer(step)}

    def to_tx(step):
        return {"tx": tx_peer(step)}

    barrier = pltpu.get_barrier_semaphore()

    def greet(device):
        pl.semaphore_signal(barrier, inc=1, device_id=device, device_id_type=MESH)

    @pl.loop(1, n_ty)
    def _(step):
        greet(to_ty(n_ty - step))

    @pl.loop(1, n_flat)
    def _(step):
        greet(flat_peer(n_flat - step))

    for load in loads[8:14]:
        load.start()

    started = []

    class Exchange:
        def __init__(self, n, source, target, send_sems, recv_sems, device, begin=True):
            self.n = n
            self.make = lambda step: pltpu.make_async_remote_copy(
                src_ref=source(step), dst_ref=target(step), send_sem=send_sems.at[step], recv_sem=recv_sems.at[step],
                device_id=device(step), device_id_type=MESH,
            )
            started.append(self)
            if begin:
                self.begin()

        def begin(self):
            @pl.loop(1, self.n)
            def _(step):
                self.make(self.n - step).start()

        def arrive(self):
            @pl.loop(1, self.n)
            def _(step):
                self.make(step).wait_recv()

        def finish(self):
            @pl.loop(1, self.n)
            def _(step):
                self.make(step).wait_send()

    def add_up(exchange, first, recv):
        def body(step, total):
            exchange.make(step).wait_recv()
            return total + recv[step].astype(F32)

        return lax.fori_loop(1, exchange.n, body, first)

    n_rows = 2 * half_rows
    block = half_rows // n_ty
    order = one_hot(
        n_rows, lambda o: (o // block) % 2 * half_rows + o // (2 * block) * block + o % block
    )
    l_hid_e.wait()
    wide_e = mm(order, v_hid_e[...].reshape(n_rows, width_e))
    x_e[...] = wide_e.reshape(n_ty, 8, width_e)
    l_hid_a.wait()
    wide_a = mm(order, v_hid_a[...].reshape(n_rows, width_a))
    x_a[...] = wide_a.reshape(n_ty, 8, width_a)
    partial = jnp.concatenate([lane_fold(wide_e * wide_e), lane_fold(wide_a * wide_a)], axis=0)
    own = jnp.broadcast_to(jnp.sum(partial.T, axis=0, keepdims=True), (8, HEAD))
    sq_send[...] = own

    pl.semaphore_wait(barrier, n_ty - 1 + n_flat - 1)

    squares = Exchange(n_ty, lambda d: sq_send, lambda d: sq_recv.at[d], ty_send.at[0], ty_recv.at[0], to_ty)
    for load in loads[14:18]:
        load.start()

    row8, lane8 = iota((8, HEAD), 0), iota((8, HEAD), 1)
    position = jnp.zeros((8, HEAD), jnp.int32)
    l_lengths.wait()
    for i in range(block):
        position = jnp.where(row8 % block == i, lengths[i], position)
    position = (position + row8 // block).astype(F32)
    exponent = (lane8 % (HEAD // 2)).astype(F32) * (2.0 / HEAD)
    angle = position * jnp.exp(exponent * (-math.log(BASE)))
    cosine = jnp.cos(angle)
    sine = jnp.where(lane8 < HEAD // 2, -1.0, 1.0) * jnp.sin(angle)

    def rotated(values):
        turned = jnp.concatenate([values[:, HEAD // 2 :], values[:, : HEAD // 2]], axis=1)
        return values * cosine + turned * sine

    total = add_up(squares, own, sq_recv)
    square = jnp.broadcast_to(total[0:1], (HEAD, HEAD)).T
    root_e = lax.rsqrt(square[:n_rows] / (width_e * n_ty) + EPS)
    root_a = lax.rsqrt(square[n_rows:] / (width_a * n_ty) + EPS)

    def project(x, root, g_load, gain, weights, send, recv, kind):
        width = x.shape[2]
        g_load.wait()
        values = x[...].reshape(n_rows, width)
        normed = (values * widen(root, width) * gain[...].astype(F32).reshape(1, width)).astype(BF16)
        parts = []
        for load, weight in weights:
            load.wait()
            columns = weight.shape[1]
            for at in range(0, columns, CHUNK):
                parts.append(mm(normed, weight[:, at : at + min(CHUNK, columns - at)]))
        send[...] = packed(jnp.concatenate(parts, axis=1).reshape(n_ty, 8, -1), send)
        return Exchange(n_ty, lambda d: send.at[ty_peer(d)], lambda d: recv.at[d], ty_send.at[kind], ty_recv.at[kind], to_ty)

    sent_pa = project(x_a, root_a, l_gain_a, v_gain_a, ((l_wq_a, v_wq_a), (l_wk_a, v_wk_a), (l_wv_a, v_wv_a)), p_send_a, p_recv_a, 2)
    sent_pe = project(x_e, root_e, l_gain_e, v_gain_e, ((l_wq_e, v_wq_e), (l_wk_e, v_wk_e), (l_wv_e, v_wv_e)), p_send_e, p_recv_e, 1)

    for load in loads[18:]:
        load.start()

    def summed(exchange, send, recv, me):
        total = add_up(exchange, send[me].astype(F32), recv)
        return total if send.dtype == F32 else unfolded(total)

    def padded(rows, size):
        if rows.shape[0] == size:
            return rows
        return jnp.concatenate([rows, jnp.zeros((size - rows.shape[0], rows.shape[1]), F32)], axis=0)

    def attend(acc, heads, key_heads, k_load, keys, v_load, values):
        group = heads // key_heads
        n_query = heads * 8
        per_row = 2 * heads
        cache = keys.shape[1]
        wide = key_heads * HEAD
        query = jnp.concatenate([rotated(acc[:, h * HEAD : (h + 1) * HEAD]) for h in range(heads)], axis=0)
        at = heads * HEAD
        fresh_k = jnp.concatenate(
            [rotated(acc[:, at + h * HEAD : at + (h + 1) * HEAD]) for h in range(key_heads)], axis=0
        )
        at += wide
        fresh_v = jnp.concatenate(
            [acc[:, at + h * HEAD : at + (h + 1) * HEAD] for h in range(key_heads)], axis=0
        )
        fresh_k = padded(fresh_k, HEAD).astype(BF16)
        fresh_v = padded(fresh_v, HEAD).astype(BF16)
        forth = one_hot(n_query, lambda o: o % heads * 8 + o // heads % 2 * block + o // per_row)
        back = one_hot(n_query, lambda o: o % block * per_row + o // block % 2 * heads + o // 8)
        query = mm(forth, query.astype(BF16))
        owner = iota((n_query, HEAD), 0)
        lane = iota((n_query, HEAD), 1)
        fresh = mm_t(query.astype(BF16), fresh_k) * SCALE
        seen = (
            (lane < key_heads * 8)
            & (lane // 8 == owner % heads // group)
            & (lane % block == owner // per_row)
            & (lane // block % 2 <= owner // heads % 2)
        )
        fresh = jnp.where(seen, fresh, -jnp.inf)
        if key_heads > 1:
            spread = widen(query, wide)
            keep = iota((n_query, wide), 1) // HEAD == iota((n_query, wide), 0) % heads // group
            query = jnp.where(keep, spread, 0.0)
        k_load.wait()
        cached = []
        for i in range(block):
            part = query[i * per_row : (i + 1) * per_row].astype(BF16)
            score = mm_t(part, keys[i]) * SCALE
            cached.append(jnp.where(iota((per_row, cache), 1) < lengths[i], score, -jnp.inf))
        cached = jnp.concatenate(cached, axis=0)
        peak = jnp.maximum(jnp.max(cached, axis=1, keepdims=True), jnp.max(fresh, axis=1, keepdims=True))
        cached = jnp.exp(cached - peak)
        fresh = jnp.exp(fresh - peak)
        total = jnp.sum(cached, axis=1, keepdims=True) + jnp.sum(fresh, axis=1, keepdims=True)
        v_load.wait()
        mixture = jnp.concatenate(
            [mm(cached[i * per_row : (i + 1) * per_row].astype(BF16), values[i]) for i in range(block)], axis=0
        )
        if key_heads > 1:
            picked = jnp.zeros((n_query, HEAD), F32)
            for h in range(key_heads):
                picked = picked + jnp.where(owner % heads // group == h, mixture[:, h * HEAD : (h + 1) * HEAD], 0.0)
            mixture = picked
        mixture = mixture + mm(fresh.astype(BF16), fresh_v)
        ready = mm(back, (mixture / total).astype(BF16))
        return jnp.concatenate([ready[h * 8 : (h + 1) * 8] for h in range(heads)], axis=1)

    def gather(rows, buffer, kind):
        buffer[ty] = folded(rows).astype(BF16)
        return Exchange(n_ty, lambda d: buffer.at[ty], lambda d: buffer.at[ty], ty_send.at[kind], ty_recv.at[kind], to_ty)

    acc = summed(sent_pa, p_send_a, p_recv_a, ty)
    sent_ga = gather(attend(acc, heads_a, v_wk_a.shape[1] // HEAD, l_kc_a, v_kc_a, l_vc_a, v_vc_a), g_a, 4)
    acc = summed(sent_pe, p_send_e, p_recv_e, ty)
    sent_ge = gather(attend(acc, heads_e, v_wk_e.shape[1] // HEAD, l_kc_e, v_kc_e, l_vc_e, v_vc_e), g_e, 3)

    def output(exchange, buffer, load, weight, send, recv, kind):
        exchange.arrive()
        rows = unfolded(buffer[...].astype(F32)).reshape(n_rows, weight.shape[0]).astype(BF16)
        load.wait()
        columns = weight.shape[1]
        parts = [mm(rows, weight[:, at : at + CHUNK]) for at in range(0, columns, CHUNK)]
        send[...] = packed(jnp.concatenate(parts, axis=1).reshape(n_tx, 8, columns), send)
        return Exchange(n_tx, lambda d: send.at[tx_peer(d)], lambda d: recv.at[d], tx_send.at[kind], tx_recv.at[kind], to_tx)

    sent_oa = output(sent_ga, g_a, l_wo_a, v_wo_a, o_send_a, o_recv_a, 1)
    sent_oe = output(sent_ge, g_e, l_wo_e, v_wo_e, o_send_e, o_recv_e, 0)

    def residual(exchange, x, send, recv, s_send, s_recv, kind):
        values = x[tx] + summed(exchange, send, recv, tx)
        part = lane_fold(values * values)
        s_send[...] = part
        return values, part, Exchange(
            n_ty, lambda d: s_send, lambda d: s_recv.at[d], ty_send.at[kind], ty_recv.at[kind], to_ty
        )

    def final(values, part, exchange, s_recv, g_load, gain, buffer, kind):
        width = values.shape[1]
        g_load.wait()
        part = add_up(exchange, part, s_recv)
        mean = jnp.sum(part, axis=1, keepdims=True) / (width * n_ty)
        rows = values * lax.rsqrt(mean + EPS) * gain[...].astype(F32).reshape(1, width)
        buffer[flat] = folded(rows).astype(BF16)
        across = Exchange(
            n_tx, lambda d: buffer.at[flat], lambda d: buffer.at[flat], tx_send.at[kind], tx_recv.at[kind], to_tx
        )

        def from_tx(step):
            return grp * n_tx + lax.rem(tx // 4 + n_tx // 4 - step // 4, n_tx // 4) * 4 + lax.rem(tx + 4 - lax.rem(step, 4), 4)

        forward = Exchange(
            n_tx, lambda d: buffer.at[from_tx(d)], lambda d: buffer.at[from_tx(d)], fw_send.at[kind - 2],
            fw_recv.at[kind - 2], lambda d: {"grp": 1 - grp}, begin=False,
        )
        forward.make(0).start()
        return across, forward

    def pass_on(pair):
        across, forward = pair

        @pl.loop(1, n_tx)
        def _(step):
            across.make(step).wait_recv()
            forward.make(step).start()

    def passed_on(pair):
        pair[1].make(0).wait_recv()
        pair[1].arrive()

    res_a, part_a, sent_sa = residual(sent_oa, x_a, o_send_a, o_recv_a, s_send_a, s_recv_a, 6)
    pair_a = final(res_a, part_a, sent_sa, s_recv_a, l_fin_a, v_fin_a, f_a, 3)
    res_e, part_e, sent_se = residual(sent_oe, x_e, o_send_e, o_recv_e, s_send_e, s_recv_e, 5)

    padding = v_head_e.shape[0] - vocab
    l_head_a.wait()
    v_head_a[pl.ds(vocab, padding), :] = jnp.zeros((padding, width_a), BF16)
    l_head_e.wait()
    v_head_e[pl.ds(vocab, padding), :] = jnp.zeros((padding, width_e), BF16)

    n_slab = v_head_e.shape[0] // SLAB

    ring, coarse = lax.rem(ty, 4), ty // 4
    halves = (grp, 1 - grp)

    def along(step):
        return lax.rem(ring + step, 4)

    def remote(kind, number, source, target, device):
        return pltpu.make_async_remote_copy(
            src_ref=source, dst_ref=target, send_sem=l_ssem.at[kind, number], recv_sem=l_rsem.at[kind, number],
            device_id={"ty": device}, device_id_type=MESH,
        )

    def place(m, half, slab):
        return (m * 2 + half) * n_slab + slab

    def over_x_first(m, step):
        return remote(
            0, m * 4 + step, l_send.at[place(m, 1 - coarse, 0), along(step)], xa_recv.at[m, step], (1 - coarse) * 4 + ring
        )

    def over_y_second(m, step):
        return remote(1, m * 4 + step, yb_send.at[m, step], yb_recv.at[m, step], coarse * 4 + along(step))

    def over_y_first(m, part, step):
        source = l_send.at[place(m, halves[part], 1), along(step)]
        return remote(2, (m * 2 + part) * 4 + step, source, ya_recv.at[m * 2 + part, step], coarse * 4 + along(step))

    def over_x_second(m):
        return remote(3, m, xb_send.at[m, 1 - coarse], xb_recv.at[m], (1 - coarse) * 4 + ring)

    farthest_first = (2, 1, 3, 0)

    def logits(m, part, rows, head):
        half = halves[part]
        for slab in range(n_slab):
            at_place = place(m, half, slab)
            for at in range(0, SLAB, CHUNK):
                piece = mm_t(rows, head[slab * SLAB + at : slab * SLAB + at + CHUNK, :]).reshape(4, 16, CHUNK)
                l_own[at_place, :, :, at : at + CHUNK] = piece
                l_send[at_place, :, :, at : at + CHUNK] = piece.astype(BF16)
            if slab == 0:

                @pl.when(half != coarse)
                def _():
                    for step in farthest_first:
                        over_x_first(m, step).start()
            else:
                for step in farthest_first[:3]:
                    over_y_first(m, part, step).start()

    def combine(m):
        for step in farthest_first:
            over_x_first(m, step).wait_recv()
            total = l_own[place(m, coarse, 0), along(step)] + xa_recv[m, step].astype(F32)
            if step == 0:
                kept[m] = total
            else:
                yb_send[m, step] = total.astype(BF16)
                over_y_second(m, step).start()

    def settle(m, part):
        half = halves[part]
        total = l_own[place(m, half, 1), ring]
        for step in (1, 3, 2):
            over_y_first(m, part, step).wait_recv()
            total = total + ya_recv[m * 2 + part, step].astype(F32)
        summed_y[m, half] = total
        xb_send[m, half] = total.astype(BF16)

        @pl.when(half != coarse)
        def _():
            over_x_second(m).start()

    def half_of(buffer, half, width):
        return unfolded(buffer[pl.ds(half * n_tx, n_tx)].astype(F32)).reshape(n_rows, width).astype(BF16)

    pass_on(pair_a)
    logits(1, 0, half_of(f_a, halves[0], width_a), v_head_a)
    pair_e = final(res_e, part_e, sent_se, s_recv_e, l_fin_e, v_fin_e, f_e, 2)
    passed_on(pair_a)
    logits(1, 1, half_of(f_a, halves[1], width_a), v_head_a)
    settle(1, 0)
    pass_on(pair_e)
    combine(1)
    settle(1, 1)
    logits(0, 0, half_of(f_e, halves[0], width_e), v_head_e)
    passed_on(pair_e)
    logits(0, 1, half_of(f_e, halves[1], width_e), v_head_e)
    settle(0, 0)
    combine(0)
    settle(0, 1)

    def slab_sums(m):
        first = kept[m]
        for step in (1, 3, 2):
            over_y_second(m, step).wait_recv()
            first = first + yb_recv[m, step].astype(F32)
        over_x_second(m).wait_recv()
        return [first, summed_y[m, coarse] + xb_recv[m].astype(F32)]

    lane_c = iota((16, SLAB), 1)

    def peak_and_total(parts):
        masked = [jnp.where(lane_c + c * SLAB < vocab, part, -jnp.inf) for c, part in enumerate(parts)]
        peak = masked[0]
        for part in masked[1:]:
            peak = jnp.maximum(peak, part)
        peak = jnp.max(peak, axis=1, keepdims=True)
        total = jnp.exp(masked[0] - peak)
        for part in masked[1:]:
            total = total + jnp.exp(part - peak)
        return peak, jnp.sum(total, axis=1, keepdims=True)

    l_tokens.wait()
    row16 = iota((16, HEAD), 0)
    token = jnp.zeros((16, HEAD), jnp.int32)
    for s in range(2):
        for r in range(8):
            token = jnp.where(row16 == r // block * 8 + s * block + r % block, tokens[s, r], token)
    token = widen(token - flat * vocab, SLAB)

    amateur = slab_sums(1)
    peak_a, total_a = peak_and_total(amateur)
    expert = slab_sums(0)
    peak_e, total_e = peak_and_total(expert)
    chosen = jnp.zeros((16, SLAB), F32)
    mixed = []
    for c in range(n_slab):
        mixed.append(expert[c] - AMATEUR * amateur[c])
        column = lane_c + c * SLAB
        chosen = chosen + jnp.where((column == token) & (column < vocab), mixed[c], 0.0)
    chosen = jnp.sum(chosen, axis=1, keepdims=True)

    lane16 = iota((16, HEAD), 1) % 64
    tile = jnp.where(lane16 == 0, peak_e, jnp.where(lane16 == 1, total_e, 0.0))
    tile = jnp.where(lane16 == 2, peak_a, jnp.where(lane16 == 3, total_a, tile))
    tile = jnp.where(lane16 == 4, chosen, tile)
    tile = jnp.where(lane8 < 64, tile[:8], tile[8:])
    t_send[...] = tile
    Exchange(n_flat, lambda d: t_send, lambda d: t_recv.at[d], t_ssem, t_rsem, flat_peer).arrive()
    tiles = [tile] + [t_recv[step] for step in range(1, n_flat)]
    highest = functools.reduce(jnp.maximum, tiles)
    picked = functools.reduce(jnp.add, tiles)

    def shifted(values):
        return jnp.concatenate([values[:, 1:], values[:, :1]], axis=1)

    summed_up = functools.reduce(jnp.add, [jnp.exp(t - highest) * shifted(t) for t in tiles])
    log_total = highest + jnp.log(summed_up)

    def column(values, lane):
        return jnp.concatenate([values[:, lane : lane + 1], values[:, lane + 64 : lane + 65]], axis=0)

    offset = column(log_total, 0) - AMATEUR * column(log_total, 2)
    for c in range(n_slab):
        size = min(SLAB, vocab - c * SLAB)
        contrast = mixed[c] - offset
        for s in range(2):
            low = s * block
            out_ref[s, :, c * SLAB : c * SLAB + size] = jnp.concatenate(
                [contrast[low : low + block], contrast[8 + low : 8 + low + block]], axis=0
            )[:, :size]
    value = jnp.broadcast_to(column(picked, 4) - offset, (16, HEAD))
    lane_r = iota((16, HEAD), 1)
    for s in range(2):
        mine = row16 == lane_r // block * 8 + s * block + lane_r % block
        line = jnp.sum(jnp.where(mine & (lane_r < 8), value, 0.0), axis=0, keepdims=True)
        score_ref[s : s + 1, :] = line[:, :8]

    for exchange in started:
        exchange.finish()
    pair_e[1].make(0).wait_send()
    pair_a[1].make(0).wait_send()

    for m in range(2):
        for step in range(4):
            over_x_first(m, step).wait_send()
        for step in range(1, 4):
            over_y_second(m, step).wait_send()
            over_y_first(m, 0, step).wait_send()
            over_y_first(m, 1, step).wait_send()
        over_x_second(m).wait_send()


def on_device(axes, *args):
    (
        hid_e, gain_e, wq_e, wk_e, wv_e, wo_e, fin_e, head_e, kc_e, vc_e,
        hid_a, gain_a, wq_a, wk_a, wv_a, wo_a, fin_a, head_a, kc_a, vc_a,
        lengths, tokens,
    ) = args
    n_grp, n_tx, n_ty = axes
    n_flat = n_grp * n_tx
    half = hid_e.shape[1] // n_grp
    vocab = head_e.shape[0]
    padded = -(-vocab // SLAB) * SLAB
    n_slab = padded // SLAB
    n_rows = 2 * half
    width_e, width_a = hid_e.shape[2], hid_a.shape[2]
    cols_e = wq_e.shape[1] + wk_e.shape[1] + wv_e.shape[1]
    cols_a = wq_a.shape[1] + wk_a.shape[1] + wv_a.shape[1]
    inner_e, inner_a = wo_e.shape[0], wo_a.shape[0]

    def like(array):
        return pltpu.VMEM(array.shape, array.dtype)

    scratch = [
        pltpu.SMEM(lengths.shape, jnp.int32), pltpu.SMEM(tokens.shape, jnp.int32),
        like(gain_e), like(fin_e), like(gain_a), like(fin_a),
    ]
    for hid, wq, wk, wv, wo, head, kc, vc in (
        (hid_e, wq_e, wk_e, wv_e, wo_e, head_e, kc_e, vc_e),
        (hid_a, wq_a, wk_a, wv_a, wo_a, head_a, kc_a, vc_a),
    ):
        scratch += [
            pltpu.VMEM((2, half, hid.shape[2]), BF16), like(wq), like(wk), like(wv), like(wo),
            pltpu.VMEM((padded, head.shape[1]), BF16), like(kc), like(vc),
        ]
    scratch += [
        pltpu.VMEM((n_ty, 8, width_e), F32), pltpu.VMEM((n_ty, 8, width_a), F32),
        pltpu.VMEM((8, HEAD), F32), pltpu.VMEM((n_ty, 8, HEAD), F32),
        pltpu.VMEM((n_ty, 8, cols_e), F32), pltpu.VMEM((n_ty, 8, cols_e), F32),
        pltpu.VMEM((n_ty, 16, cols_a // 2), BF16), pltpu.VMEM((n_ty, 16, cols_a // 2), BF16),
        pltpu.VMEM((n_ty, 16, inner_e // 2), BF16), pltpu.VMEM((n_ty, 16, inner_a // 2), BF16),
        pltpu.VMEM((n_tx, 16, width_e // 2), BF16), pltpu.VMEM((n_tx, 16, width_e // 2), BF16),
        pltpu.VMEM((n_tx, 16, width_a // 2), BF16), pltpu.VMEM((n_tx, 16, width_a // 2), BF16),
        pltpu.VMEM((8, HEAD), F32), pltpu.VMEM((n_ty, 8, HEAD), F32),
        pltpu.VMEM((8, HEAD), F32), pltpu.VMEM((n_ty, 8, HEAD), F32),
        pltpu.VMEM((n_flat, 16, width_e // 2), BF16), pltpu.VMEM((n_flat, 16, width_a // 2), BF16),
        pltpu.VMEM((4 * n_slab, 4, 16, SLAB), BF16), pltpu.VMEM((4 * n_slab, 4, 16, SLAB), F32),
        pltpu.VMEM((2, 4, 16, SLAB), BF16), pltpu.VMEM((2, 4, 16, SLAB), BF16), pltpu.VMEM((2, 4, 16, SLAB), BF16),
        pltpu.VMEM((2, 16, SLAB), F32), pltpu.VMEM((4, 4, 16, SLAB), BF16),
        pltpu.VMEM((2, 2, 16, SLAB), F32), pltpu.VMEM((2, 2, 16, SLAB), BF16), pltpu.VMEM((2, 16, SLAB), BF16),
        pltpu.VMEM((8, HEAD), F32), pltpu.VMEM((n_flat, 8, HEAD), F32),
        pltpu.SemaphoreType.DMA((22,)),
        pltpu.SemaphoreType.DMA((7, n_ty)), pltpu.SemaphoreType.DMA((7, n_ty)),
        pltpu.SemaphoreType.DMA((4, n_tx)), pltpu.SemaphoreType.DMA((4, n_tx)),
        pltpu.SemaphoreType.DMA((2, n_tx)), pltpu.SemaphoreType.DMA((2, n_tx)),
        pltpu.SemaphoreType.DMA((4, 16)), pltpu.SemaphoreType.DMA((4, 16)),
        pltpu.SemaphoreType.DMA((n_flat,)), pltpu.SemaphoreType.DMA((n_flat,)),
    ]
    hbm = pl.BlockSpec(memory_space=pl.ANY)
    vmem = pl.BlockSpec(memory_space=pltpu.VMEM)
    macs = n_rows * (width_e * (cols_e + inner_e) + width_a * (cols_a + inner_a)) + 2 * n_rows * vocab * (width_e + width_a)
    read = sum(array.size * array.dtype.itemsize for array in args)
    return pl.pallas_call(
        functools.partial(kernel, axes, None),
        out_shape=(
            jax.ShapeDtypeStruct((2, hid_e.shape[1] // n_ty, vocab), F32),
            jax.ShapeDtypeStruct((2, hid_e.shape[1] // n_ty), F32),
        ),
        in_specs=[hbm] * len(args),
        out_specs=(vmem, vmem),
        scratch_shapes=scratch,
        compiler_params=pltpu.CompilerParams(
            collective_id=0, has_side_effects=True, vmem_limit_bytes=56 * 1024 * 1024
        ),
        cost_estimate=pl.CostEstimate(flops=2 * macs, bytes_accessed=read, transcendentals=0),
        name="contrast",
    )(*args)


def solution(mesh):
    model = (
        P(None, None, "ty"), P("ty"), P("ty", "tx"), P("ty", "tx"), P("ty", "tx"), P("tx", "ty"), P("ty"),
        P(("grp", "tx"), "ty"), P(("grp", "ty"), None, "tx"), P(("grp", "ty"), None, "tx"),
    )
    axes = tuple(mesh.shape[name] for name in ("grp", "tx", "ty"))
    return jax.shard_map(
        functools.partial(on_device, axes),
        mesh=mesh,
        in_specs=model + model + (P(("grp", "ty")), P(None, "ty")),
        out_specs=(P(None, "ty", ("grp", "tx")), P(None, "ty")),
        check_vma=False,
    )
```

```python
import functools
import math

import jax
import jax.numpy as jnp
from jax import lax
from jax.experimental import pallas as pl
from jax.experimental.pallas import tpu as pltpu
from jax.sharding import PartitionSpec as P

HEAD = 128
EPS = 1e-05
BASE = 10000.0
AMATEUR = 0.5
SCALE = HEAD**-0.5
CHUNK = 512
SLAB = 1024
F32 = jnp.float32
BF16 = jnp.bfloat16
MESH = pl.DeviceIdType.MESH


def iota(shape, axis):
    return lax.broadcasted_iota(jnp.int32, shape, axis)


def mm(a, b):
    return lax.dot_general(a, b, (((1,), (0,)), ((), ())), preferred_element_type=F32)


def mm_t(a, b):
    return lax.dot_general(a, b, (((1,), (1,)), ((), ())), preferred_element_type=F32)


def one_hot(size, source):
    out = iota((size, size), 0)
    return jnp.where(iota((size, size), 1) == source(out), 1.0, 0.0).astype(BF16)


def folded(values):
    half = values.shape[-1] // 2
    return jnp.concatenate([values[..., :half], values[..., half:]], axis=-2)


def unfolded(values):
    return jnp.concatenate([values[..., :8, :], values[..., 8:, :]], axis=-1)


def packed(values, ref):
    return values if ref.dtype == F32 else folded(values).astype(ref.dtype)


def lane_fold(values):
    total = values[:, :HEAD]
    for start in range(HEAD, values.shape[1], HEAD):
        total = total + values[:, start : start + HEAD]
    return total


def widen(column, width):
    return jnp.concatenate([column] * (width // HEAD), axis=1)


def kernel(axes, dims, *refs):
    n_grp, n_tx, n_ty = axes
    (
        hid_e, gain_e, wq_e, wk_e, wv_e, wo_e, fin_e, head_e, kc_e, vc_e,
        hid_a, gain_a, wq_a, wk_a, wv_a, wo_a, fin_a, head_a, kc_a, vc_a,
        h_lengths, h_tokens,
        out_ref, score_ref,
        lengths, tokens, v_gain_e, v_fin_e, v_gain_a, v_fin_a,
        v_hid_e, v_wq_e, v_wk_e, v_wv_e, v_wo_e, v_head_e, v_kc_e, v_vc_e,
        v_hid_a, v_wq_a, v_wk_a, v_wv_a, v_wo_a, v_head_a, v_kc_a, v_vc_a,
        x_e, x_a, sq_send, sq_recv,
        p_send_e, p_recv_e, p_send_a, p_recv_a,
        g_e, g_a,
        o_send_e, o_recv_e, o_send_a, o_recv_a,
        s_send_e, s_recv_e, s_send_a, s_recv_a,
        f_e, f_a,
        l_send, l_recv, t_send, t_recv,
        local_sem, ty_send, ty_recv, tx_send, tx_recv, fw_send, fw_recv, l_ssem, l_rsem, t_ssem, t_rsem,
    ) = refs
    grp, tx, ty = lax.axis_index("grp"), lax.axis_index("tx"), lax.axis_index("ty")
    half_rows = v_hid_e.shape[1]
    width_e, width_a = v_hid_e.shape[2], v_hid_a.shape[2]
    heads_e, heads_a = v_wq_e.shape[1] // HEAD, v_wq_a.shape[1] // HEAD
    vocab = head_e.shape[0]

    first = pl.multiple_of(grp * half_rows, half_rows)
    pairs = [
        (hid_e.at[:, pl.ds(first, half_rows)], v_hid_e),
        (hid_a.at[:, pl.ds(first, half_rows)], v_hid_a),
        (h_lengths, lengths), (gain_e, v_gain_e), (gain_a, v_gain_a),
        (fin_e, v_fin_e), (fin_a, v_fin_a), (h_tokens, tokens),
        (wq_a, v_wq_a), (wk_a, v_wk_a), (wv_a, v_wv_a),
        (wq_e, v_wq_e), (wk_e, v_wk_e), (wv_e, v_wv_e),
        (kc_a, v_kc_a), (vc_a, v_vc_a), (kc_e, v_kc_e), (vc_e, v_vc_e),
        (wo_a, v_wo_a), (wo_e, v_wo_e),
        (head_a, v_head_a.at[pl.ds(0, vocab)]), (head_e, v_head_e.at[pl.ds(0, vocab)]),
    ]
    loads = [
        pltpu.make_async_copy(source, target, local_sem.at[number])
        for number, (source, target) in enumerate(pairs)
    ]
    for load in loads[:8]:
        load.start()
    (l_hid_e, l_hid_a, l_lengths, l_gain_e, l_gain_a, l_fin_e, l_fin_a, l_tokens, l_wq_a, l_wk_a, l_wv_a, l_wq_e, l_wk_e, l_wv_e,
     l_kc_a, l_vc_a, l_kc_e, l_vc_e, l_wo_a, l_wo_e, l_head_a, l_head_e) = loads

    def ty_peer(step):
        return lax.rem(ty // 4 + step // 4, n_ty // 4) * 4 + lax.rem(ty + step, 4)

    def tx_peer(step):
        return lax.rem(tx // 4 + step // 4, n_tx // 4) * 4 + lax.rem(tx + step, 4)

    flat = grp * n_tx + tx
    n_flat = n_grp * n_tx

    def flat_peer(step):
        return {"grp": lax.rem(grp + step // n_tx, n_grp), "tx": tx_peer(lax.rem(step, n_tx))}

    def to_ty(step):
        return {"ty": ty_peer(step)}

    def to_tx(step):
        return {"tx": tx_peer(step)}

    def near(step):
        return {"tx": lax.rem(tx // 4 + step // 4, n_tx // 4) * 4 + lax.rem(tx, 4), "ty": ty_peer(step)}

    barrier = pltpu.get_barrier_semaphore()

    def greet(device):
        pl.semaphore_signal(barrier, inc=1, device_id=device, device_id_type=MESH)

    @pl.loop(1, n_ty)
    def _(step):
        greet(to_ty(n_ty - step))

    @pl.loop(4, n_ty)
    def _(step):
        greet(near(step))

    @pl.loop(1, n_flat)
    def _(step):
        greet(flat_peer(n_flat - step))

    for load in loads[8:14]:
        load.start()

    started = []

    class Exchange:
        def __init__(self, n, source, target, send_sem, recv_sem, device, bulk, begin=True, each=False, low=1):
            self.n, self.low = n, low
            self.make = lambda step: pltpu.make_async_remote_copy(
                src_ref=source(step), dst_ref=target(step), send_sem=send_sem,
                recv_sem=recv_sem.at[step] if each else recv_sem, device_id=device(step), device_id_type=MESH,
            )
            self.all = lambda: pltpu.make_async_remote_copy(
                src_ref=bulk, dst_ref=bulk, send_sem=send_sem, recv_sem=recv_sem.at[0] if each else recv_sem,
                device_id=device(low), device_id_type=MESH,
            )
            started.append(self)
            if begin:
                self.begin()

        def begin(self):
            @pl.loop(1, self.n)
            def _(step):
                self.make(self.n - step).start()

        def arrive(self):
            self.all().wait_recv()

        def finish(self):
            self.all().wait_send()

    def drain(keep):
        while len(started) > keep:
            started.pop(0).finish()

    def add_up(exchange, total, recv):
        exchange.arrive()
        for step in range(1, exchange.n):
            total = total + recv[step].astype(F32)
        return total

    n_rows = 2 * half_rows
    block = half_rows // n_ty
    order = one_hot(
        n_rows, lambda o: (o // block) % 2 * half_rows + o // (2 * block) * block + o % block
    )
    l_hid_e.wait()
    wide_e = mm(order, v_hid_e[...].reshape(n_rows, width_e))
    x_e[...] = wide_e.reshape(n_ty, 8, width_e)
    l_hid_a.wait()
    wide_a = mm(order, v_hid_a[...].reshape(n_rows, width_a))
    x_a[...] = wide_a.reshape(n_ty, 8, width_a)
    partial = jnp.concatenate([lane_fold(wide_e * wide_e), lane_fold(wide_a * wide_a)], axis=0)
    own = jnp.broadcast_to(jnp.sum(partial.T, axis=0, keepdims=True), (8, HEAD))
    sq_send[...] = own

    pl.semaphore_wait(barrier, n_ty - 1 + n_ty - 4 + n_flat - 1)

    squares = Exchange(n_ty, lambda d: sq_send, lambda d: sq_recv.at[d], ty_send.at[0], ty_recv.at[0], near,
                       sq_recv.at[pl.ds(1, n_ty - 1)])
    for load in loads[14:18]:
        load.start()

    row8, lane8 = iota((8, HEAD), 0), iota((8, HEAD), 1)
    position = jnp.zeros((8, HEAD), jnp.int32)
    l_lengths.wait()
    for i in range(block):
        position = jnp.where(row8 % block == i, lengths[i], position)
    position = (position + row8 // block).astype(F32)
    exponent = (lane8 % (HEAD // 2)).astype(F32) * (2.0 / HEAD)
    angle = position * jnp.exp(exponent * (-math.log(BASE)))
    cosine = jnp.cos(angle)
    sine = jnp.where(lane8 < HEAD // 2, -1.0, 1.0) * jnp.sin(angle)

    def rotated(values):
        turned = jnp.concatenate([values[:, HEAD // 2 :], values[:, : HEAD // 2]], axis=1)
        return values * cosine + turned * sine

    total = add_up(squares, own, sq_recv)
    square = jnp.broadcast_to(total[0:1], (HEAD, HEAD)).T
    root_e = lax.rsqrt(square[:n_rows] / (width_e * n_ty) + EPS)
    root_a = lax.rsqrt(square[n_rows:] / (width_a * n_ty) + EPS)

    def project(x, root, g_load, gain, weights, send, recv, kind):
        width = x.shape[2]
        g_load.wait()
        values = x[...].reshape(n_rows, width)
        normed = (values * widen(root, width) * gain[...].astype(F32).reshape(1, width)).astype(BF16)
        parts = []
        for load, weight in weights:
            load.wait()
            columns = weight.shape[1]
            for at in range(0, columns, CHUNK):
                parts.append(mm(normed, weight[:, at : at + min(CHUNK, columns - at)]))
        send[...] = packed(jnp.concatenate(parts, axis=1).reshape(n_ty, 8, -1), send)
        return Exchange(n_ty, lambda d: send.at[ty_peer(d)], lambda d: recv.at[d], ty_send.at[kind], ty_recv.at[kind], to_ty,
                        recv.at[pl.ds(1, n_ty - 1)])

    sent_pa = project(x_a, root_a, l_gain_a, v_gain_a, ((l_wq_a, v_wq_a), (l_wk_a, v_wk_a), (l_wv_a, v_wv_a)), p_send_a, p_recv_a, 2)
    sent_pe = project(x_e, root_e, l_gain_e, v_gain_e, ((l_wq_e, v_wq_e), (l_wk_e, v_wk_e), (l_wv_e, v_wv_e)), p_send_e, p_recv_e, 1)

    for load in loads[18:]:
        load.start()

    def summed(exchange, send, recv, me):
        total = add_up(exchange, send[me].astype(F32), recv)
        return total if send.dtype == F32 else unfolded(total)

    def padded(rows, size):
        if rows.shape[0] == size:
            return rows
        return jnp.concatenate([rows, jnp.zeros((size - rows.shape[0], rows.shape[1]), F32)], axis=0)

    def attend(acc, heads, key_heads, k_load, keys, v_load, values):
        group = heads // key_heads
        n_query = heads * 8
        per_row = 2 * heads
        cache = keys.shape[1]
        wide = key_heads * HEAD
        query = jnp.concatenate([rotated(acc[:, h * HEAD : (h + 1) * HEAD]) for h in range(heads)], axis=0)
        at = heads * HEAD
        fresh_k = jnp.concatenate(
            [rotated(acc[:, at + h * HEAD : at + (h + 1) * HEAD]) for h in range(key_heads)], axis=0
        )
        at += wide
        fresh_v = jnp.concatenate(
            [acc[:, at + h * HEAD : at + (h + 1) * HEAD] for h in range(key_heads)], axis=0
        )
        fresh_k = padded(fresh_k, HEAD).astype(BF16)
        fresh_v = padded(fresh_v, HEAD).astype(BF16)
        forth = one_hot(n_query, lambda o: o % heads * 8 + o // heads % 2 * block + o // per_row)
        back = one_hot(n_query, lambda o: o % block * per_row + o // block % 2 * heads + o // 8)
        query = mm(forth, query.astype(BF16))
        owner = iota((n_query, HEAD), 0)
        lane = iota((n_query, HEAD), 1)
        fresh = mm_t(query.astype(BF16), fresh_k) * SCALE
        seen = (
            (lane < key_heads * 8)
            & (lane // 8 == owner % heads // group)
            & (lane % block == owner // per_row)
            & (lane // block % 2 <= owner // heads % 2)
        )
        fresh = jnp.where(seen, fresh, -jnp.inf)
        if key_heads > 1:
            spread = widen(query, wide)
            keep = iota((n_query, wide), 1) // HEAD == iota((n_query, wide), 0) % heads // group
            query = jnp.where(keep, spread, 0.0)
        k_load.wait()
        cached = []
        for i in range(block):
            part = query[i * per_row : (i + 1) * per_row].astype(BF16)
            score = mm_t(part, keys[i]) * SCALE
            cached.append(jnp.where(iota((per_row, cache), 1) < lengths[i], score, -jnp.inf))
        cached = jnp.concatenate(cached, axis=0)
        peak = jnp.maximum(jnp.max(cached, axis=1, keepdims=True), jnp.max(fresh, axis=1, keepdims=True))
        cached = jnp.exp(cached - peak)
        fresh = jnp.exp(fresh - peak)
        total = jnp.sum(cached, axis=1, keepdims=True) + jnp.sum(fresh, axis=1, keepdims=True)
        v_load.wait()
        mixture = jnp.concatenate(
            [mm(cached[i * per_row : (i + 1) * per_row].astype(BF16), values[i]) for i in range(block)], axis=0
        )
        if key_heads > 1:
            picked = jnp.zeros((n_query, HEAD), F32)
            for h in range(key_heads):
                picked = picked + jnp.where(owner % heads // group == h, mixture[:, h * HEAD : (h + 1) * HEAD], 0.0)
            mixture = picked
        mixture = mixture + mm(fresh.astype(BF16), fresh_v)
        ready = mm(back, (mixture / total).astype(BF16))
        return jnp.concatenate([ready[h * 8 : (h + 1) * 8] for h in range(heads)], axis=1)

    def gather(rows, buffer, kind):
        buffer[ty] = folded(rows).astype(BF16)
        return Exchange(n_ty, lambda d: buffer.at[ty], lambda d: buffer.at[ty], ty_send.at[kind], ty_recv.at[kind], to_ty,
                        buffer.at[pl.ds(0, n_ty - 1)])

    acc = summed(sent_pa, p_send_a, p_recv_a, ty)
    sent_ga = gather(attend(acc, heads_a, v_wk_a.shape[1] // HEAD, l_kc_a, v_kc_a, l_vc_a, v_vc_a), g_a, 4)
    acc = summed(sent_pe, p_send_e, p_recv_e, ty)
    sent_ge = gather(attend(acc, heads_e, v_wk_e.shape[1] // HEAD, l_kc_e, v_kc_e, l_vc_e, v_vc_e), g_e, 3)
    drain(2)

    def output(exchange, buffer, load, weight, send, recv, kind):
        exchange.arrive()
        rows = unfolded(buffer[...].astype(F32)).reshape(n_rows, weight.shape[0]).astype(BF16)
        load.wait()
        columns = weight.shape[1]
        parts = [mm(rows, weight[:, at : at + CHUNK]) for at in range(0, columns, CHUNK)]
        send[...] = packed(jnp.concatenate(parts, axis=1).reshape(n_tx, 8, columns), send)
        return Exchange(n_tx, lambda d: send.at[tx_peer(d)], lambda d: recv.at[d], tx_send.at[kind], tx_recv.at[kind, 0], to_tx,
                        recv.at[pl.ds(1, n_tx - 1)])

    sent_oa = output(sent_ga, g_a, l_wo_a, v_wo_a, o_send_a, o_recv_a, 1)
    sent_oe = output(sent_ge, g_e, l_wo_e, v_wo_e, o_send_e, o_recv_e, 0)
    drain(2)

    def residual(exchange, x, send, recv, s_send, s_recv, kind):
        values = x[tx] + summed(exchange, send, recv, tx)
        part = lane_fold(values * values)
        s_send[...] = part
        return values, part, Exchange(
            n_ty, lambda d: s_send, lambda d: s_recv.at[d], ty_send.at[kind], ty_recv.at[kind], to_ty,
            s_recv.at[pl.ds(1, n_ty - 1)],
        )

    res_a, part_a, sent_sa = residual(sent_oa, x_a, o_send_a, o_recv_a, s_send_a, s_recv_a, 6)
    res_e, part_e, sent_se = residual(sent_oe, x_e, o_send_e, o_recv_e, s_send_e, s_recv_e, 5)
    drain(2)

    def final(values, part, exchange, s_recv, g_load, gain, buffer, kind):
        width = values.shape[1]
        g_load.wait()
        part = add_up(exchange, part, s_recv)
        mean = jnp.sum(part, axis=1, keepdims=True) / (width * n_ty)
        rows = values * lax.rsqrt(mean + EPS) * gain[...].astype(F32).reshape(1, width)
        buffer[flat] = folded(rows).astype(BF16)
        across = Exchange(
            n_tx, lambda d: buffer.at[flat], lambda d: buffer.at[flat], tx_send.at[kind], tx_recv.at[kind], to_tx,
            buffer.at[pl.ds(0, n_tx - 1)], each=True,
        )

        def from_tx(step):
            return grp * n_tx + lax.rem(tx // 4 + n_tx // 4 - step // 4, n_tx // 4) * 4 + lax.rem(tx + 4 - lax.rem(step, 4), 4)

        forward = Exchange(
            n_tx, lambda d: buffer.at[from_tx(d)], lambda d: buffer.at[from_tx(d)], fw_send.at[kind - 2],
            fw_recv.at[kind - 2], lambda d: {"grp": 1 - grp}, buffer.at[pl.ds((1 - grp) * n_tx, n_tx)], begin=False, low=0,
        )
        forward.make(0).start()
        return across, forward

    def pass_on(pair):
        across, forward = pair

        @pl.loop(1, n_tx)
        def _(step):
            across.make(step).wait_recv()
            forward.make(step).start()

    def passed_on(pair):
        pair[1].arrive()

    pair_a = final(res_a, part_a, sent_sa, s_recv_a, l_fin_a, v_fin_a, f_a, 3)
    pair_e = final(res_e, part_e, sent_se, s_recv_e, l_fin_e, v_fin_e, f_e, 2)

    padding = v_head_e.shape[0] - vocab
    l_head_a.wait()
    v_head_a[pl.ds(vocab, padding), :] = jnp.zeros((padding, width_a), BF16)
    l_head_e.wait()
    v_head_e[pl.ds(vocab, padding), :] = jnp.zeros((padding, width_e), BF16)

    n_slab = v_head_e.shape[0] // SLAB

    logit_exchanges = [
        Exchange(
            n_ty, lambda d, slab=slab: l_send.at[slab, ty_peer(d)], lambda d, slab=slab: l_recv.at[slab, d], l_ssem.at[slab],
            l_rsem.at[slab], to_ty, l_recv.at[slab, pl.ds(1, n_ty - 1)], begin=False,
        )
        for slab in range(2 * n_slab)
    ]

    own_coarse = ty // 4 == grp
    first_from, first_to = jnp.where(own_coarse, 1, 4), jnp.where(own_coarse, 4, n_ty)
    second_from, second_to = jnp.where(own_coarse, 4, 1), jnp.where(own_coarse, n_ty, 4)

    def logits(buffer, half, head, base, low, high):
        rows = unfolded(buffer[pl.ds(half * n_tx, n_tx)].astype(F32)).reshape(n_rows, head.shape[1]).astype(BF16)
        for slab in range(n_slab):
            for at in range(0, SLAB, CHUNK):
                part = mm_t(rows, head[slab * SLAB + at : slab * SLAB + at + CHUNK, :])
                part = part.reshape(n_ty // n_grp, 16, CHUNK).astype(BF16)
                l_send[base + slab, pl.ds(half * (n_ty // n_grp), n_ty // n_grp), :, at : at + CHUNK] = part
            exchange = logit_exchanges[base + slab]

            @pl.loop(low, high)
            def _(step):
                exchange.make(step).start()

    pass_on(pair_a)
    logits(f_a, grp, v_head_a, n_slab, first_from, first_to)
    passed_on(pair_a)
    logits(f_a, 1 - grp, v_head_a, n_slab, second_from, second_to)
    pass_on(pair_e)
    logits(f_e, grp, v_head_e, 0, first_from, first_to)
    passed_on(pair_e)
    logits(f_e, 1 - grp, v_head_e, 0, second_from, second_to)

    def slab_sum(slab):
        return add_up(logit_exchanges[slab], l_send[slab, ty].astype(F32), l_recv.at[slab])

    lane_c = iota((16, SLAB), 1)

    def peak_and_total(parts):
        masked = [jnp.where(lane_c + c * SLAB < vocab, part, -jnp.inf) for c, part in enumerate(parts)]
        peak = masked[0]
        for part in masked[1:]:
            peak = jnp.maximum(peak, part)
        peak = jnp.max(peak, axis=1, keepdims=True)
        total = jnp.exp(masked[0] - peak)
        for part in masked[1:]:
            total = total + jnp.exp(part - peak)
        return peak, jnp.sum(total, axis=1, keepdims=True)

    l_tokens.wait()
    row16 = iota((16, HEAD), 0)
    token = jnp.zeros((16, HEAD), jnp.int32)
    for s in range(2):
        for r in range(8):
            token = jnp.where(row16 == r // block * 8 + s * block + r % block, tokens[s, r], token)
    token = widen(token - flat * vocab, SLAB)

    drain(2 * n_slab)
    amateur = [slab_sum(n_slab + c) for c in range(n_slab)]
    peak_a, total_a = peak_and_total(amateur)
    expert = [slab_sum(c) for c in range(n_slab)]
    peak_e, total_e = peak_and_total(expert)
    chosen = jnp.zeros((16, SLAB), F32)
    mixed = []
    for c in range(n_slab):
        mixed.append(expert[c] - AMATEUR * amateur[c])
        column = lane_c + c * SLAB
        chosen = chosen + jnp.where((column == token) & (column < vocab), mixed[c], 0.0)
    chosen = jnp.sum(chosen, axis=1, keepdims=True)

    lane16 = iota((16, HEAD), 1) % 64
    tile = jnp.where(lane16 == 0, peak_e, jnp.where(lane16 == 1, total_e, 0.0))
    tile = jnp.where(lane16 == 2, peak_a, jnp.where(lane16 == 3, total_a, tile))
    tile = jnp.where(lane16 == 4, chosen, tile)
    tile = jnp.where(lane8 < 64, tile[:8], tile[8:])
    t_send[...] = tile
    stats = Exchange(n_flat, lambda d: t_send, lambda d: t_recv.at[d], t_ssem.at[0], t_rsem.at[0], flat_peer,
             t_recv.at[pl.ds(1, n_flat - 1)])
    drain(1)
    stats.arrive()
    tiles = [tile] + [t_recv[step] for step in range(1, n_flat)]
    highest = functools.reduce(jnp.maximum, tiles)
    picked = functools.reduce(jnp.add, tiles)

    def shifted(values):
        return jnp.concatenate([values[:, 1:], values[:, :1]], axis=1)

    summed_up = functools.reduce(jnp.add, [jnp.exp(t - highest) * shifted(t) for t in tiles])
    log_total = highest + jnp.log(summed_up)

    def column(values, lane):
        return jnp.concatenate([values[:, lane : lane + 1], values[:, lane + 64 : lane + 65]], axis=0)

    offset = column(log_total, 0) - AMATEUR * column(log_total, 2)
    for c in range(n_slab):
        size = min(SLAB, vocab - c * SLAB)
        contrast = mixed[c] - offset
        for s in range(2):
            low = s * block
            out_ref[s, :, c * SLAB : c * SLAB + size] = jnp.concatenate(
                [contrast[low : low + block], contrast[8 + low : 8 + low + block]], axis=0
            )[:, :size]
    value = jnp.broadcast_to(column(picked, 4) - offset, (16, HEAD))
    lane_r = iota((16, HEAD), 1)
    for s in range(2):
        mine = row16 == lane_r // block * 8 + s * block + lane_r % block
        line = jnp.sum(jnp.where(mine & (lane_r < 8), value, 0.0), axis=0, keepdims=True)
        score_ref[s : s + 1, :] = line[:, :8]

    drain(0)


def on_device(axes, *args):
    (
        hid_e, gain_e, wq_e, wk_e, wv_e, wo_e, fin_e, head_e, kc_e, vc_e,
        hid_a, gain_a, wq_a, wk_a, wv_a, wo_a, fin_a, head_a, kc_a, vc_a,
        lengths, tokens,
    ) = args
    n_grp, n_tx, n_ty = axes
    n_flat = n_grp * n_tx
    half = hid_e.shape[1] // n_grp
    vocab = head_e.shape[0]
    padded = -(-vocab // SLAB) * SLAB
    n_slab = padded // SLAB
    n_rows = 2 * half
    width_e, width_a = hid_e.shape[2], hid_a.shape[2]
    cols_e = wq_e.shape[1] + wk_e.shape[1] + wv_e.shape[1]
    cols_a = wq_a.shape[1] + wk_a.shape[1] + wv_a.shape[1]
    inner_e, inner_a = wo_e.shape[0], wo_a.shape[0]

    def like(array):
        return pltpu.VMEM(array.shape, array.dtype)

    scratch = [
        pltpu.SMEM(lengths.shape, jnp.int32), pltpu.SMEM(tokens.shape, jnp.int32),
        like(gain_e), like(fin_e), like(gain_a), like(fin_a),
    ]
    for hid, wq, wk, wv, wo, head, kc, vc in (
        (hid_e, wq_e, wk_e, wv_e, wo_e, head_e, kc_e, vc_e),
        (hid_a, wq_a, wk_a, wv_a, wo_a, head_a, kc_a, vc_a),
    ):
        scratch += [
            pltpu.VMEM((2, half, hid.shape[2]), BF16), like(wq), like(wk), like(wv), like(wo),
            pltpu.VMEM((padded, head.shape[1]), BF16), like(kc), like(vc),
        ]
    scratch += [
        pltpu.VMEM((n_ty, 8, width_e), F32), pltpu.VMEM((n_ty, 8, width_a), F32),
        pltpu.VMEM((8, HEAD), F32), pltpu.VMEM((n_ty, 8, HEAD), F32),
        pltpu.VMEM((n_ty, 8, cols_e), F32), pltpu.VMEM((n_ty, 8, cols_e), F32),
        pltpu.VMEM((n_ty, 16, cols_a // 2), BF16), pltpu.VMEM((n_ty, 16, cols_a // 2), BF16),
        pltpu.VMEM((n_ty, 16, inner_e // 2), BF16), pltpu.VMEM((n_ty, 16, inner_a // 2), BF16),
        pltpu.VMEM((n_tx, 16, width_e // 2), BF16), pltpu.VMEM((n_tx, 16, width_e // 2), BF16),
        pltpu.VMEM((n_tx, 16, width_a // 2), BF16), pltpu.VMEM((n_tx, 16, width_a // 2), BF16),
        pltpu.VMEM((8, HEAD), F32), pltpu.VMEM((n_ty, 8, HEAD), F32),
        pltpu.VMEM((8, HEAD), F32), pltpu.VMEM((n_ty, 8, HEAD), F32),
        pltpu.VMEM((n_flat, 16, width_e // 2), BF16), pltpu.VMEM((n_flat, 16, width_a // 2), BF16),
        pltpu.VMEM((2 * n_slab, n_ty, 16, SLAB), BF16), pltpu.VMEM((2 * n_slab, n_ty, 16, SLAB), BF16),
        pltpu.VMEM((8, HEAD), F32), pltpu.VMEM((n_flat, 8, HEAD), F32),
        pltpu.SemaphoreType.DMA((22,)),
        pltpu.SemaphoreType.DMA((7,)), pltpu.SemaphoreType.DMA((7,)),
        pltpu.SemaphoreType.DMA((4,)), pltpu.SemaphoreType.DMA((4, n_tx)),
        pltpu.SemaphoreType.DMA((2,)), pltpu.SemaphoreType.DMA((2,)),
        pltpu.SemaphoreType.DMA((2 * n_slab,)), pltpu.SemaphoreType.DMA((2 * n_slab,)),
        pltpu.SemaphoreType.DMA((1,)), pltpu.SemaphoreType.DMA((1,)),
    ]
    hbm = pl.BlockSpec(memory_space=pl.ANY)
    vmem = pl.BlockSpec(memory_space=pltpu.VMEM)
    macs = n_rows * (width_e * (cols_e + inner_e) + width_a * (cols_a + inner_a)) + 2 * n_rows * vocab * (width_e + width_a)
    read = sum(array.size * array.dtype.itemsize for array in args)
    return pl.pallas_call(
        functools.partial(kernel, axes, None),
        out_shape=(
            jax.ShapeDtypeStruct((2, hid_e.shape[1] // n_ty, vocab), F32),
            jax.ShapeDtypeStruct((2, hid_e.shape[1] // n_ty), F32),
        ),
        in_specs=[hbm] * len(args),
        out_specs=(vmem, vmem),
        scratch_shapes=scratch,
        compiler_params=pltpu.CompilerParams(
            collective_id=0, has_side_effects=True, vmem_limit_bytes=56 * 1024 * 1024
        ),
        cost_estimate=pl.CostEstimate(flops=2 * macs, bytes_accessed=read, transcendentals=0),
        name="contrast",
    )(*args)


def solution(mesh):
    model = (
        P(None, None, "ty"), P("ty"), P("ty", "tx"), P("ty", "tx"), P("ty", "tx"), P("tx", "ty"), P("ty"),
        P(("grp", "tx"), "ty"), P(("grp", "ty"), None, "tx"), P(("grp", "ty"), None, "tx"),
    )
    axes = tuple(mesh.shape[name] for name in ("grp", "tx", "ty"))
    return jax.shard_map(
        functools.partial(on_device, axes),
        mesh=mesh,
        in_specs=model + model + (P(("grp", "ty")), P(None, "ty")),
        out_specs=(P(None, "ty", ("grp", "tx")), P(None, "ty")),
        check_vma=False,
    )
```

```python
import functools
import math

import jax
import jax.numpy as jnp
from jax import lax
from jax.experimental import pallas as pl
from jax.experimental.pallas import tpu as pltpu
from jax.sharding import PartitionSpec as P

HEAD = 128
EPS = 1e-05
BASE = 10000.0
AMATEUR = 0.5
SCALE = HEAD**-0.5
CHUNK = 512
SLAB = 1024
F32 = jnp.float32
BF16 = jnp.bfloat16
MESH = pl.DeviceIdType.MESH


def iota(shape, axis):
    return lax.broadcasted_iota(jnp.int32, shape, axis)


def mm(a, b):
    return lax.dot_general(a, b, (((1,), (0,)), ((), ())), preferred_element_type=F32)


def mm_t(a, b):
    return lax.dot_general(a, b, (((1,), (1,)), ((), ())), preferred_element_type=F32)


def one_hot(size, source):
    out = iota((size, size), 0)
    return jnp.where(iota((size, size), 1) == source(out), 1.0, 0.0).astype(BF16)


def folded(values):
    half = values.shape[-1] // 2
    return jnp.concatenate([values[..., :half], values[..., half:]], axis=-2)


def unfolded(values):
    return jnp.concatenate([values[..., :8, :], values[..., 8:, :]], axis=-1)


def packed(values, ref):
    return values if ref.dtype == F32 else folded(values).astype(ref.dtype)


def lane_fold(values):
    total = values[:, :HEAD]
    for start in range(HEAD, values.shape[1], HEAD):
        total = total + values[:, start : start + HEAD]
    return total


def widen(column, width):
    return jnp.concatenate([column] * (width // HEAD), axis=1)


def kernel(axes, dims, *refs):
    n_grp, n_tx, n_ty = axes
    (
        hid_e, gain_e, wq_e, wk_e, wv_e, wo_e, fin_e, head_e, kc_e, vc_e,
        hid_a, gain_a, wq_a, wk_a, wv_a, wo_a, fin_a, head_a, kc_a, vc_a,
        h_lengths, h_tokens,
        out_ref, score_ref,
        lengths, tokens, v_gain_e, v_fin_e, v_gain_a, v_fin_a,
        v_hid_e, v_wq_e, v_wk_e, v_wv_e, v_wo_e, v_head_e, v_kc_e, v_vc_e,
        v_hid_a, v_wq_a, v_wk_a, v_wv_a, v_wo_a, v_head_a, v_kc_a, v_vc_a,
        x_e, x_a, sq_send, sq_recv,
        p_send_e, p_recv_e, p_send_a, p_recv_a,
        g_e, g_a,
        o_send_e, o_recv_e, o_send_a, o_recv_a,
        s_send_e, s_recv_e, s_send_a, s_recv_a,
        f_e, f_a,
        l_send, l_recv, t_send, t_recv,
        local_sem, ty_send, ty_recv, tx_send, tx_recv, fw_send, fw_recv, l_ssem, l_rsem, t_ssem, t_rsem,
    ) = refs
    grp, tx, ty = lax.axis_index("grp"), lax.axis_index("tx"), lax.axis_index("ty")
    half_rows = v_hid_e.shape[1]
    width_e, width_a = v_hid_e.shape[2], v_hid_a.shape[2]
    heads_e, heads_a = v_wq_e.shape[1] // HEAD, v_wq_a.shape[1] // HEAD
    vocab = head_e.shape[0]

    first = pl.multiple_of(grp * half_rows, half_rows)
    pairs = [
        (hid_e.at[:, pl.ds(first, half_rows)], v_hid_e),
        (hid_a.at[:, pl.ds(first, half_rows)], v_hid_a),
        (h_lengths, lengths), (gain_e, v_gain_e), (gain_a, v_gain_a),
        (fin_e, v_fin_e), (fin_a, v_fin_a), (h_tokens, tokens),
        (wq_a, v_wq_a), (wk_a, v_wk_a), (wv_a, v_wv_a),
        (wq_e, v_wq_e), (wk_e, v_wk_e), (wv_e, v_wv_e),
        (kc_a, v_kc_a), (vc_a, v_vc_a), (kc_e, v_kc_e), (vc_e, v_vc_e),
        (wo_a, v_wo_a), (wo_e, v_wo_e),
        (head_a, v_head_a.at[pl.ds(0, vocab)]), (head_e, v_head_e.at[pl.ds(0, vocab)]),
    ]
    loads = [
        pltpu.make_async_copy(source, target, local_sem.at[number])
        for number, (source, target) in enumerate(pairs)
    ]
    for load in loads[:8]:
        load.start()
    (l_hid_e, l_hid_a, l_lengths, l_gain_e, l_gain_a, l_fin_e, l_fin_a, l_tokens, l_wq_a, l_wk_a, l_wv_a, l_wq_e, l_wk_e, l_wv_e,
     l_kc_a, l_vc_a, l_kc_e, l_vc_e, l_wo_a, l_wo_e, l_head_a, l_head_e) = loads

    coarse, ring = ty // 4, lax.rem(ty, 4)
    tx_coarse, tx_ring = tx // 4, lax.rem(tx, 4)
    rings = [lax.rem(ring + step, 4) for step in range(4)]
    ty_peers = [lax.rem(coarse + step // 4, n_ty // 4) * 4 + rings[step % 4] for step in range(n_ty)]
    tx_rings = [lax.rem(tx_ring + step, 4) for step in range(4)]
    tx_sides = [lax.rem(tx_coarse + step, n_tx // 4) * 4 for step in range(n_tx // 4)]
    tx_peers = [tx_sides[step // 4] + tx_rings[step % 4] for step in range(n_tx)]
    tx_sources = [tx_sides[step // 4] + tx_rings[-step % 4] for step in range(n_tx)]
    flat = grp * n_tx + tx
    n_flat = n_grp * n_tx

    def to_ty(step):
        return {"ty": ty_peers[step]}

    def to_tx(step):
        return {"tx": tx_peers[step]}

    def flat_peer(step):
        return {"grp": lax.rem(grp + step // n_tx, n_grp), "tx": tx_peers[step % n_tx]}

    def near(step):
        return {"tx": tx_sides[step // 4] + tx_ring, "ty": ty_peers[step]}

    barrier = pltpu.get_barrier_semaphore()

    def greet(device):
        pl.semaphore_signal(barrier, inc=1, device_id=device, device_id_type=MESH)

    for step in range(n_ty - 1, 0, -1):
        greet(near(step))
    for step in range(4, n_ty):
        greet(to_ty(step))
    for step in range(n_flat - 1, 0, -1):
        greet(flat_peer(step))

    for load in loads[8:14]:
        load.start()

    started = []

    class Exchange:
        def __init__(self, n, source, target, send_sem, recv_sem, device, bulk, begin=True, each=False, low=1):
            self.n, self.low = n, low
            self.make = lambda step: pltpu.make_async_remote_copy(
                src_ref=source(step), dst_ref=target(step), send_sem=send_sem,
                recv_sem=recv_sem.at[step] if each else recv_sem, device_id=device(step), device_id_type=MESH,
            )
            self.all = lambda: pltpu.make_async_remote_copy(
                src_ref=bulk, dst_ref=bulk, send_sem=send_sem, recv_sem=recv_sem.at[0] if each else recv_sem,
                device_id=device(low), device_id_type=MESH,
            )
            started.append(self)
            if begin:
                self.begin()

        def begin(self):
            for step in range(self.n - 1, 0, -1):
                self.make(step).start()

        def arrive(self):
            self.all().wait_recv()

        def finish(self):
            self.all().wait_send()

    def drain(keep):
        while len(started) > keep:
            started.pop(0).finish()

    def add_up(exchange, total, recv):
        exchange.arrive()
        for step in range(1, exchange.n):
            total = total + recv[step].astype(F32)
        return total

    n_rows = 2 * half_rows
    block = half_rows // n_ty
    order = one_hot(
        n_rows, lambda o: (o // block) % 2 * half_rows + o // (2 * block) * block + o % block
    )
    l_hid_e.wait()
    wide_e = mm(order, v_hid_e[...].reshape(n_rows, width_e))
    x_e[...] = wide_e.reshape(n_ty, 8, width_e)
    l_hid_a.wait()
    wide_a = mm(order, v_hid_a[...].reshape(n_rows, width_a))
    x_a[...] = wide_a.reshape(n_ty, 8, width_a)
    partial = jnp.concatenate([lane_fold(wide_e * wide_e), lane_fold(wide_a * wide_a)], axis=0)
    own = jnp.broadcast_to(jnp.sum(partial.T, axis=0, keepdims=True), (8, HEAD))
    sq_send[...] = own

    pl.semaphore_wait(barrier, n_ty - 1 + n_ty - 4 + n_flat - 1)

    squares = Exchange(n_ty, lambda d: sq_send, lambda d: sq_recv.at[d], ty_send.at[0], ty_recv.at[0], near,
                       sq_recv.at[pl.ds(1, n_ty - 1)])
    for load in loads[14:18]:
        load.start()

    row8, lane8 = iota((8, HEAD), 0), iota((8, HEAD), 1)
    position = jnp.zeros((8, HEAD), jnp.int32)
    l_lengths.wait()
    for i in range(block):
        position = jnp.where(row8 % block == i, lengths[i], position)
    position = (position + row8 // block).astype(F32)
    exponent = (lane8 % (HEAD // 2)).astype(F32) * (2.0 / HEAD)
    angle = position * jnp.exp(exponent * (-math.log(BASE)))
    cosine = jnp.cos(angle)
    sine = jnp.where(lane8 < HEAD // 2, -1.0, 1.0) * jnp.sin(angle)

    def rotated(values):
        turned = jnp.concatenate([values[:, HEAD // 2 :], values[:, : HEAD // 2]], axis=1)
        return values * cosine + turned * sine

    total = add_up(squares, own, sq_recv)
    square = jnp.broadcast_to(total[0:1], (HEAD, HEAD)).T
    root_e = lax.rsqrt(square[:n_rows] / (width_e * n_ty) + EPS)
    root_a = lax.rsqrt(square[n_rows:] / (width_a * n_ty) + EPS)

    def project(x, root, g_load, gain, weights, send, recv, kind):
        width = x.shape[2]
        g_load.wait()
        values = x[...].reshape(n_rows, width)
        normed = (values * widen(root, width) * gain[...].astype(F32).reshape(1, width)).astype(BF16)
        parts = []
        for load, weight in weights:
            load.wait()
            columns = weight.shape[1]
            for at in range(0, columns, CHUNK):
                parts.append(mm(normed, weight[:, at : at + min(CHUNK, columns - at)]))
        send[...] = packed(jnp.concatenate(parts, axis=1).reshape(n_ty, 8, -1), send)
        return Exchange(n_ty, lambda d: send.at[ty_peers[d]], lambda d: recv.at[d], ty_send.at[kind], ty_recv.at[kind], to_ty,
                        recv.at[pl.ds(1, n_ty - 1)])

    sent_pa = project(x_a, root_a, l_gain_a, v_gain_a, ((l_wq_a, v_wq_a), (l_wk_a, v_wk_a), (l_wv_a, v_wv_a)), p_send_a, p_recv_a, 2)
    sent_pe = project(x_e, root_e, l_gain_e, v_gain_e, ((l_wq_e, v_wq_e), (l_wk_e, v_wk_e), (l_wv_e, v_wv_e)), p_send_e, p_recv_e, 1)

    for load in loads[18:]:
        load.start()

    def summed(exchange, send, recv, me):
        total = add_up(exchange, send[me].astype(F32), recv)
        return total if send.dtype == F32 else unfolded(total)

    def padded(rows, size):
        if rows.shape[0] == size:
            return rows
        return jnp.concatenate([rows, jnp.zeros((size - rows.shape[0], rows.shape[1]), F32)], axis=0)

    def attend(acc, heads, key_heads, k_load, keys, v_load, values):
        group = heads // key_heads
        n_query = heads * 8
        per_row = 2 * heads
        cache = keys.shape[1]
        wide = key_heads * HEAD
        query = jnp.concatenate([rotated(acc[:, h * HEAD : (h + 1) * HEAD]) for h in range(heads)], axis=0)
        at = heads * HEAD
        fresh_k = jnp.concatenate(
            [rotated(acc[:, at + h * HEAD : at + (h + 1) * HEAD]) for h in range(key_heads)], axis=0
        )
        at += wide
        fresh_v = jnp.concatenate(
            [acc[:, at + h * HEAD : at + (h + 1) * HEAD] for h in range(key_heads)], axis=0
        )
        fresh_k = padded(fresh_k, HEAD).astype(BF16)
        fresh_v = padded(fresh_v, HEAD).astype(BF16)
        forth = one_hot(n_query, lambda o: o % heads * 8 + o // heads % 2 * block + o // per_row)
        back = one_hot(n_query, lambda o: o % block * per_row + o // block % 2 * heads + o // 8)
        query = mm(forth, query.astype(BF16))
        owner = iota((n_query, HEAD), 0)
        lane = iota((n_query, HEAD), 1)
        fresh = mm_t(query.astype(BF16), fresh_k) * SCALE
        seen = (
            (lane < key_heads * 8)
            & (lane // 8 == owner % heads // group)
            & (lane % block == owner // per_row)
            & (lane // block % 2 <= owner // heads % 2)
        )
        fresh = jnp.where(seen, fresh, -jnp.inf)
        if key_heads > 1:
            spread = widen(query, wide)
            keep = iota((n_query, wide), 1) // HEAD == iota((n_query, wide), 0) % heads // group
            query = jnp.where(keep, spread, 0.0)
        k_load.wait()
        cached = []
        for i in range(block):
            part = query[i * per_row : (i + 1) * per_row].astype(BF16)
            score = mm_t(part, keys[i]) * SCALE
            cached.append(jnp.where(iota((per_row, cache), 1) < lengths[i], score, -jnp.inf))
        cached = jnp.concatenate(cached, axis=0)
        peak = jnp.maximum(jnp.max(cached, axis=1, keepdims=True), jnp.max(fresh, axis=1, keepdims=True))
        cached = jnp.exp(cached - peak)
        fresh = jnp.exp(fresh - peak)
        total = jnp.sum(cached, axis=1, keepdims=True) + jnp.sum(fresh, axis=1, keepdims=True)
        v_load.wait()
        mixture = jnp.concatenate(
            [mm(cached[i * per_row : (i + 1) * per_row].astype(BF16), values[i]) for i in range(block)], axis=0
        )
        if key_heads > 1:
            picked = jnp.zeros((n_query, HEAD), F32)
            for h in range(key_heads):
                picked = picked + jnp.where(owner % heads // group == h, mixture[:, h * HEAD : (h + 1) * HEAD], 0.0)
            mixture = picked
        mixture = mixture + mm(fresh.astype(BF16), fresh_v)
        ready = mm(back, (mixture / total).astype(BF16))
        return jnp.concatenate([ready[h * 8 : (h + 1) * 8] for h in range(heads)], axis=1)

    def gather(rows, buffer, kind):
        buffer[ty] = folded(rows).astype(BF16)
        return Exchange(n_ty, lambda d: buffer.at[ty], lambda d: buffer.at[ty], ty_send.at[kind], ty_recv.at[kind], to_ty,
                        buffer.at[pl.ds(0, n_ty - 1)])

    acc = summed(sent_pa, p_send_a, p_recv_a, ty)
    sent_ga = gather(attend(acc, heads_a, v_wk_a.shape[1] // HEAD, l_kc_a, v_kc_a, l_vc_a, v_vc_a), g_a, 4)
    acc = summed(sent_pe, p_send_e, p_recv_e, ty)
    sent_ge = gather(attend(acc, heads_e, v_wk_e.shape[1] // HEAD, l_kc_e, v_kc_e, l_vc_e, v_vc_e), g_e, 3)
    drain(2)

    def output(exchange, buffer, load, weight, send, recv, kind):
        exchange.arrive()
        rows = unfolded(buffer[...].astype(F32)).reshape(n_rows, weight.shape[0]).astype(BF16)
        load.wait()
        columns = weight.shape[1]
        parts = [mm(rows, weight[:, at : at + CHUNK]) for at in range(0, columns, CHUNK)]
        send[...] = packed(jnp.concatenate(parts, axis=1).reshape(n_tx, 8, columns), send)
        return Exchange(n_tx, lambda d: send.at[tx_peers[d]], lambda d: recv.at[d], tx_send.at[kind], tx_recv.at[kind, 0], to_tx,
                        recv.at[pl.ds(1, n_tx - 1)])

    sent_oa = output(sent_ga, g_a, l_wo_a, v_wo_a, o_send_a, o_recv_a, 1)
    sent_oe = output(sent_ge, g_e, l_wo_e, v_wo_e, o_send_e, o_recv_e, 0)
    drain(2)

    def residual(exchange, x, send, recv, s_send, s_recv, kind):
        values = x[tx] + summed(exchange, send, recv, tx)
        part = lane_fold(values * values)
        s_send[...] = part
        return values, part, Exchange(
            n_ty, lambda d: s_send, lambda d: s_recv.at[d], ty_send.at[kind], ty_recv.at[kind], to_ty,
            s_recv.at[pl.ds(1, n_ty - 1)],
        )

    res_a, part_a, sent_sa = residual(sent_oa, x_a, o_send_a, o_recv_a, s_send_a, s_recv_a, 6)
    res_e, part_e, sent_se = residual(sent_oe, x_e, o_send_e, o_recv_e, s_send_e, s_recv_e, 5)
    drain(2)

    def final(values, part, exchange, s_recv, g_load, gain, buffer, kind):
        width = values.shape[1]
        g_load.wait()
        part = add_up(exchange, part, s_recv)
        mean = jnp.sum(part, axis=1, keepdims=True) / (width * n_ty)
        rows = values * lax.rsqrt(mean + EPS) * gain[...].astype(F32).reshape(1, width)
        buffer[flat] = folded(rows).astype(BF16)
        across = Exchange(
            n_tx, lambda d: buffer.at[flat], lambda d: buffer.at[flat], tx_send.at[kind], tx_recv.at[kind], to_tx,
            buffer.at[pl.ds(0, n_tx - 1)], each=True,
        )

        def from_tx(step):
            return grp * n_tx + tx_sources[step]

        forward = Exchange(
            n_tx, lambda d: buffer.at[from_tx(d)], lambda d: buffer.at[from_tx(d)], fw_send.at[kind - 2],
            fw_recv.at[kind - 2], lambda d: {"grp": 1 - grp}, buffer.at[pl.ds((1 - grp) * n_tx, n_tx)], begin=False, low=0,
        )
        forward.make(0).start()
        return across, forward

    def pass_on(pair):
        across, forward = pair

        for step in (1, 3, 4, 2, 5, 7, 6):
            across.make(step).wait_recv()
            forward.make(step).start()

    def passed_on(pair):
        pair[1].arrive()

    pair_a = final(res_a, part_a, sent_sa, s_recv_a, l_fin_a, v_fin_a, f_a, 3)
    pair_e = final(res_e, part_e, sent_se, s_recv_e, l_fin_e, v_fin_e, f_e, 2)

    padding = v_head_e.shape[0] - vocab
    l_head_a.wait()
    v_head_a[pl.ds(vocab, padding), :] = jnp.zeros((padding, width_a), BF16)
    l_head_e.wait()
    v_head_e[pl.ds(vocab, padding), :] = jnp.zeros((padding, width_e), BF16)

    n_slab = v_head_e.shape[0] // SLAB

    logit_exchanges = [
        Exchange(
            n_ty, None, None, l_ssem.at[slab], l_rsem.at[slab], to_ty, l_recv.at[slab, pl.ds(1, n_ty - 1)], begin=False,
        )
        for slab in range(2 * n_slab)
    ]

    def logits(buffer, half, head, base):
        rows = unfolded(buffer[pl.ds(half * n_tx, n_tx)].astype(F32)).reshape(n_rows, head.shape[1]).astype(BF16)
        side = jnp.where(half == coarse, 0, 4)

        def copy(slab, step):
            target = half * 4 + rings[step]
            return pltpu.make_async_remote_copy(
                src_ref=l_send.at[slab, target], dst_ref=l_recv.at[slab, side + step], send_sem=l_ssem.at[slab],
                recv_sem=l_rsem.at[slab], device_id={"ty": target}, device_id_type=MESH,
            )

        for slab in range(n_slab):
            for at in range(0, SLAB, CHUNK):
                part = mm_t(rows, head[slab * SLAB + at : slab * SLAB + at + CHUNK, :])
                part = part.reshape(4, 16, CHUNK).astype(BF16)
                l_send[base + slab, pl.ds(half * 4, 4), :, at : at + CHUNK] = part
            for step in (2, 1, 3):
                copy(base + slab, step).start()

            @pl.when(half != coarse)
            def _():
                copy(base + slab, 0).start()

    pass_on(pair_a)
    logits(f_a, grp, v_head_a, n_slab)
    pass_on(pair_e)
    passed_on(pair_a)
    logits(f_a, 1 - grp, v_head_a, n_slab)
    logits(f_e, grp, v_head_e, 0)
    passed_on(pair_e)
    logits(f_e, 1 - grp, v_head_e, 0)

    def slab_sum(slab):
        return add_up(logit_exchanges[slab], l_send[slab, ty].astype(F32), l_recv.at[slab])

    lane_c = iota((16, SLAB), 1)

    def peak_and_total(parts):
        masked = [jnp.where(lane_c + c * SLAB < vocab, part, -jnp.inf) for c, part in enumerate(parts)]
        peak = masked[0]
        for part in masked[1:]:
            peak = jnp.maximum(peak, part)
        peak = jnp.max(peak, axis=1, keepdims=True)
        total = jnp.exp(masked[0] - peak)
        for part in masked[1:]:
            total = total + jnp.exp(part - peak)
        return peak, jnp.sum(total, axis=1, keepdims=True)

    l_tokens.wait()
    row16 = iota((16, HEAD), 0)
    token = jnp.zeros((16, HEAD), jnp.int32)
    for s in range(2):
        for r in range(8):
            token = jnp.where(row16 == r // block * 8 + s * block + r % block, tokens[s, r], token)
    token = widen(token - flat * vocab, SLAB)

    drain(2 * n_slab)
    amateur = [slab_sum(n_slab + c) for c in range(n_slab)]
    peak_a, total_a = peak_and_total(amateur)
    expert = [slab_sum(c) for c in range(n_slab)]
    peak_e, total_e = peak_and_total(expert)
    chosen = jnp.zeros((16, SLAB), F32)
    mixed = []
    for c in range(n_slab):
        mixed.append(expert[c] - AMATEUR * amateur[c])
        column = lane_c + c * SLAB
        chosen = chosen + jnp.where((column == token) & (column < vocab), mixed[c], 0.0)
    chosen = jnp.sum(chosen, axis=1, keepdims=True)

    lane16 = iota((16, HEAD), 1) % 64
    tile = jnp.where(lane16 == 0, peak_e, jnp.where(lane16 == 1, total_e, 0.0))
    tile = jnp.where(lane16 == 2, peak_a, jnp.where(lane16 == 3, total_a, tile))
    tile = jnp.where(lane16 == 4, chosen, tile)
    tile = jnp.where(lane8 < 64, tile[:8], tile[8:])
    t_send[...] = tile
    stats = Exchange(n_flat, lambda d: t_send, lambda d: t_recv.at[d], t_ssem.at[0], t_rsem.at[0], flat_peer,
             t_recv.at[pl.ds(1, n_flat - 1)])
    drain(1)
    stats.arrive()
    tiles = [tile] + [t_recv[step] for step in range(1, n_flat)]
    highest = functools.reduce(jnp.maximum, tiles)
    picked = functools.reduce(jnp.add, tiles)

    def shifted(values):
        return jnp.concatenate([values[:, 1:], values[:, :1]], axis=1)

    summed_up = functools.reduce(jnp.add, [jnp.exp(t - highest) * shifted(t) for t in tiles])
    log_total = highest + jnp.log(summed_up)

    def column(values, lane):
        return jnp.concatenate([values[:, lane : lane + 1], values[:, lane + 64 : lane + 65]], axis=0)

    offset = column(log_total, 0) - AMATEUR * column(log_total, 2)
    for c in range(n_slab):
        size = min(SLAB, vocab - c * SLAB)
        contrast = mixed[c] - offset
        for s in range(2):
            low = s * block
            out_ref[s, :, c * SLAB : c * SLAB + size] = jnp.concatenate(
                [contrast[low : low + block], contrast[8 + low : 8 + low + block]], axis=0
            )[:, :size]
    value = jnp.broadcast_to(column(picked, 4) - offset, (16, HEAD))
    lane_r = iota((16, HEAD), 1)
    for s in range(2):
        mine = row16 == lane_r // block * 8 + s * block + lane_r % block
        line = jnp.sum(jnp.where(mine & (lane_r < 8), value, 0.0), axis=0, keepdims=True)
        score_ref[s : s + 1, :] = line[:, :8]

    drain(0)


def on_device(axes, *args):
    (
        hid_e, gain_e, wq_e, wk_e, wv_e, wo_e, fin_e, head_e, kc_e, vc_e,
        hid_a, gain_a, wq_a, wk_a, wv_a, wo_a, fin_a, head_a, kc_a, vc_a,
        lengths, tokens,
    ) = args
    n_grp, n_tx, n_ty = axes
    n_flat = n_grp * n_tx
    half = hid_e.shape[1] // n_grp
    vocab = head_e.shape[0]
    padded = -(-vocab // SLAB) * SLAB
    n_slab = padded // SLAB
    n_rows = 2 * half
    width_e, width_a = hid_e.shape[2], hid_a.shape[2]
    cols_e = wq_e.shape[1] + wk_e.shape[1] + wv_e.shape[1]
    cols_a = wq_a.shape[1] + wk_a.shape[1] + wv_a.shape[1]
    inner_e, inner_a = wo_e.shape[0], wo_a.shape[0]

    def like(array):
        return pltpu.VMEM(array.shape, array.dtype)

    scratch = [
        pltpu.SMEM(lengths.shape, jnp.int32), pltpu.SMEM(tokens.shape, jnp.int32),
        like(gain_e), like(fin_e), like(gain_a), like(fin_a),
    ]
    for hid, wq, wk, wv, wo, head, kc, vc in (
        (hid_e, wq_e, wk_e, wv_e, wo_e, head_e, kc_e, vc_e),
        (hid_a, wq_a, wk_a, wv_a, wo_a, head_a, kc_a, vc_a),
    ):
        scratch += [
            pltpu.VMEM((2, half, hid.shape[2]), BF16), like(wq), like(wk), like(wv), like(wo),
            pltpu.VMEM((padded, head.shape[1]), BF16), like(kc), like(vc),
        ]
    scratch += [
        pltpu.VMEM((n_ty, 8, width_e), F32), pltpu.VMEM((n_ty, 8, width_a), F32),
        pltpu.VMEM((8, HEAD), F32), pltpu.VMEM((n_ty, 8, HEAD), F32),
        pltpu.VMEM((n_ty, 8, cols_e), F32), pltpu.VMEM((n_ty, 8, cols_e), F32),
        pltpu.VMEM((n_ty, 16, cols_a // 2), BF16), pltpu.VMEM((n_ty, 16, cols_a // 2), BF16),
        pltpu.VMEM((n_ty, 16, inner_e // 2), BF16), pltpu.VMEM((n_ty, 16, inner_a // 2), BF16),
        pltpu.VMEM((n_tx, 16, width_e // 2), BF16), pltpu.VMEM((n_tx, 16, width_e // 2), BF16),
        pltpu.VMEM((n_tx, 16, width_a // 2), BF16), pltpu.VMEM((n_tx, 16, width_a // 2), BF16),
        pltpu.VMEM((8, HEAD), F32), pltpu.VMEM((n_ty, 8, HEAD), F32),
        pltpu.VMEM((8, HEAD), F32), pltpu.VMEM((n_ty, 8, HEAD), F32),
        pltpu.VMEM((n_flat, 16, width_e // 2), BF16), pltpu.VMEM((n_flat, 16, width_a // 2), BF16),
        pltpu.VMEM((2 * n_slab, n_ty, 16, SLAB), BF16), pltpu.VMEM((2 * n_slab, n_ty, 16, SLAB), BF16),
        pltpu.VMEM((8, HEAD), F32), pltpu.VMEM((n_flat, 8, HEAD), F32),
        pltpu.SemaphoreType.DMA((22,)),
        pltpu.SemaphoreType.DMA((7,)), pltpu.SemaphoreType.DMA((7,)),
        pltpu.SemaphoreType.DMA((4,)), pltpu.SemaphoreType.DMA((4, n_tx)),
        pltpu.SemaphoreType.DMA((2,)), pltpu.SemaphoreType.DMA((2,)),
        pltpu.SemaphoreType.DMA((2 * n_slab,)), pltpu.SemaphoreType.DMA((2 * n_slab,)),
        pltpu.SemaphoreType.DMA((1,)), pltpu.SemaphoreType.DMA((1,)),
    ]
    hbm = pl.BlockSpec(memory_space=pl.ANY)
    vmem = pl.BlockSpec(memory_space=pltpu.VMEM)
    macs = n_rows * (width_e * (cols_e + inner_e) + width_a * (cols_a + inner_a)) + 2 * n_rows * vocab * (width_e + width_a)
    read = sum(array.size * array.dtype.itemsize for array in args)
    return pl.pallas_call(
        functools.partial(kernel, axes, None),
        out_shape=(
            pltpu.VMEM((2, hid_e.shape[1] // n_ty, vocab), F32),
            pltpu.VMEM((2, hid_e.shape[1] // n_ty), F32),
        ),
        in_specs=[hbm] * len(args),
        out_specs=(vmem, vmem),
        scratch_shapes=scratch,
        compiler_params=pltpu.CompilerParams(
            collective_id=0, has_side_effects=True, vmem_limit_bytes=56 * 1024 * 1024
        ),
        cost_estimate=pl.CostEstimate(flops=2 * macs, bytes_accessed=read, transcendentals=0),
        name="contrast",
    )(*args)


def solution(mesh):
    model = (
        P(None, None, "ty"), P("ty"), P("ty", "tx"), P("ty", "tx"), P("ty", "tx"), P("tx", "ty"), P("ty"),
        P(("grp", "tx"), "ty"), P(("grp", "ty"), None, "tx"), P(("grp", "ty"), None, "tx"),
    )
    axes = tuple(mesh.shape[name] for name in ("grp", "tx", "ty"))
    return jax.shard_map(
        functools.partial(on_device, axes),
        mesh=mesh,
        in_specs=model + model + (P(("grp", "ty")), P(None, "ty")),
        out_specs=(P(None, "ty", ("grp", "tx")), P(None, "ty")),
        check_vma=False,
    )
```

```python
import functools
import math

import jax
import jax.numpy as jnp
from jax import lax
from jax.experimental import pallas as pl
from jax.experimental.pallas import tpu as pltpu
from jax.sharding import PartitionSpec as P

HEAD = 128
EPS = 1e-05
BASE = 10000.0
AMATEUR = 0.5
SCALE = HEAD**-0.5
CHUNK = 512
SLAB = 1024
F32 = jnp.float32
BF16 = jnp.bfloat16
MESH = pl.DeviceIdType.MESH


def iota(shape, axis):
    return lax.broadcasted_iota(jnp.int32, shape, axis)


def mm(a, b):
    return lax.dot_general(a, b, (((1,), (0,)), ((), ())), preferred_element_type=F32)


def mm_t(a, b):
    return lax.dot_general(a, b, (((1,), (1,)), ((), ())), preferred_element_type=F32)


def one_hot(size, source):
    out = iota((size, size), 0)
    return jnp.where(iota((size, size), 1) == source(out), 1.0, 0.0).astype(BF16)


def folded(values):
    half = values.shape[-1] // 2
    return jnp.concatenate([values[..., :half], values[..., half:]], axis=-2)


def unfolded(values):
    return jnp.concatenate([values[..., :8, :], values[..., 8:, :]], axis=-1)


def packed(values, ref):
    return values if ref.dtype == F32 else folded(values).astype(ref.dtype)


def lane_fold(values):
    total = values[:, :HEAD]
    for start in range(HEAD, values.shape[1], HEAD):
        total = total + values[:, start : start + HEAD]
    return total


def widen(column, width):
    return jnp.concatenate([column] * (width // HEAD), axis=1)


def kernel(axes, dims, *refs):
    n_grp, n_tx, n_ty = axes
    (
        hid_e, gain_e, wq_e, wk_e, wv_e, wo_e, fin_e, head_e, kc_e, vc_e,
        hid_a, gain_a, wq_a, wk_a, wv_a, wo_a, fin_a, head_a, kc_a, vc_a,
        h_lengths, h_tokens,
        out_ref, score_ref,
        lengths, tokens, v_gain_e, v_fin_e, v_gain_a, v_fin_a,
        v_hid_e, v_wq_e, v_wk_e, v_wv_e, v_wo_e, v_head_e, v_kc_e, v_vc_e,
        v_hid_a, v_wq_a, v_wk_a, v_wv_a, v_wo_a, v_head_a, v_kc_a, v_vc_a,
        x_e, x_a, sq_send, sq_recv,
        p_send_e, p_recv_e, p_send_a, p_recv_a,
        g_e, g_a,
        o_send_e, o_recv_e, o_send_a, o_recv_a,
        s_send_e, s_recv_e, s_send_a, s_recv_a,
        f_e, f_a,
        l_send, l_recv, t_send, t_recv,
        local_sem, ty_send, ty_recv, tx_send, tx_recv, fw_send, fw_recv, l_ssem, l_rsem, t_ssem, t_rsem,
    ) = refs
    grp, tx, ty = lax.axis_index("grp"), lax.axis_index("tx"), lax.axis_index("ty")
    half_rows = v_hid_e.shape[1]
    width_e, width_a = v_hid_e.shape[2], v_hid_a.shape[2]
    heads_e, heads_a = v_wq_e.shape[1] // HEAD, v_wq_a.shape[1] // HEAD
    vocab = head_e.shape[0]

    first = pl.multiple_of(grp * half_rows, half_rows)
    pairs = [
        (hid_e.at[:, pl.ds(first, half_rows)], v_hid_e),
        (hid_a.at[:, pl.ds(first, half_rows)], v_hid_a),
        (h_lengths, lengths), (gain_e, v_gain_e), (gain_a, v_gain_a),
        (fin_e, v_fin_e), (fin_a, v_fin_a), (h_tokens, tokens),
        (wq_a, v_wq_a), (wk_a, v_wk_a), (wv_a, v_wv_a),
        (wq_e, v_wq_e), (wk_e, v_wk_e), (wv_e, v_wv_e),
        (kc_a, v_kc_a), (vc_a, v_vc_a), (kc_e, v_kc_e), (vc_e, v_vc_e),
        (wo_a, v_wo_a), (wo_e, v_wo_e),
        (head_a, v_head_a.at[pl.ds(0, vocab)]), (head_e, v_head_e.at[pl.ds(0, vocab)]),
    ]
    loads = [
        pltpu.make_async_copy(source, target, local_sem.at[number])
        for number, (source, target) in enumerate(pairs)
    ]
    for load in loads[:2]:
        load.start()
    (l_hid_e, l_hid_a, l_lengths, l_gain_e, l_gain_a, l_fin_e, l_fin_a, l_tokens, l_wq_a, l_wk_a, l_wv_a, l_wq_e, l_wk_e, l_wv_e,
     l_kc_a, l_vc_a, l_kc_e, l_vc_e, l_wo_a, l_wo_e, l_head_a, l_head_e) = loads

    coarse, ring = ty // 4, lax.rem(ty, 4)
    tx_coarse, tx_ring = tx // 4, lax.rem(tx, 4)
    rings = [lax.rem(ring + step, 4) for step in range(4)]
    ty_peers = [lax.rem(coarse + step // 4, n_ty // 4) * 4 + rings[step % 4] for step in range(n_ty)]
    tx_rings = [lax.rem(tx_ring + step, 4) for step in range(4)]
    tx_sides = [lax.rem(tx_coarse + step, n_tx // 4) * 4 for step in range(n_tx // 4)]
    tx_peers = [tx_sides[step // 4] + tx_rings[step % 4] for step in range(n_tx)]
    tx_sources = [tx_sides[step // 4] + tx_rings[-step % 4] for step in range(n_tx)]
    flat = grp * n_tx + tx
    n_flat = n_grp * n_tx

    def to_ty(step):
        return {"ty": ty_peers[step]}

    def to_tx(step):
        return {"tx": tx_peers[step]}

    def flat_peer(step):
        return {"grp": lax.rem(grp + step // n_tx, n_grp), "tx": tx_peers[step % n_tx]}

    def near(step):
        return {"tx": tx_sides[step // 4] + tx_ring, "ty": ty_peers[step]}

    barrier = pltpu.get_barrier_semaphore()

    def greet(device):
        pl.semaphore_signal(barrier, inc=1, device_id=device, device_id_type=MESH)

    for step in range(n_ty - 1, 0, -1):
        greet(near(step))
    for step in range(4, n_ty):
        greet(to_ty(step))
    for step in range(n_flat - 1, 0, -1):
        greet(flat_peer(step))

    for load in loads[2:14]:
        load.start()

    started = []

    class Exchange:
        def __init__(self, n, source, target, send_sem, recv_sem, device, bulk, begin=True, each=False, low=1):
            self.n, self.low = n, low
            self.make = lambda step: pltpu.make_async_remote_copy(
                src_ref=source(step), dst_ref=target(step), send_sem=send_sem,
                recv_sem=recv_sem.at[step] if each else recv_sem, device_id=device(step), device_id_type=MESH,
            )
            self.all = lambda: pltpu.make_async_remote_copy(
                src_ref=bulk, dst_ref=bulk, send_sem=send_sem, recv_sem=recv_sem.at[0] if each else recv_sem,
                device_id=device(low), device_id_type=MESH,
            )
            started.append(self)
            if begin:
                self.begin()

        def begin(self):
            for step in range(self.n - 1, 0, -1):
                self.make(step).start()

        def arrive(self):
            self.all().wait_recv()

        def finish(self):
            self.all().wait_send()

    def drain(keep):
        while len(started) > keep:
            started.pop(0).finish()

    def add_up(exchange, total, recv):
        exchange.arrive()
        for step in range(1, exchange.n):
            total = total + recv[step].astype(F32)
        return total

    n_rows = 2 * half_rows
    block = half_rows // n_ty
    order = one_hot(
        n_rows, lambda o: (o // block) % 2 * half_rows + o // (2 * block) * block + o % block
    )
    l_hid_e.wait()
    wide_e = mm(order, v_hid_e[...].reshape(n_rows, width_e))
    x_e[...] = wide_e.reshape(n_ty, 8, width_e)
    l_hid_a.wait()
    wide_a = mm(order, v_hid_a[...].reshape(n_rows, width_a))
    x_a[...] = wide_a.reshape(n_ty, 8, width_a)
    partial = jnp.concatenate([lane_fold(wide_e * wide_e), lane_fold(wide_a * wide_a)], axis=0)
    own = jnp.broadcast_to(jnp.sum(partial.T, axis=0, keepdims=True), (8, HEAD))
    sq_send[...] = own

    pl.semaphore_wait(barrier, n_ty - 1 + n_ty - 4 + n_flat - 1)

    squares = Exchange(n_ty, lambda d: sq_send, lambda d: sq_recv.at[d], ty_send.at[0], ty_recv.at[0], near,
                       sq_recv.at[pl.ds(1, n_ty - 1)])
    for load in loads[14:18]:
        load.start()

    row8, lane8 = iota((8, HEAD), 0), iota((8, HEAD), 1)
    position = jnp.zeros((8, HEAD), jnp.int32)
    l_lengths.wait()
    for i in range(block):
        position = jnp.where(row8 % block == i, lengths[i], position)
    position = (position + row8 // block).astype(F32)
    exponent = (lane8 % (HEAD // 2)).astype(F32) * (2.0 / HEAD)
    angle = position * jnp.exp(exponent * (-math.log(BASE)))
    cosine = jnp.cos(angle)
    sine = jnp.where(lane8 < HEAD // 2, -1.0, 1.0) * jnp.sin(angle)

    def rotated(values):
        turned = jnp.concatenate([values[:, HEAD // 2 :], values[:, : HEAD // 2]], axis=1)
        return values * cosine + turned * sine

    total = add_up(squares, own, sq_recv)
    square = jnp.broadcast_to(total[0:1], (HEAD, HEAD)).T
    root_e = lax.rsqrt(square[:n_rows] / (width_e * n_ty) + EPS)
    root_a = lax.rsqrt(square[n_rows:] / (width_a * n_ty) + EPS)

    def project(x, root, g_load, gain, weights, send, recv, kind):
        width = x.shape[2]
        g_load.wait()
        values = x[...].reshape(n_rows, width)
        normed = (values * widen(root, width) * gain[...].astype(F32).reshape(1, width)).astype(BF16)
        parts = []
        for load, weight in weights:
            load.wait()
            columns = weight.shape[1]
            for at in range(0, columns, CHUNK):
                parts.append(mm(normed, weight[:, at : at + min(CHUNK, columns - at)]))
        send[...] = packed(jnp.concatenate(parts, axis=1).reshape(n_ty, 8, -1), send)
        return Exchange(n_ty, lambda d: send.at[ty_peers[d]], lambda d: recv.at[d], ty_send.at[kind], ty_recv.at[kind], to_ty,
                        recv.at[pl.ds(1, n_ty - 1)])

    sent_pa = project(x_a, root_a, l_gain_a, v_gain_a, ((l_wq_a, v_wq_a), (l_wk_a, v_wk_a), (l_wv_a, v_wv_a)), p_send_a, p_recv_a, 2)
    sent_pe = project(x_e, root_e, l_gain_e, v_gain_e, ((l_wq_e, v_wq_e), (l_wk_e, v_wk_e), (l_wv_e, v_wv_e)), p_send_e, p_recv_e, 1)

    for load in loads[18:]:
        load.start()

    def summed(exchange, send, recv, me):
        total = add_up(exchange, send[me].astype(F32), recv)
        return total if send.dtype == F32 else unfolded(total)

    def padded(rows, size):
        if rows.shape[0] == size:
            return rows
        return jnp.concatenate([rows, jnp.zeros((size - rows.shape[0], rows.shape[1]), F32)], axis=0)

    def attend(acc, heads, key_heads, k_load, keys, v_load, values):
        group = heads // key_heads
        n_query = heads * 8
        cache = keys.shape[1]
        wide = key_heads * HEAD
        query = jnp.concatenate([rotated(acc[:, h * HEAD : (h + 1) * HEAD]) for h in range(heads)], axis=0)
        at = heads * HEAD
        fresh_k = jnp.concatenate(
            [rotated(acc[:, at + h * HEAD : at + (h + 1) * HEAD]) for h in range(key_heads)], axis=0
        )
        at += wide
        fresh_v = jnp.concatenate(
            [acc[:, at + h * HEAD : at + (h + 1) * HEAD] for h in range(key_heads)], axis=0
        )
        fresh_k = padded(fresh_k, HEAD).astype(BF16)
        fresh_v = padded(fresh_v, HEAD).astype(BF16)
        owner = iota((n_query, HEAD), 0)
        lane = iota((n_query, HEAD), 1)
        fresh = mm_t(query.astype(BF16), fresh_k) * SCALE
        seen = (
            (lane < key_heads * 8)
            & (lane // 8 == owner // 8 // group)
            & (lane % block == owner % block)
            & (lane // block % 2 <= owner // block % 2)
        )
        fresh = jnp.where(seen, fresh, -jnp.inf)
        if key_heads > 1:
            keep = iota((n_query, wide), 1) // HEAD == iota((n_query, wide), 0) // 8 // group
            query = jnp.where(keep, widen(query, wide), 0.0)
        query = query.astype(BF16)
        length = jnp.zeros((n_query, HEAD), jnp.int32)
        for i in range(block):
            length = jnp.where(owner % block == i, lengths[i], length)

        def of_own_row(operand, rows, multiply):
            picked = None
            for i in range(block):
                part = multiply(operand, rows[i])
                own = widen(owner % block == i, part.shape[1])
                picked = part if i == 0 else jnp.where(own, part, picked)
            return picked

        k_load.wait()
        cached = of_own_row(query, keys, mm_t) * SCALE
        cached = jnp.where(iota((n_query, cache), 1) < widen(length, cache), cached, -jnp.inf)
        peak = jnp.maximum(jnp.max(cached, axis=1, keepdims=True), jnp.max(fresh, axis=1, keepdims=True))
        cached = jnp.exp(cached - peak)
        fresh = jnp.exp(fresh - peak)
        total = jnp.sum(cached, axis=1, keepdims=True) + jnp.sum(fresh, axis=1, keepdims=True)
        v_load.wait()
        mixture = of_own_row(cached.astype(BF16), values, mm)
        if key_heads > 1:
            picked = jnp.zeros((n_query, HEAD), F32)
            for h in range(key_heads):
                picked = picked + jnp.where(owner // 8 // group == h, mixture[:, h * HEAD : (h + 1) * HEAD], 0.0)
            mixture = picked
        ready = (mixture + mm(fresh.astype(BF16), fresh_v)) / total
        return jnp.concatenate([ready[h * 8 : (h + 1) * 8] for h in range(heads)], axis=1)

    def gather(rows, buffer, kind):
        buffer[ty] = folded(rows).astype(BF16)
        return Exchange(n_ty, lambda d: buffer.at[ty], lambda d: buffer.at[ty], ty_send.at[kind], ty_recv.at[kind], to_ty,
                        buffer.at[pl.ds(0, n_ty - 1)])

    acc = summed(sent_pa, p_send_a, p_recv_a, ty)
    sent_ga = gather(attend(acc, heads_a, v_wk_a.shape[1] // HEAD, l_kc_a, v_kc_a, l_vc_a, v_vc_a), g_a, 4)
    acc = summed(sent_pe, p_send_e, p_recv_e, ty)
    sent_ge = gather(attend(acc, heads_e, v_wk_e.shape[1] // HEAD, l_kc_e, v_kc_e, l_vc_e, v_vc_e), g_e, 3)
    drain(2)

    def output(exchange, buffer, load, weight, send, recv, kind):
        exchange.arrive()
        rows = unfolded(buffer[...].astype(F32)).reshape(n_rows, weight.shape[0]).astype(BF16)
        load.wait()
        columns = weight.shape[1]
        parts = [mm(rows, weight[:, at : at + CHUNK]) for at in range(0, columns, CHUNK)]
        send[...] = packed(jnp.concatenate(parts, axis=1).reshape(n_tx, 8, columns), send)
        return Exchange(n_tx, lambda d: send.at[tx_peers[d]], lambda d: recv.at[d], tx_send.at[kind], tx_recv.at[kind, 0], to_tx,
                        recv.at[pl.ds(1, n_tx - 1)])

    sent_oa = output(sent_ga, g_a, l_wo_a, v_wo_a, o_send_a, o_recv_a, 1)
    sent_oe = output(sent_ge, g_e, l_wo_e, v_wo_e, o_send_e, o_recv_e, 0)
    drain(2)

    def residual(exchange, x, send, recv, s_send, s_recv, kind):
        values = x[tx] + summed(exchange, send, recv, tx)
        part = lane_fold(values * values)
        s_send[...] = part
        return values, part, Exchange(
            n_ty, lambda d: s_send, lambda d: s_recv.at[d], ty_send.at[kind], ty_recv.at[kind], to_ty,
            s_recv.at[pl.ds(1, n_ty - 1)],
        )

    res_a, part_a, sent_sa = residual(sent_oa, x_a, o_send_a, o_recv_a, s_send_a, s_recv_a, 6)
    res_e, part_e, sent_se = residual(sent_oe, x_e, o_send_e, o_recv_e, s_send_e, s_recv_e, 5)
    drain(2)

    def final(values, part, exchange, s_recv, g_load, gain, buffer, kind):
        width = values.shape[1]
        g_load.wait()
        part = add_up(exchange, part, s_recv)
        mean = jnp.sum(part, axis=1, keepdims=True) / (width * n_ty)
        rows = values * lax.rsqrt(mean + EPS) * gain[...].astype(F32).reshape(1, width)
        buffer[flat] = folded(rows).astype(BF16)
        across = Exchange(
            n_tx, lambda d: buffer.at[flat], lambda d: buffer.at[flat], tx_send.at[kind], tx_recv.at[kind], to_tx,
            buffer.at[pl.ds(0, n_tx - 1)], each=True,
        )

        def from_tx(step):
            return grp * n_tx + tx_sources[step]

        forward = Exchange(
            n_tx, lambda d: buffer.at[from_tx(d)], lambda d: buffer.at[from_tx(d)], fw_send.at[kind - 2],
            fw_recv.at[kind - 2], lambda d: {"grp": 1 - grp}, buffer.at[pl.ds((1 - grp) * n_tx, n_tx)], begin=False, low=0,
        )
        forward.make(0).start()
        return across, forward

    def pass_on(pair):
        across, forward = pair

        for step in (1, 3, 4, 2, 5, 7, 6):
            across.make(step).wait_recv()
            forward.make(step).start()

    def passed_on(pair):
        pair[1].arrive()

    pair_a = final(res_a, part_a, sent_sa, s_recv_a, l_fin_a, v_fin_a, f_a, 3)
    pair_e = final(res_e, part_e, sent_se, s_recv_e, l_fin_e, v_fin_e, f_e, 2)

    padding = v_head_e.shape[0] - vocab
    l_head_a.wait()
    v_head_a[pl.ds(vocab, padding), :] = jnp.zeros((padding, width_a), BF16)
    l_head_e.wait()
    v_head_e[pl.ds(vocab, padding), :] = jnp.zeros((padding, width_e), BF16)

    n_slab = v_head_e.shape[0] // SLAB

    logit_exchanges = [
        Exchange(
            n_ty, None, None, l_ssem.at[slab], l_rsem.at[slab], to_ty, l_recv.at[slab, pl.ds(1, n_ty - 1)], begin=False,
        )
        for slab in range(2 * n_slab)
    ]

    def logits(buffer, half, head, base):
        rows = unfolded(buffer[pl.ds(half * n_tx, n_tx)].astype(F32)).reshape(n_rows, head.shape[1]).astype(BF16)
        side = jnp.where(half == coarse, 0, 4)

        def copy(slab, step):
            target = half * 4 + rings[step]
            return pltpu.make_async_remote_copy(
                src_ref=l_send.at[slab, target], dst_ref=l_recv.at[slab, side + step], send_sem=l_ssem.at[slab],
                recv_sem=l_rsem.at[slab], device_id={"ty": target}, device_id_type=MESH,
            )

        for slab in range(n_slab):
            for at in range(0, SLAB, CHUNK):
                part = mm_t(rows, head[slab * SLAB + at : slab * SLAB + at + CHUNK, :])
                part = part.reshape(4, 16, CHUNK).astype(BF16)
                l_send[base + slab, pl.ds(half * 4, 4), :, at : at + CHUNK] = part
            for step in (2, 1, 3):
                copy(base + slab, step).start()

            @pl.when(half != coarse)
            def _():
                copy(base + slab, 0).start()

    pass_on(pair_a)
    logits(f_a, grp, v_head_a, n_slab)
    pass_on(pair_e)
    passed_on(pair_a)
    logits(f_a, 1 - grp, v_head_a, n_slab)
    logits(f_e, grp, v_head_e, 0)
    passed_on(pair_e)
    logits(f_e, 1 - grp, v_head_e, 0)

    def slab_sum(slab):
        return add_up(logit_exchanges[slab], l_send[slab, ty].astype(F32), l_recv.at[slab])

    lane_c = iota((16, SLAB), 1)

    def peak_and_total(part, c):
        masked = jnp.where(lane_c + c * SLAB < vocab, part, -jnp.inf)
        peak = jnp.max(masked, axis=1, keepdims=True)
        return peak, jnp.sum(jnp.exp(masked - peak), axis=1, keepdims=True)

    def merged(pairs):
        peak = functools.reduce(jnp.maximum, [peak for peak, _ in pairs])
        return peak, functools.reduce(jnp.add, [total * jnp.exp(own - peak) for own, total in pairs])

    l_tokens.wait()
    row16 = iota((16, HEAD), 0)
    token = jnp.zeros((16, HEAD), jnp.int32)
    for s in range(2):
        for r in range(8):
            token = jnp.where(row16 == r // block * 8 + s * block + r % block, tokens[s, r], token)
    token = widen(token - flat * vocab, SLAB)

    drain(2 * n_slab)
    amateur = [slab_sum(n_slab + c) for c in range(n_slab)]
    peak_a, total_a = merged([peak_and_total(amateur[c], c) for c in range(n_slab)])
    chosen = jnp.zeros((16, SLAB), F32)
    mixed, pairs = [], []
    for c in range(n_slab):
        expert = slab_sum(c)
        pairs.append(peak_and_total(expert, c))
        mixed.append(expert - AMATEUR * amateur[c])
        column = lane_c + c * SLAB
        chosen = chosen + jnp.where((column == token) & (column < vocab), mixed[c], 0.0)
    peak_e, total_e = merged(pairs)
    chosen = jnp.sum(chosen, axis=1, keepdims=True)

    lane16 = iota((16, HEAD), 1) % 64
    tile = jnp.where(lane16 == 0, peak_e, jnp.where(lane16 == 1, total_e, 0.0))
    tile = jnp.where(lane16 == 2, peak_a, jnp.where(lane16 == 3, total_a, tile))
    tile = jnp.where(lane16 == 4, chosen, tile)
    tile = jnp.where(lane8 < 64, tile[:8], tile[8:])
    t_send[...] = tile
    stats = Exchange(n_flat, lambda d: t_send, lambda d: t_recv.at[d], t_ssem.at[0], t_rsem.at[0], flat_peer,
             t_recv.at[pl.ds(1, n_flat - 1)])
    drain(1)
    stats.arrive()
    tiles = [tile] + [t_recv[step] for step in range(1, n_flat)]
    highest = functools.reduce(jnp.maximum, tiles)
    picked = functools.reduce(jnp.add, tiles)

    def shifted(values):
        return jnp.concatenate([values[:, 1:], values[:, :1]], axis=1)

    summed_up = functools.reduce(jnp.add, [jnp.exp(t - highest) * shifted(t) for t in tiles])
    log_total = highest + jnp.log(summed_up)

    def column(values, lane):
        return jnp.concatenate([values[:, lane : lane + 1], values[:, lane + 64 : lane + 65]], axis=0)

    offset = column(log_total, 0) - AMATEUR * column(log_total, 2)
    for c in range(n_slab):
        size = min(SLAB, vocab - c * SLAB)
        contrast = mixed[c] - offset
        for s in range(2):
            low = s * block
            out_ref[s, :, c * SLAB : c * SLAB + size] = jnp.concatenate(
                [contrast[low : low + block], contrast[8 + low : 8 + low + block]], axis=0
            )[:, :size]
    value = jnp.broadcast_to(column(picked, 4) - offset, (16, HEAD))
    lane_r = iota((16, HEAD), 1)
    for s in range(2):
        mine = row16 == lane_r // block * 8 + s * block + lane_r % block
        line = jnp.sum(jnp.where(mine & (lane_r < 8), value, 0.0), axis=0, keepdims=True)
        score_ref[s : s + 1, :] = line[:, :8]

    drain(0)


def on_device(axes, *args):
    (
        hid_e, gain_e, wq_e, wk_e, wv_e, wo_e, fin_e, head_e, kc_e, vc_e,
        hid_a, gain_a, wq_a, wk_a, wv_a, wo_a, fin_a, head_a, kc_a, vc_a,
        lengths, tokens,
    ) = args
    n_grp, n_tx, n_ty = axes
    n_flat = n_grp * n_tx
    half = hid_e.shape[1] // n_grp
    vocab = head_e.shape[0]
    padded = -(-vocab // SLAB) * SLAB
    n_slab = padded // SLAB
    n_rows = 2 * half
    width_e, width_a = hid_e.shape[2], hid_a.shape[2]
    cols_e = wq_e.shape[1] + wk_e.shape[1] + wv_e.shape[1]
    cols_a = wq_a.shape[1] + wk_a.shape[1] + wv_a.shape[1]
    inner_e, inner_a = wo_e.shape[0], wo_a.shape[0]

    def like(array):
        return pltpu.VMEM(array.shape, array.dtype)

    scratch = [
        pltpu.SMEM(lengths.shape, jnp.int32), pltpu.SMEM(tokens.shape, jnp.int32),
        like(gain_e), like(fin_e), like(gain_a), like(fin_a),
    ]
    for hid, wq, wk, wv, wo, head, kc, vc in (
        (hid_e, wq_e, wk_e, wv_e, wo_e, head_e, kc_e, vc_e),
        (hid_a, wq_a, wk_a, wv_a, wo_a, head_a, kc_a, vc_a),
    ):
        scratch += [
            pltpu.VMEM((2, half, hid.shape[2]), BF16), like(wq), like(wk), like(wv), like(wo),
            pltpu.VMEM((padded, head.shape[1]), BF16), like(kc), like(vc),
        ]
    scratch += [
        pltpu.VMEM((n_ty, 8, width_e), F32), pltpu.VMEM((n_ty, 8, width_a), F32),
        pltpu.VMEM((8, HEAD), F32), pltpu.VMEM((n_ty, 8, HEAD), F32),
        pltpu.VMEM((n_ty, 8, cols_e), F32), pltpu.VMEM((n_ty, 8, cols_e), F32),
        pltpu.VMEM((n_ty, 16, cols_a // 2), BF16), pltpu.VMEM((n_ty, 16, cols_a // 2), BF16),
        pltpu.VMEM((n_ty, 16, inner_e // 2), BF16), pltpu.VMEM((n_ty, 16, inner_a // 2), BF16),
        pltpu.VMEM((n_tx, 16, width_e // 2), BF16), pltpu.VMEM((n_tx, 16, width_e // 2), BF16),
        pltpu.VMEM((n_tx, 16, width_a // 2), BF16), pltpu.VMEM((n_tx, 16, width_a // 2), BF16),
        pltpu.VMEM((8, HEAD), F32), pltpu.VMEM((n_ty, 8, HEAD), F32),
        pltpu.VMEM((8, HEAD), F32), pltpu.VMEM((n_ty, 8, HEAD), F32),
        pltpu.VMEM((n_flat, 16, width_e // 2), BF16), pltpu.VMEM((n_flat, 16, width_a // 2), BF16),
        pltpu.VMEM((2 * n_slab, n_ty, 16, SLAB), BF16), pltpu.VMEM((2 * n_slab, n_ty, 16, SLAB), BF16),
        pltpu.VMEM((8, HEAD), F32), pltpu.VMEM((n_flat, 8, HEAD), F32),
        pltpu.SemaphoreType.DMA((22,)),
        pltpu.SemaphoreType.DMA((7,)), pltpu.SemaphoreType.DMA((7,)),
        pltpu.SemaphoreType.DMA((4,)), pltpu.SemaphoreType.DMA((4, n_tx)),
        pltpu.SemaphoreType.DMA((2,)), pltpu.SemaphoreType.DMA((2,)),
        pltpu.SemaphoreType.DMA((2 * n_slab,)), pltpu.SemaphoreType.DMA((2 * n_slab,)),
        pltpu.SemaphoreType.DMA((1,)), pltpu.SemaphoreType.DMA((1,)),
    ]
    hbm = pl.BlockSpec(memory_space=pl.ANY)
    vmem = pl.BlockSpec(memory_space=pltpu.VMEM)
    macs = n_rows * (width_e * (cols_e + inner_e) + width_a * (cols_a + inner_a)) + 2 * n_rows * vocab * (width_e + width_a)
    read = sum(array.size * array.dtype.itemsize for array in args)
    return pl.pallas_call(
        functools.partial(kernel, axes, None),
        out_shape=(
            pltpu.VMEM((2, hid_e.shape[1] // n_ty, vocab), F32),
            pltpu.VMEM((2, hid_e.shape[1] // n_ty), F32),
        ),
        in_specs=[hbm] * len(args),
        out_specs=(vmem, vmem),
        scratch_shapes=scratch,
        compiler_params=pltpu.CompilerParams(
            collective_id=0, has_side_effects=True, vmem_limit_bytes=56 * 1024 * 1024
        ),
        cost_estimate=pl.CostEstimate(flops=2 * macs, bytes_accessed=read, transcendentals=0),
        name="contrast",
    )(*args)


def solution(mesh):
    model = (
        P(None, None, "ty"), P("ty"), P("ty", "tx"), P("ty", "tx"), P("ty", "tx"), P("tx", "ty"), P("ty"),
        P(("grp", "tx"), "ty"), P(("grp", "ty"), None, "tx"), P(("grp", "ty"), None, "tx"),
    )
    axes = tuple(mesh.shape[name] for name in ("grp", "tx", "ty"))
    return jax.shard_map(
        functools.partial(on_device, axes),
        mesh=mesh,
        in_specs=model + model + (P(("grp", "ty")), P(None, "ty")),
        out_specs=(P(None, "ty", ("grp", "tx")), P(None, "ty")),
        check_vma=False,
    )
```

```python
import functools
import math

import jax
import jax.numpy as jnp
from jax import lax
from jax.experimental import pallas as pl
from jax.experimental.pallas import tpu as pltpu
from jax.sharding import PartitionSpec as P

HEAD = 128
EPS = 1e-05
BASE = 10000.0
AMATEUR = 0.5
SCALE = HEAD**-0.5
CHUNK = 512
SLAB = 1024
F32 = jnp.float32
BF16 = jnp.bfloat16
MESH = pl.DeviceIdType.MESH


def iota(shape, axis):
    return lax.broadcasted_iota(jnp.int32, shape, axis)


def mm(a, b):
    return lax.dot_general(a, b, (((1,), (0,)), ((), ())), preferred_element_type=F32)


def mm_t(a, b):
    return lax.dot_general(a, b, (((1,), (1,)), ((), ())), preferred_element_type=F32)


def one_hot(size, source):
    out = iota((size, size), 0)
    return jnp.where(iota((size, size), 1) == source(out), 1.0, 0.0).astype(BF16)


def folded(values):
    half = values.shape[-1] // 2
    return jnp.concatenate([values[..., :half], values[..., half:]], axis=-2)


def unfolded(values):
    return jnp.concatenate([values[..., :8, :], values[..., 8:, :]], axis=-1)


def packed(values, ref):
    return values if ref.dtype == F32 else folded(values).astype(ref.dtype)


def lane_fold(values):
    total = values[:, :HEAD]
    for start in range(HEAD, values.shape[1], HEAD):
        total = total + values[:, start : start + HEAD]
    return total


def widen(column, width):
    return jnp.concatenate([column] * (width // HEAD), axis=1)


def kernel(axes, dims, *refs):
    n_grp, n_tx, n_ty = axes
    (
        hid_e, gain_e, wq_e, wk_e, wv_e, wo_e, fin_e, head_e, kc_e, vc_e,
        hid_a, gain_a, wq_a, wk_a, wv_a, wo_a, fin_a, head_a, kc_a, vc_a,
        h_lengths, h_tokens,
        out_ref, score_ref,
        lengths, tokens, v_gain_e, v_fin_e, v_gain_a, v_fin_a,
        v_hid_e, v_wq_e, v_wk_e, v_wv_e, v_wo_e, v_head_e, v_kc_e, v_vc_e,
        v_hid_a, v_wq_a, v_wk_a, v_wv_a, v_wo_a, v_head_a, v_kc_a, v_vc_a,
        x_e, x_a, sq_send, sq_recv,
        p_send_e, p_recv_e, p_send_a, p_recv_a,
        g_e, g_a,
        o_send_e, o_recv_e, o_send_a, o_recv_a,
        s_send_e, s_recv_e, s_send_a, s_recv_a,
        f_e, f_a,
        l_send, l_recv, t_send, t_recv,
        local_sem, ty_send, ty_recv, tx_send, tx_recv, fw_send, fw_recv, l_ssem, l_rsem, t_ssem, t_rsem,
    ) = refs
    grp, tx, ty = lax.axis_index("grp"), lax.axis_index("tx"), lax.axis_index("ty")
    half_rows = v_hid_e.shape[1]
    width_e, width_a = v_hid_e.shape[2], v_hid_a.shape[2]
    heads_e, heads_a = v_wq_e.shape[1] // HEAD, v_wq_a.shape[1] // HEAD
    vocab = head_e.shape[0]

    first = pl.multiple_of(grp * half_rows, half_rows)
    pairs = [
        (hid_e.at[:, pl.ds(first, half_rows)], v_hid_e),
        (hid_a.at[:, pl.ds(first, half_rows)], v_hid_a),
        (h_lengths, lengths), (gain_e, v_gain_e), (gain_a, v_gain_a),
        (fin_e, v_fin_e), (fin_a, v_fin_a), (h_tokens, tokens),
        (wq_a, v_wq_a), (wk_a, v_wk_a), (wv_a, v_wv_a),
        (wq_e, v_wq_e), (wk_e, v_wk_e), (wv_e, v_wv_e),
        (kc_a, v_kc_a), (vc_a, v_vc_a), (kc_e, v_kc_e), (vc_e, v_vc_e),
        (wo_a, v_wo_a), (wo_e, v_wo_e),
        (head_a, v_head_a.at[pl.ds(0, vocab)]), (head_e, v_head_e.at[pl.ds(0, vocab)]),
    ]
    loads = [
        pltpu.make_async_copy(source, target, local_sem.at[number])
        for number, (source, target) in enumerate(pairs)
    ]
    for load in loads[:8]:
        load.start()
    (l_hid_e, l_hid_a, l_lengths, l_gain_e, l_gain_a, l_fin_e, l_fin_a, l_tokens, l_wq_a, l_wk_a, l_wv_a, l_wq_e, l_wk_e, l_wv_e,
     l_kc_a, l_vc_a, l_kc_e, l_vc_e, l_wo_a, l_wo_e, l_head_a, l_head_e) = loads

    coarse, ring = ty // 4, lax.rem(ty, 4)
    tx_coarse, tx_ring = tx // 4, lax.rem(tx, 4)
    rings = [lax.rem(ring + step, 4) for step in range(4)]
    ty_peers = [lax.rem(coarse + step // 4, n_ty // 4) * 4 + rings[step % 4] for step in range(n_ty)]
    tx_rings = [lax.rem(tx_ring + step, 4) for step in range(4)]
    tx_sides = [lax.rem(tx_coarse + step, n_tx // 4) * 4 for step in range(n_tx // 4)]
    tx_peers = [tx_sides[step // 4] + tx_rings[step % 4] for step in range(n_tx)]
    tx_sources = [tx_sides[step // 4] + tx_rings[-step % 4] for step in range(n_tx)]
    flat = grp * n_tx + tx
    n_flat = n_grp * n_tx

    def to_ty(step):
        return {"ty": ty_peers[step]}

    def to_tx(step):
        return {"tx": tx_peers[step]}

    def flat_peer(step):
        return {"grp": lax.rem(grp + step // n_tx, n_grp), "tx": tx_peers[step % n_tx]}

    def near(step):
        return {"tx": tx_sides[step // 4] + tx_ring, "ty": ty_peers[step]}

    barrier = pltpu.get_barrier_semaphore()

    def greet(device):
        pl.semaphore_signal(barrier, inc=1, device_id=device, device_id_type=MESH)

    for step in range(n_ty - 1, 0, -1):
        greet(near(step))
    for step in range(4, n_ty):
        greet(to_ty(step))
    for step in range(n_flat - 1, 0, -1):
        greet(flat_peer(step))

    for load in loads[8:14]:
        load.start()

    started = []

    class Exchange:
        def __init__(self, n, source, target, send_sem, recv_sem, device, bulk, begin=True, each=False, low=1):
            self.n, self.low = n, low
            self.make = lambda step: pltpu.make_async_remote_copy(
                src_ref=source(step), dst_ref=target(step), send_sem=send_sem,
                recv_sem=recv_sem.at[step] if each else recv_sem, device_id=device(step), device_id_type=MESH,
            )
            self.all = lambda: pltpu.make_async_remote_copy(
                src_ref=bulk, dst_ref=bulk, send_sem=send_sem, recv_sem=recv_sem.at[0] if each else recv_sem,
                device_id=device(low), device_id_type=MESH,
            )
            started.append(self)
            if begin:
                self.begin()

        def begin(self):
            for step in range(self.n - 1, 0, -1):
                self.make(step).start()

        def arrive(self):
            self.all().wait_recv()

        def finish(self):
            self.all().wait_send()

    def drain(keep):
        while len(started) > keep:
            started.pop(0).finish()

    def add_up(exchange, total, recv):
        exchange.arrive()
        for step in range(1, exchange.n):
            total = total + recv[step].astype(F32)
        return total

    n_rows = 2 * half_rows
    block = half_rows // n_ty
    order = one_hot(
        n_rows, lambda o: (o // block) % 2 * half_rows + o // (2 * block) * block + o % block
    )
    l_hid_e.wait()
    wide_e = mm(order, v_hid_e[...].reshape(n_rows, width_e))
    x_e[...] = wide_e.reshape(n_ty, 8, width_e)
    l_hid_a.wait()
    wide_a = mm(order, v_hid_a[...].reshape(n_rows, width_a))
    x_a[...] = wide_a.reshape(n_ty, 8, width_a)
    partial = jnp.concatenate([lane_fold(wide_e * wide_e), lane_fold(wide_a * wide_a)], axis=0)
    own = jnp.broadcast_to(jnp.sum(partial.T, axis=0, keepdims=True), (8, HEAD))
    sq_send[...] = own

    pl.semaphore_wait(barrier, n_ty - 1 + n_ty - 4 + n_flat - 1)

    squares = Exchange(n_ty, lambda d: sq_send, lambda d: sq_recv.at[d], ty_send.at[0], ty_recv.at[0], near,
                       sq_recv.at[pl.ds(1, n_ty - 1)])
    for load in loads[14:18]:
        load.start()

    row8, lane8 = iota((8, HEAD), 0), iota((8, HEAD), 1)
    position = jnp.zeros((8, HEAD), jnp.int32)
    l_lengths.wait()
    for i in range(block):
        position = jnp.where(row8 % block == i, lengths[i], position)
    position = (position + row8 // block).astype(F32)
    exponent = (lane8 % (HEAD // 2)).astype(F32) * (2.0 / HEAD)
    angle = position * jnp.exp(exponent * (-math.log(BASE)))
    cosine = jnp.cos(angle)
    sine = jnp.where(lane8 < HEAD // 2, -1.0, 1.0) * jnp.sin(angle)

    def rotated(values):
        turned = jnp.concatenate([values[:, HEAD // 2 :], values[:, : HEAD // 2]], axis=1)
        return values * cosine + turned * sine

    total = add_up(squares, own, sq_recv)
    square = jnp.broadcast_to(total[0:1], (HEAD, HEAD)).T
    root_e = lax.rsqrt(square[:n_rows] / (width_e * n_ty) + EPS)
    root_a = lax.rsqrt(square[n_rows:] / (width_a * n_ty) + EPS)

    def project(x, root, g_load, gain, weights, send, recv, kind):
        width = x.shape[2]
        g_load.wait()
        values = x[...].reshape(n_rows, width)
        normed = (values * widen(root, width) * gain[...].astype(F32).reshape(1, width)).astype(BF16)
        parts = []
        for load, weight in weights:
            load.wait()
            columns = weight.shape[1]
            for at in range(0, columns, CHUNK):
                parts.append(mm(normed, weight[:, at : at + min(CHUNK, columns - at)]))
        send[...] = packed(jnp.concatenate(parts, axis=1).reshape(n_ty, 8, -1), send)
        return Exchange(n_ty, lambda d: send.at[ty_peers[d]], lambda d: recv.at[d], ty_send.at[kind], ty_recv.at[kind], to_ty,
                        recv.at[pl.ds(1, n_ty - 1)])

    sent_pa = project(x_a, root_a, l_gain_a, v_gain_a, ((l_wq_a, v_wq_a), (l_wk_a, v_wk_a), (l_wv_a, v_wv_a)), p_send_a, p_recv_a, 2)
    sent_pe = project(x_e, root_e, l_gain_e, v_gain_e, ((l_wq_e, v_wq_e), (l_wk_e, v_wk_e), (l_wv_e, v_wv_e)), p_send_e, p_recv_e, 1)

    for load in loads[18:]:
        load.start()

    def summed(exchange, send, recv, me):
        total = add_up(exchange, send[me].astype(F32), recv)
        return total if send.dtype == F32 else unfolded(total)

    def padded(rows, size):
        if rows.shape[0] == size:
            return rows
        return jnp.concatenate([rows, jnp.zeros((size - rows.shape[0], rows.shape[1]), F32)], axis=0)

    def attend(acc, heads, key_heads, k_load, keys, v_load, values):
        group = heads // key_heads
        n_query = heads * 8
        per_row = 2 * heads
        cache = keys.shape[1]
        wide = key_heads * HEAD
        query = jnp.concatenate([rotated(acc[:, h * HEAD : (h + 1) * HEAD]) for h in range(heads)], axis=0)
        at = heads * HEAD
        fresh_k = jnp.concatenate(
            [rotated(acc[:, at + h * HEAD : at + (h + 1) * HEAD]) for h in range(key_heads)], axis=0
        )
        at += wide
        fresh_v = jnp.concatenate(
            [acc[:, at + h * HEAD : at + (h + 1) * HEAD] for h in range(key_heads)], axis=0
        )
        fresh_k = padded(fresh_k, HEAD).astype(BF16)
        fresh_v = padded(fresh_v, HEAD).astype(BF16)
        forth = one_hot(n_query, lambda o: o % heads * 8 + o // heads % 2 * block + o // per_row)
        back = one_hot(n_query, lambda o: o % block * per_row + o // block % 2 * heads + o // 8)
        query = mm(forth, query.astype(BF16))
        owner = iota((n_query, HEAD), 0)
        lane = iota((n_query, HEAD), 1)
        fresh = mm_t(query.astype(BF16), fresh_k) * SCALE
        seen = (
            (lane < key_heads * 8)
            & (lane // 8 == owner % heads // group)
            & (lane % block == owner // per_row)
            & (lane // block % 2 <= owner // heads % 2)
        )
        fresh = jnp.where(seen, fresh, -jnp.inf)
        if key_heads > 1:
            spread = widen(query, wide)
            keep = iota((n_query, wide), 1) // HEAD == iota((n_query, wide), 0) % heads // group
            query = jnp.where(keep, spread, 0.0)
        k_load.wait()
        cached = []
        for i in range(block):
            part = query[i * per_row : (i + 1) * per_row].astype(BF16)
            score = mm_t(part, keys[i]) * SCALE
            cached.append(jnp.where(iota((per_row, cache), 1) < lengths[i], score, -jnp.inf))
        cached = jnp.concatenate(cached, axis=0)
        peak = jnp.maximum(jnp.max(cached, axis=1, keepdims=True), jnp.max(fresh, axis=1, keepdims=True))
        cached = jnp.exp(cached - peak)
        fresh = jnp.exp(fresh - peak)
        total = jnp.sum(cached, axis=1, keepdims=True) + jnp.sum(fresh, axis=1, keepdims=True)
        v_load.wait()
        mixture = jnp.concatenate(
            [mm(cached[i * per_row : (i + 1) * per_row].astype(BF16), values[i]) for i in range(block)], axis=0
        )
        if key_heads > 1:
            picked = jnp.zeros((n_query, HEAD), F32)
            for h in range(key_heads):
                picked = picked + jnp.where(owner % heads // group == h, mixture[:, h * HEAD : (h + 1) * HEAD], 0.0)
            mixture = picked
        mixture = mixture + mm(fresh.astype(BF16), fresh_v)
        ready = mm(back, (mixture / total).astype(BF16))
        return jnp.concatenate([ready[h * 8 : (h + 1) * 8] for h in range(heads)], axis=1)

    def gather(rows, buffer, kind):
        buffer[ty] = folded(rows).astype(BF16)
        return Exchange(n_ty, lambda d: buffer.at[ty], lambda d: buffer.at[ty], ty_send.at[kind], ty_recv.at[kind], to_ty,
                        buffer.at[pl.ds(0, n_ty - 1)])

    acc = summed(sent_pa, p_send_a, p_recv_a, ty)
    sent_ga = gather(attend(acc, heads_a, v_wk_a.shape[1] // HEAD, l_kc_a, v_kc_a, l_vc_a, v_vc_a), g_a, 4)

    def output(exchange, buffer, load, weight, send, recv, kind):
        exchange.arrive()
        rows = unfolded(buffer[...].astype(F32)).reshape(n_rows, weight.shape[0]).astype(BF16)
        load.wait()
        columns = weight.shape[1]
        parts = [mm(rows, weight[:, at : at + CHUNK]) for at in range(0, columns, CHUNK)]
        send[...] = packed(jnp.concatenate(parts, axis=1).reshape(n_tx, 8, columns), send)
        return Exchange(n_tx, lambda d: send.at[tx_peers[d]], lambda d: recv.at[d], tx_send.at[kind], tx_recv.at[kind, 0], to_tx,
                        recv.at[pl.ds(1, n_tx - 1)])


    def residual(exchange, x, send, recv, s_send, s_recv, kind):
        values = x[tx] + summed(exchange, send, recv, tx)
        part = lane_fold(values * values)
        s_send[...] = part
        return values, part, Exchange(
            n_ty, lambda d: s_send, lambda d: s_recv.at[d], ty_send.at[kind], ty_recv.at[kind], to_ty,
            s_recv.at[pl.ds(1, n_ty - 1)],
        )


    def final(values, part, exchange, s_recv, g_load, gain, buffer, kind):
        width = values.shape[1]
        g_load.wait()
        part = add_up(exchange, part, s_recv)
        mean = jnp.sum(part, axis=1, keepdims=True) / (width * n_ty)
        rows = values * lax.rsqrt(mean + EPS) * gain[...].astype(F32).reshape(1, width)
        buffer[flat] = folded(rows).astype(BF16)
        across = Exchange(
            n_tx, lambda d: buffer.at[flat], lambda d: buffer.at[flat], tx_send.at[kind], tx_recv.at[kind], to_tx,
            buffer.at[pl.ds(0, n_tx - 1)], each=True,
        )

        def from_tx(step):
            return grp * n_tx + tx_sources[step]

        forward = Exchange(
            n_tx, lambda d: buffer.at[from_tx(d)], lambda d: buffer.at[from_tx(d)], fw_send.at[kind - 2],
            fw_recv.at[kind - 2], lambda d: {"grp": 1 - grp}, buffer.at[pl.ds((1 - grp) * n_tx, n_tx)], begin=False, low=0,
        )
        forward.make(0).start()
        return across, forward

    def pass_on(pair):
        across, forward = pair

        for step in (1, 3, 4, 2, 5, 7, 6):
            across.make(step).wait_recv()
            forward.make(step).start()

    def passed_on(pair):
        pair[1].arrive()


    sent_oa = output(sent_ga, g_a, l_wo_a, v_wo_a, o_send_a, o_recv_a, 1)
    acc = summed(sent_pe, p_send_e, p_recv_e, ty)
    sent_ge = gather(attend(acc, heads_e, v_wk_e.shape[1] // HEAD, l_kc_e, v_kc_e, l_vc_e, v_vc_e), g_e, 3)
    drain(2)
    res_a, part_a, sent_sa = residual(sent_oa, x_a, o_send_a, o_recv_a, s_send_a, s_recv_a, 6)
    sent_oe = output(sent_ge, g_e, l_wo_e, v_wo_e, o_send_e, o_recv_e, 0)
    drain(2)
    padding = v_head_e.shape[0] - vocab
    l_head_a.wait()
    v_head_a[pl.ds(vocab, padding), :] = jnp.zeros((padding, width_a), BF16)
    l_head_e.wait()
    v_head_e[pl.ds(vocab, padding), :] = jnp.zeros((padding, width_e), BF16)
    pair_a = final(res_a, part_a, sent_sa, s_recv_a, l_fin_a, v_fin_a, f_a, 3)
    res_e, part_e, sent_se = residual(sent_oe, x_e, o_send_e, o_recv_e, s_send_e, s_recv_e, 5)

    n_slab = v_head_e.shape[0] // SLAB

    def logits(buffer, half, head, base):
        rows = unfolded(buffer[pl.ds(half * n_tx, n_tx)].astype(F32)).reshape(n_rows, head.shape[1]).astype(BF16)
        side = jnp.where(half == coarse, 0, 4)

        def copy(slab, step):
            target = half * 4 + rings[step]
            return pltpu.make_async_remote_copy(
                src_ref=l_send.at[slab, target], dst_ref=l_recv.at[slab, side + step], send_sem=l_ssem.at[slab],
                recv_sem=l_rsem.at[slab], device_id={"ty": target}, device_id_type=MESH,
            )

        for slab in range(n_slab):
            for at in range(0, SLAB, CHUNK):
                part = mm_t(rows, head[slab * SLAB + at : slab * SLAB + at + CHUNK, :])
                part = part.reshape(4, 16, CHUNK).astype(BF16)
                l_send[base + slab, pl.ds(half * 4, 4), :, at : at + CHUNK] = part
            for step in (2, 1, 3):
                copy(base + slab, step).start()

            @pl.when(half != coarse)
            def _():
                copy(base + slab, 0).start()

    pass_on(pair_a)
    logits(f_a, grp, v_head_a, n_slab)
    pair_e = final(res_e, part_e, sent_se, s_recv_e, l_fin_e, v_fin_e, f_e, 2)
    passed_on(pair_a)
    logits(f_a, 1 - grp, v_head_a, n_slab)
    pass_on(pair_e)
    logits(f_e, grp, v_head_e, 0)
    passed_on(pair_e)
    logits(f_e, 1 - grp, v_head_e, 0)

    logit_exchanges = [
        Exchange(
            n_ty, None, None, l_ssem.at[slab], l_rsem.at[slab], to_ty, l_recv.at[slab, pl.ds(1, n_ty - 1)], begin=False,
        )
        for slab in range(2 * n_slab)
    ]

    def slab_sum(slab):
        return add_up(logit_exchanges[slab], l_send[slab, ty].astype(F32), l_recv.at[slab])

    lane_c = iota((16, SLAB), 1)

    def peak_and_total(parts):
        masked = [jnp.where(lane_c + c * SLAB < vocab, part, -jnp.inf) for c, part in enumerate(parts)]
        peak = masked[0]
        for part in masked[1:]:
            peak = jnp.maximum(peak, part)
        peak = jnp.max(peak, axis=1, keepdims=True)
        total = jnp.exp(masked[0] - peak)
        for part in masked[1:]:
            total = total + jnp.exp(part - peak)
        return peak, jnp.sum(total, axis=1, keepdims=True)

    l_tokens.wait()
    row16 = iota((16, HEAD), 0)
    token = jnp.zeros((16, HEAD), jnp.int32)
    for s in range(2):
        for r in range(8):
            token = jnp.where(row16 == r // block * 8 + s * block + r % block, tokens[s, r], token)
    token = widen(token - flat * vocab, SLAB)

    drain(2 * n_slab)
    amateur = [slab_sum(n_slab + c) for c in range(n_slab)]
    peak_a, total_a = peak_and_total(amateur)
    expert = [slab_sum(c) for c in range(n_slab)]
    peak_e, total_e = peak_and_total(expert)
    chosen = jnp.zeros((16, SLAB), F32)
    mixed = []
    for c in range(n_slab):
        mixed.append(expert[c] - AMATEUR * amateur[c])
        column = lane_c + c * SLAB
        chosen = chosen + jnp.where((column == token) & (column < vocab), mixed[c], 0.0)
    chosen = jnp.sum(chosen, axis=1, keepdims=True)

    lane16 = iota((16, HEAD), 1) % 64
    tile = jnp.where(lane16 == 0, peak_e, jnp.where(lane16 == 1, total_e, 0.0))
    tile = jnp.where(lane16 == 2, peak_a, jnp.where(lane16 == 3, total_a, tile))
    tile = jnp.where(lane16 == 4, chosen, tile)
    tile = jnp.where(lane8 < 64, tile[:8], tile[8:])
    t_send[...] = tile
    stats = Exchange(n_flat, lambda d: t_send, lambda d: t_recv.at[d], t_ssem.at[0], t_rsem.at[0], flat_peer,
             t_recv.at[pl.ds(1, n_flat - 1)])
    drain(1)
    stats.arrive()
    tiles = [tile] + [t_recv[step] for step in range(1, n_flat)]
    highest = functools.reduce(jnp.maximum, tiles)
    picked = functools.reduce(jnp.add, tiles)

    def shifted(values):
        return jnp.concatenate([values[:, 1:], values[:, :1]], axis=1)

    summed_up = functools.reduce(jnp.add, [jnp.exp(t - highest) * shifted(t) for t in tiles])
    log_total = highest + jnp.log(summed_up)

    def column(values, lane):
        return jnp.concatenate([values[:, lane : lane + 1], values[:, lane + 64 : lane + 65]], axis=0)

    offset = column(log_total, 0) - AMATEUR * column(log_total, 2)
    for c in range(n_slab):
        size = min(SLAB, vocab - c * SLAB)
        contrast = mixed[c] - offset
        for s in range(2):
            low = s * block
            out_ref[s, :, c * SLAB : c * SLAB + size] = jnp.concatenate(
                [contrast[low : low + block], contrast[8 + low : 8 + low + block]], axis=0
            )[:, :size]
    value = jnp.broadcast_to(column(picked, 4) - offset, (16, HEAD))
    lane_r = iota((16, HEAD), 1)
    for s in range(2):
        mine = row16 == lane_r // block * 8 + s * block + lane_r % block
        line = jnp.sum(jnp.where(mine & (lane_r < 8), value, 0.0), axis=0, keepdims=True)
        score_ref[s : s + 1, :] = line[:, :8]

    drain(0)


def on_device(axes, *args):
    (
        hid_e, gain_e, wq_e, wk_e, wv_e, wo_e, fin_e, head_e, kc_e, vc_e,
        hid_a, gain_a, wq_a, wk_a, wv_a, wo_a, fin_a, head_a, kc_a, vc_a,
        lengths, tokens,
    ) = args
    n_grp, n_tx, n_ty = axes
    n_flat = n_grp * n_tx
    half = hid_e.shape[1] // n_grp
    vocab = head_e.shape[0]
    padded = -(-vocab // SLAB) * SLAB
    n_slab = padded // SLAB
    n_rows = 2 * half
    width_e, width_a = hid_e.shape[2], hid_a.shape[2]
    cols_e = wq_e.shape[1] + wk_e.shape[1] + wv_e.shape[1]
    cols_a = wq_a.shape[1] + wk_a.shape[1] + wv_a.shape[1]
    inner_e, inner_a = wo_e.shape[0], wo_a.shape[0]

    def like(array):
        return pltpu.VMEM(array.shape, array.dtype)

    scratch = [
        pltpu.SMEM(lengths.shape, jnp.int32), pltpu.SMEM(tokens.shape, jnp.int32),
        like(gain_e), like(fin_e), like(gain_a), like(fin_a),
    ]
    for hid, wq, wk, wv, wo, head, kc, vc in (
        (hid_e, wq_e, wk_e, wv_e, wo_e, head_e, kc_e, vc_e),
        (hid_a, wq_a, wk_a, wv_a, wo_a, head_a, kc_a, vc_a),
    ):
        scratch += [
            pltpu.VMEM((2, half, hid.shape[2]), BF16), like(wq), like(wk), like(wv), like(wo),
            pltpu.VMEM((padded, head.shape[1]), BF16), like(kc), like(vc),
        ]
    scratch += [
        pltpu.VMEM((n_ty, 8, width_e), F32), pltpu.VMEM((n_ty, 8, width_a), F32),
        pltpu.VMEM((8, HEAD), F32), pltpu.VMEM((n_ty, 8, HEAD), F32),
        pltpu.VMEM((n_ty, 8, cols_e), F32), pltpu.VMEM((n_ty, 8, cols_e), F32),
        pltpu.VMEM((n_ty, 16, cols_a // 2), BF16), pltpu.VMEM((n_ty, 16, cols_a // 2), BF16),
        pltpu.VMEM((n_ty, 16, inner_e // 2), BF16), pltpu.VMEM((n_ty, 16, inner_a // 2), BF16),
        pltpu.VMEM((n_tx, 16, width_e // 2), BF16), pltpu.VMEM((n_tx, 16, width_e // 2), BF16),
        pltpu.VMEM((n_tx, 16, width_a // 2), BF16), pltpu.VMEM((n_tx, 16, width_a // 2), BF16),
        pltpu.VMEM((8, HEAD), F32), pltpu.VMEM((n_ty, 8, HEAD), F32),
        pltpu.VMEM((8, HEAD), F32), pltpu.VMEM((n_ty, 8, HEAD), F32),
        pltpu.VMEM((n_flat, 16, width_e // 2), BF16), pltpu.VMEM((n_flat, 16, width_a // 2), BF16),
        pltpu.VMEM((2 * n_slab, n_ty, 16, SLAB), BF16), pltpu.VMEM((2 * n_slab, n_ty, 16, SLAB), BF16),
        pltpu.VMEM((8, HEAD), F32), pltpu.VMEM((n_flat, 8, HEAD), F32),
        pltpu.SemaphoreType.DMA((22,)),
        pltpu.SemaphoreType.DMA((7,)), pltpu.SemaphoreType.DMA((7,)),
        pltpu.SemaphoreType.DMA((4,)), pltpu.SemaphoreType.DMA((4, n_tx)),
        pltpu.SemaphoreType.DMA((2,)), pltpu.SemaphoreType.DMA((2,)),
        pltpu.SemaphoreType.DMA((2 * n_slab,)), pltpu.SemaphoreType.DMA((2 * n_slab,)),
        pltpu.SemaphoreType.DMA((1,)), pltpu.SemaphoreType.DMA((1,)),
    ]
    hbm = pl.BlockSpec(memory_space=pl.ANY)
    vmem = pl.BlockSpec(memory_space=pltpu.VMEM)
    macs = n_rows * (width_e * (cols_e + inner_e) + width_a * (cols_a + inner_a)) + 2 * n_rows * vocab * (width_e + width_a)
    read = sum(array.size * array.dtype.itemsize for array in args)
    return pl.pallas_call(
        functools.partial(kernel, axes, None),
        out_shape=(
            pltpu.VMEM((2, hid_e.shape[1] // n_ty, vocab), F32),
            pltpu.VMEM((2, hid_e.shape[1] // n_ty), F32),
        ),
        in_specs=[hbm] * len(args),
        out_specs=(vmem, vmem),
        scratch_shapes=scratch,
        compiler_params=pltpu.CompilerParams(
            collective_id=0, has_side_effects=True, vmem_limit_bytes=56 * 1024 * 1024
        ),
        cost_estimate=pl.CostEstimate(flops=2 * macs, bytes_accessed=read, transcendentals=0),
        name="contrast",
    )(*args)


def solution(mesh):
    model = (
        P(None, None, "ty"), P("ty"), P("ty", "tx"), P("ty", "tx"), P("ty", "tx"), P("tx", "ty"), P("ty"),
        P(("grp", "tx"), "ty"), P(("grp", "ty"), None, "tx"), P(("grp", "ty"), None, "tx"),
    )
    axes = tuple(mesh.shape[name] for name in ("grp", "tx", "ty"))
    return jax.shard_map(
        functools.partial(on_device, axes),
        mesh=mesh,
        in_specs=model + model + (P(("grp", "ty")), P(None, "ty")),
        out_specs=(P(None, "ty", ("grp", "tx")), P(None, "ty")),
        check_vma=False,
    )
```

```python
import functools
import math

import jax
import jax.numpy as jnp
from jax import lax
from jax.experimental import pallas as pl
from jax.experimental.pallas import tpu as pltpu
from jax.sharding import PartitionSpec as P

HEAD = 128
EPS = 1e-05
BASE = 10000.0
AMATEUR = 0.5
SCALE = HEAD**-0.5
CHUNK = 512
SLAB = 1024
F32 = jnp.float32
BF16 = jnp.bfloat16
MESH = pl.DeviceIdType.MESH


def iota(shape, axis):
    return lax.broadcasted_iota(jnp.int32, shape, axis)


def mm(a, b):
    return lax.dot_general(a, b, (((1,), (0,)), ((), ())), preferred_element_type=F32)


def mm_t(a, b):
    return lax.dot_general(a, b, (((1,), (1,)), ((), ())), preferred_element_type=F32)


def one_hot(size, source):
    out = iota((size, size), 0)
    return jnp.where(iota((size, size), 1) == source(out), 1.0, 0.0).astype(BF16)


def folded(values):
    half = values.shape[-1] // 2
    return jnp.concatenate([values[..., :half], values[..., half:]], axis=-2)


def unfolded(values):
    return jnp.concatenate([values[..., :8, :], values[..., 8:, :]], axis=-1)


def packed(values, ref):
    return values if ref.dtype == F32 else folded(values).astype(ref.dtype)


def lane_fold(values):
    total = values[:, :HEAD]
    for start in range(HEAD, values.shape[1], HEAD):
        total = total + values[:, start : start + HEAD]
    return total


def widen(column, width):
    return jnp.concatenate([column] * (width // HEAD), axis=1)


def kernel(axes, dims, *refs):
    n_grp, n_tx, n_ty = axes
    (
        hid_e, gain_e, wq_e, wk_e, wv_e, wo_e, fin_e, head_e, kc_e, vc_e,
        hid_a, gain_a, wq_a, wk_a, wv_a, wo_a, fin_a, head_a, kc_a, vc_a,
        h_lengths, h_tokens,
        out_ref, score_ref,
        lengths, tokens, v_gain_e, v_fin_e, v_gain_a, v_fin_a,
        v_hid_e, v_wq_e, v_wk_e, v_wv_e, v_wo_e, v_head_e, v_kc_e, v_vc_e,
        v_hid_a, v_wq_a, v_wk_a, v_wv_a, v_wo_a, v_head_a, v_kc_a, v_vc_a,
        x_e, x_a, sq_send, sq_recv,
        p_send_e, p_recv_e, p_send_a, p_recv_a,
        g_e, g_a,
        o_send_e, o_recv_e, o_send_a, o_recv_a,
        s_send_e, s_recv_e, s_send_a, s_recv_a,
        f_e, f_a,
        l_send, l_recv, t_send, t_recv,
        local_sem, ty_send, ty_recv, tx_send, tx_recv, fw_send, fw_recv, l_ssem, l_rsem, t_ssem, t_rsem,
    ) = refs
    grp, tx, ty = lax.axis_index("grp"), lax.axis_index("tx"), lax.axis_index("ty")
    half_rows = v_hid_e.shape[1]
    width_e, width_a = v_hid_e.shape[2], v_hid_a.shape[2]
    heads_e, heads_a = v_wq_e.shape[1] // HEAD, v_wq_a.shape[1] // HEAD
    vocab = head_e.shape[0]

    first = pl.multiple_of(grp * half_rows, half_rows)
    pairs = [
        (hid_e.at[:, pl.ds(first, half_rows)], v_hid_e),
        (hid_a.at[:, pl.ds(first, half_rows)], v_hid_a),
        (h_lengths, lengths), (gain_e, v_gain_e), (gain_a, v_gain_a),
        (fin_e, v_fin_e), (fin_a, v_fin_a), (h_tokens, tokens),
        (wq_e, v_wq_e), (wk_e, v_wk_e), (wv_e, v_wv_e),
        (wq_a, v_wq_a), (wk_a, v_wk_a), (wv_a, v_wv_a),
        (kc_e, v_kc_e), (vc_e, v_vc_e), (kc_a, v_kc_a), (vc_a, v_vc_a),
        (wo_e, v_wo_e), (wo_a, v_wo_a),
        (head_e, v_head_e.at[pl.ds(0, vocab)]), (head_a, v_head_a.at[pl.ds(0, vocab)]),
    ]
    loads = [
        pltpu.make_async_copy(source, target, local_sem.at[number])
        for number, (source, target) in enumerate(pairs)
    ]
    for load in loads[:8]:
        load.start()
    (l_hid_e, l_hid_a, l_lengths, l_gain_e, l_gain_a, l_fin_e, l_fin_a, l_tokens, l_wq_e, l_wk_e, l_wv_e, l_wq_a, l_wk_a, l_wv_a,
     l_kc_e, l_vc_e, l_kc_a, l_vc_a, l_wo_e, l_wo_a, l_head_e, l_head_a) = loads

    coarse, ring = ty // 4, lax.rem(ty, 4)
    tx_coarse, tx_ring = tx // 4, lax.rem(tx, 4)
    rings = [lax.rem(ring + step, 4) for step in range(4)]
    ty_peers = [lax.rem(coarse + step // 4, n_ty // 4) * 4 + rings[step % 4] for step in range(n_ty)]
    tx_rings = [lax.rem(tx_ring + step, 4) for step in range(4)]
    tx_sides = [lax.rem(tx_coarse + step, n_tx // 4) * 4 for step in range(n_tx // 4)]
    tx_peers = [tx_sides[step // 4] + tx_rings[step % 4] for step in range(n_tx)]
    tx_sources = [tx_sides[step // 4] + tx_rings[-step % 4] for step in range(n_tx)]
    flat = grp * n_tx + tx
    n_flat = n_grp * n_tx

    def to_ty(step):
        return {"ty": ty_peers[step]}

    def to_tx(step):
        return {"tx": tx_peers[step]}

    def flat_peer(step):
        return {"grp": lax.rem(grp + step // n_tx, n_grp), "tx": tx_peers[step % n_tx]}

    def near(step):
        return {"tx": tx_sides[step // 4] + tx_ring, "ty": ty_peers[step]}

    barrier = pltpu.get_barrier_semaphore()

    def greet(device):
        pl.semaphore_signal(barrier, inc=1, device_id=device, device_id_type=MESH)

    for step in range(n_ty - 1, 0, -1):
        greet(near(step))
    for step in range(4, n_ty):
        greet(to_ty(step))
    for step in range(n_flat - 1, 0, -1):
        greet(flat_peer(step))

    for load in loads[8:14]:
        load.start()

    started = []

    class Exchange:
        def __init__(self, n, source, target, send_sem, recv_sem, device, bulk, begin=True, each=False, low=1):
            self.n, self.low = n, low
            self.make = lambda step: pltpu.make_async_remote_copy(
                src_ref=source(step), dst_ref=target(step), send_sem=send_sem,
                recv_sem=recv_sem.at[step] if each else recv_sem, device_id=device(step), device_id_type=MESH,
            )
            self.all = lambda: pltpu.make_async_remote_copy(
                src_ref=bulk, dst_ref=bulk, send_sem=send_sem, recv_sem=recv_sem.at[0] if each else recv_sem,
                device_id=device(low), device_id_type=MESH,
            )
            started.append(self)
            if begin:
                self.begin()

        def begin(self):
            for step in range(self.n - 1, 0, -1):
                self.make(step).start()

        def arrive(self):
            self.all().wait_recv()

        def finish(self):
            self.all().wait_send()

    def drain(keep):
        while len(started) > keep:
            started.pop(0).finish()

    def add_up(exchange, total, recv):
        exchange.arrive()
        for step in range(1, exchange.n):
            total = total + recv[step].astype(F32)
        return total

    n_rows = 2 * half_rows
    block = half_rows // n_ty
    order = one_hot(
        n_rows, lambda o: (o // block) % 2 * half_rows + o // (2 * block) * block + o % block
    )
    l_hid_e.wait()
    wide_e = mm(order, v_hid_e[...].reshape(n_rows, width_e))
    x_e[...] = wide_e.reshape(n_ty, 8, width_e)
    l_hid_a.wait()
    wide_a = mm(order, v_hid_a[...].reshape(n_rows, width_a))
    x_a[...] = wide_a.reshape(n_ty, 8, width_a)
    partial = jnp.concatenate([lane_fold(wide_e * wide_e), lane_fold(wide_a * wide_a)], axis=0)
    own = jnp.broadcast_to(jnp.sum(partial.T, axis=0, keepdims=True), (8, HEAD))
    sq_send[...] = own

    pl.semaphore_wait(barrier, n_ty - 1 + n_ty - 4 + n_flat - 1)

    squares = Exchange(n_ty, lambda d: sq_send, lambda d: sq_recv.at[d], ty_send.at[0], ty_recv.at[0], near,
                       sq_recv.at[pl.ds(1, n_ty - 1)])
    for load in loads[14:18]:
        load.start()

    row8, lane8 = iota((8, HEAD), 0), iota((8, HEAD), 1)
    position = jnp.zeros((8, HEAD), jnp.int32)
    l_lengths.wait()
    for i in range(block):
        position = jnp.where(row8 % block == i, lengths[i], position)
    position = (position + row8 // block).astype(F32)
    exponent = (lane8 % (HEAD // 2)).astype(F32) * (2.0 / HEAD)
    angle = position * jnp.exp(exponent * (-math.log(BASE)))
    cosine = jnp.cos(angle)
    sine = jnp.where(lane8 < HEAD // 2, -1.0, 1.0) * jnp.sin(angle)

    def rotated(values):
        turned = jnp.concatenate([values[:, HEAD // 2 :], values[:, : HEAD // 2]], axis=1)
        return values * cosine + turned * sine

    total = add_up(squares, own, sq_recv)
    square = jnp.broadcast_to(total[0:1], (HEAD, HEAD)).T
    root_e = lax.rsqrt(square[:n_rows] / (width_e * n_ty) + EPS)
    root_a = lax.rsqrt(square[n_rows:] / (width_a * n_ty) + EPS)

    def project(x, root, g_load, gain, weights, send, recv, kind):
        width = x.shape[2]
        g_load.wait()
        values = x[...].reshape(n_rows, width)
        normed = (values * widen(root, width) * gain[...].astype(F32).reshape(1, width)).astype(BF16)
        parts = []
        for load, weight in weights:
            load.wait()
            columns = weight.shape[1]
            for at in range(0, columns, CHUNK):
                parts.append(mm(normed, weight[:, at : at + min(CHUNK, columns - at)]))
        send[...] = packed(jnp.concatenate(parts, axis=1).reshape(n_ty, 8, -1), send)
        return Exchange(n_ty, lambda d: send.at[ty_peers[d]], lambda d: recv.at[d], ty_send.at[kind], ty_recv.at[kind], to_ty,
                        recv.at[pl.ds(1, n_ty - 1)])

    sent_pe = project(x_e, root_e, l_gain_e, v_gain_e, ((l_wq_e, v_wq_e), (l_wk_e, v_wk_e), (l_wv_e, v_wv_e)), p_send_e, p_recv_e, 1)
    sent_pa = project(x_a, root_a, l_gain_a, v_gain_a, ((l_wq_a, v_wq_a), (l_wk_a, v_wk_a), (l_wv_a, v_wv_a)), p_send_a, p_recv_a, 2)

    for load in loads[18:]:
        load.start()

    def summed(exchange, send, recv, me):
        total = add_up(exchange, send[me].astype(F32), recv)
        return total if send.dtype == F32 else unfolded(total)

    def padded(rows, size):
        if rows.shape[0] == size:
            return rows
        return jnp.concatenate([rows, jnp.zeros((size - rows.shape[0], rows.shape[1]), F32)], axis=0)

    def attend(acc, heads, key_heads, k_load, keys, v_load, values):
        group = heads // key_heads
        n_query = heads * 8
        per_row = 2 * heads
        cache = keys.shape[1]
        wide = key_heads * HEAD
        query = jnp.concatenate([rotated(acc[:, h * HEAD : (h + 1) * HEAD]) for h in range(heads)], axis=0)
        at = heads * HEAD
        fresh_k = jnp.concatenate(
            [rotated(acc[:, at + h * HEAD : at + (h + 1) * HEAD]) for h in range(key_heads)], axis=0
        )
        at += wide
        fresh_v = jnp.concatenate(
            [acc[:, at + h * HEAD : at + (h + 1) * HEAD] for h in range(key_heads)], axis=0
        )
        fresh_k = padded(fresh_k, HEAD).astype(BF16)
        fresh_v = padded(fresh_v, HEAD).astype(BF16)
        forth = one_hot(n_query, lambda o: o % heads * 8 + o // heads % 2 * block + o // per_row)
        back = one_hot(n_query, lambda o: o % block * per_row + o // block % 2 * heads + o // 8)
        query = mm(forth, query.astype(BF16))
        owner = iota((n_query, HEAD), 0)
        lane = iota((n_query, HEAD), 1)
        fresh = mm_t(query.astype(BF16), fresh_k) * SCALE
        seen = (
            (lane < key_heads * 8)
            & (lane // 8 == owner % heads // group)
            & (lane % block == owner // per_row)
            & (lane // block % 2 <= owner // heads % 2)
        )
        fresh = jnp.where(seen, fresh, -jnp.inf)
        if key_heads > 1:
            spread = widen(query, wide)
            keep = iota((n_query, wide), 1) // HEAD == iota((n_query, wide), 0) % heads // group
            query = jnp.where(keep, spread, 0.0)
        k_load.wait()
        cached = []
        for i in range(block):
            part = query[i * per_row : (i + 1) * per_row].astype(BF16)
            score = mm_t(part, keys[i]) * SCALE
            cached.append(jnp.where(iota((per_row, cache), 1) < lengths[i], score, -jnp.inf))
        cached = jnp.concatenate(cached, axis=0)
        peak = jnp.maximum(jnp.max(cached, axis=1, keepdims=True), jnp.max(fresh, axis=1, keepdims=True))
        cached = jnp.exp(cached - peak)
        fresh = jnp.exp(fresh - peak)
        total = jnp.sum(cached, axis=1, keepdims=True) + jnp.sum(fresh, axis=1, keepdims=True)
        v_load.wait()
        mixture = jnp.concatenate(
            [mm(cached[i * per_row : (i + 1) * per_row].astype(BF16), values[i]) for i in range(block)], axis=0
        )
        if key_heads > 1:
            picked = jnp.zeros((n_query, HEAD), F32)
            for h in range(key_heads):
                picked = picked + jnp.where(owner % heads // group == h, mixture[:, h * HEAD : (h + 1) * HEAD], 0.0)
            mixture = picked
        mixture = mixture + mm(fresh.astype(BF16), fresh_v)
        ready = mm(back, (mixture / total).astype(BF16))
        return jnp.concatenate([ready[h * 8 : (h + 1) * 8] for h in range(heads)], axis=1)

    def gather(rows, buffer, kind):
        buffer[ty] = folded(rows).astype(BF16)
        return Exchange(n_ty, lambda d: buffer.at[ty], lambda d: buffer.at[ty], ty_send.at[kind], ty_recv.at[kind], to_ty,
                        buffer.at[pl.ds(0, n_ty - 1)])

    acc = summed(sent_pe, p_send_e, p_recv_e, ty)
    sent_ge = gather(attend(acc, heads_e, v_wk_e.shape[1] // HEAD, l_kc_e, v_kc_e, l_vc_e, v_vc_e), g_e, 3)
    acc = summed(sent_pa, p_send_a, p_recv_a, ty)
    sent_ga = gather(attend(acc, heads_a, v_wk_a.shape[1] // HEAD, l_kc_a, v_kc_a, l_vc_a, v_vc_a), g_a, 4)
    drain(2)

    def output(exchange, buffer, load, weight, send, recv, kind):
        exchange.arrive()
        rows = unfolded(buffer[...].astype(F32)).reshape(n_rows, weight.shape[0]).astype(BF16)
        load.wait()
        columns = weight.shape[1]
        parts = [mm(rows, weight[:, at : at + CHUNK]) for at in range(0, columns, CHUNK)]
        send[...] = packed(jnp.concatenate(parts, axis=1).reshape(n_tx, 8, columns), send)
        return Exchange(n_tx, lambda d: send.at[tx_peers[d]], lambda d: recv.at[d], tx_send.at[kind], tx_recv.at[kind, 0], to_tx,
                        recv.at[pl.ds(1, n_tx - 1)])

    sent_oe = output(sent_ge, g_e, l_wo_e, v_wo_e, o_send_e, o_recv_e, 0)
    sent_oa = output(sent_ga, g_a, l_wo_a, v_wo_a, o_send_a, o_recv_a, 1)
    drain(2)

    def residual(exchange, x, send, recv, s_send, s_recv, kind):
        values = x[tx] + summed(exchange, send, recv, tx)
        part = lane_fold(values * values)
        s_send[...] = part
        return values, part, Exchange(
            n_ty, lambda d: s_send, lambda d: s_recv.at[d], ty_send.at[kind], ty_recv.at[kind], to_ty,
            s_recv.at[pl.ds(1, n_ty - 1)],
        )

    res_e, part_e, sent_se = residual(sent_oe, x_e, o_send_e, o_recv_e, s_send_e, s_recv_e, 5)
    res_a, part_a, sent_sa = residual(sent_oa, x_a, o_send_a, o_recv_a, s_send_a, s_recv_a, 6)
    drain(2)

    def final(values, part, exchange, s_recv, g_load, gain, buffer, kind):
        width = values.shape[1]
        g_load.wait()
        part = add_up(exchange, part, s_recv)
        mean = jnp.sum(part, axis=1, keepdims=True) / (width * n_ty)
        rows = values * lax.rsqrt(mean + EPS) * gain[...].astype(F32).reshape(1, width)
        buffer[flat] = folded(rows).astype(BF16)
        across = Exchange(
            n_tx, lambda d: buffer.at[flat], lambda d: buffer.at[flat], tx_send.at[kind], tx_recv.at[kind], to_tx,
            buffer.at[pl.ds(0, n_tx - 1)], each=True,
        )

        def from_tx(step):
            return grp * n_tx + tx_sources[step]

        forward = Exchange(
            n_tx, lambda d: buffer.at[from_tx(d)], lambda d: buffer.at[from_tx(d)], fw_send.at[kind - 2],
            fw_recv.at[kind - 2], lambda d: {"grp": 1 - grp}, buffer.at[pl.ds((1 - grp) * n_tx, n_tx)], begin=False, low=0,
        )
        forward.make(0).start()
        return across, forward

    def pass_on(pair):
        across, forward = pair

        for step in (1, 3, 4, 2, 5, 7, 6):
            across.make(step).wait_recv()
            forward.make(step).start()

    def passed_on(pair):
        pair[1].arrive()

    pair_e = final(res_e, part_e, sent_se, s_recv_e, l_fin_e, v_fin_e, f_e, 2)
    pair_a = final(res_a, part_a, sent_sa, s_recv_a, l_fin_a, v_fin_a, f_a, 3)

    padding = v_head_e.shape[0] - vocab
    l_head_a.wait()
    v_head_a[pl.ds(vocab, padding), :] = jnp.zeros((padding, width_a), BF16)
    l_head_e.wait()
    v_head_e[pl.ds(vocab, padding), :] = jnp.zeros((padding, width_e), BF16)

    n_slab = v_head_e.shape[0] // SLAB

    logit_exchanges = [
        Exchange(
            n_ty, None, None, l_ssem.at[slab], l_rsem.at[slab], to_ty, l_recv.at[slab, pl.ds(1, n_ty - 1)], begin=False,
        )
        for slab in range(2 * n_slab)
    ]

    def logits(buffer, half, head, base):
        rows = unfolded(buffer[pl.ds(half * n_tx, n_tx)].astype(F32)).reshape(n_rows, head.shape[1]).astype(BF16)
        side = jnp.where(half == coarse, 0, 4)

        def copy(slab, step):
            target = half * 4 + rings[step]
            return pltpu.make_async_remote_copy(
                src_ref=l_send.at[slab, target], dst_ref=l_recv.at[slab, side + step], send_sem=l_ssem.at[slab],
                recv_sem=l_rsem.at[slab], device_id={"ty": target}, device_id_type=MESH,
            )

        for slab in range(n_slab):
            for at in range(0, SLAB, CHUNK):
                part = mm_t(rows, head[slab * SLAB + at : slab * SLAB + at + CHUNK, :])
                part = part.reshape(4, 16, CHUNK).astype(BF16)
                l_send[base + slab, pl.ds(half * 4, 4), :, at : at + CHUNK] = part
            for step in (2, 1, 3):
                copy(base + slab, step).start()

            @pl.when(half != coarse)
            def _():
                copy(base + slab, 0).start()

    pass_on(pair_e)
    logits(f_e, grp, v_head_e, 0)
    pass_on(pair_a)
    passed_on(pair_e)
    logits(f_e, 1 - grp, v_head_e, 0)
    logits(f_a, grp, v_head_a, n_slab)
    passed_on(pair_a)
    logits(f_a, 1 - grp, v_head_a, n_slab)

    def slab_sum(slab):
        return add_up(logit_exchanges[slab], l_send[slab, ty].astype(F32), l_recv.at[slab])

    lane_c = iota((16, SLAB), 1)

    def peak_and_total(parts):
        masked = [jnp.where(lane_c + c * SLAB < vocab, part, -jnp.inf) for c, part in enumerate(parts)]
        peak = masked[0]
        for part in masked[1:]:
            peak = jnp.maximum(peak, part)
        peak = jnp.max(peak, axis=1, keepdims=True)
        total = jnp.exp(masked[0] - peak)
        for part in masked[1:]:
            total = total + jnp.exp(part - peak)
        return peak, jnp.sum(total, axis=1, keepdims=True)

    l_tokens.wait()
    row16 = iota((16, HEAD), 0)
    token = jnp.zeros((16, HEAD), jnp.int32)
    for s in range(2):
        for r in range(8):
            token = jnp.where(row16 == r // block * 8 + s * block + r % block, tokens[s, r], token)
    token = widen(token - flat * vocab, SLAB)

    drain(2 * n_slab)
    expert = [slab_sum(c) for c in range(n_slab)]
    peak_e, total_e = peak_and_total(expert)
    amateur = [slab_sum(n_slab + c) for c in range(n_slab)]
    peak_a, total_a = peak_and_total(amateur)
    chosen = jnp.zeros((16, SLAB), F32)
    mixed = []
    for c in range(n_slab):
        mixed.append(expert[c] - AMATEUR * amateur[c])
        column = lane_c + c * SLAB
        chosen = chosen + jnp.where((column == token) & (column < vocab), mixed[c], 0.0)
    chosen = jnp.sum(chosen, axis=1, keepdims=True)

    lane16 = iota((16, HEAD), 1) % 64
    tile = jnp.where(lane16 == 0, peak_e, jnp.where(lane16 == 1, total_e, 0.0))
    tile = jnp.where(lane16 == 2, peak_a, jnp.where(lane16 == 3, total_a, tile))
    tile = jnp.where(lane16 == 4, chosen, tile)
    tile = jnp.where(lane8 < 64, tile[:8], tile[8:])
    t_send[...] = tile
    stats = Exchange(n_flat, lambda d: t_send, lambda d: t_recv.at[d], t_ssem.at[0], t_rsem.at[0], flat_peer,
             t_recv.at[pl.ds(1, n_flat - 1)])
    drain(1)
    stats.arrive()
    tiles = [tile] + [t_recv[step] for step in range(1, n_flat)]
    highest = functools.reduce(jnp.maximum, tiles)
    picked = functools.reduce(jnp.add, tiles)

    def shifted(values):
        return jnp.concatenate([values[:, 1:], values[:, :1]], axis=1)

    summed_up = functools.reduce(jnp.add, [jnp.exp(t - highest) * shifted(t) for t in tiles])
    log_total = highest + jnp.log(summed_up)

    def column(values, lane):
        return jnp.concatenate([values[:, lane : lane + 1], values[:, lane + 64 : lane + 65]], axis=0)

    offset = column(log_total, 0) - AMATEUR * column(log_total, 2)
    for c in range(n_slab):
        size = min(SLAB, vocab - c * SLAB)
        contrast = mixed[c] - offset
        for s in range(2):
            low = s * block
            out_ref[s, :, c * SLAB : c * SLAB + size] = jnp.concatenate(
                [contrast[low : low + block], contrast[8 + low : 8 + low + block]], axis=0
            )[:, :size]
    value = jnp.broadcast_to(column(picked, 4) - offset, (16, HEAD))
    lane_r = iota((16, HEAD), 1)
    for s in range(2):
        mine = row16 == lane_r // block * 8 + s * block + lane_r % block
        line = jnp.sum(jnp.where(mine & (lane_r < 8), value, 0.0), axis=0, keepdims=True)
        score_ref[s : s + 1, :] = line[:, :8]

    drain(0)


def on_device(axes, *args):
    (
        hid_e, gain_e, wq_e, wk_e, wv_e, wo_e, fin_e, head_e, kc_e, vc_e,
        hid_a, gain_a, wq_a, wk_a, wv_a, wo_a, fin_a, head_a, kc_a, vc_a,
        lengths, tokens,
    ) = args
    n_grp, n_tx, n_ty = axes
    n_flat = n_grp * n_tx
    half = hid_e.shape[1] // n_grp
    vocab = head_e.shape[0]
    padded = -(-vocab // SLAB) * SLAB
    n_slab = padded // SLAB
    n_rows = 2 * half
    width_e, width_a = hid_e.shape[2], hid_a.shape[2]
    cols_e = wq_e.shape[1] + wk_e.shape[1] + wv_e.shape[1]
    cols_a = wq_a.shape[1] + wk_a.shape[1] + wv_a.shape[1]
    inner_e, inner_a = wo_e.shape[0], wo_a.shape[0]

    def like(array):
        return pltpu.VMEM(array.shape, array.dtype)

    scratch = [
        pltpu.SMEM(lengths.shape, jnp.int32), pltpu.SMEM(tokens.shape, jnp.int32),
        like(gain_e), like(fin_e), like(gain_a), like(fin_a),
    ]
    for hid, wq, wk, wv, wo, head, kc, vc in (
        (hid_e, wq_e, wk_e, wv_e, wo_e, head_e, kc_e, vc_e),
        (hid_a, wq_a, wk_a, wv_a, wo_a, head_a, kc_a, vc_a),
    ):
        scratch += [
            pltpu.VMEM((2, half, hid.shape[2]), BF16), like(wq), like(wk), like(wv), like(wo),
            pltpu.VMEM((padded, head.shape[1]), BF16), like(kc), like(vc),
        ]
    scratch += [
        pltpu.VMEM((n_ty, 8, width_e), F32), pltpu.VMEM((n_ty, 8, width_a), F32),
        pltpu.VMEM((8, HEAD), F32), pltpu.VMEM((n_ty, 8, HEAD), F32),
        pltpu.VMEM((n_ty, 8, cols_e), F32), pltpu.VMEM((n_ty, 8, cols_e), F32),
        pltpu.VMEM((n_ty, 16, cols_a // 2), BF16), pltpu.VMEM((n_ty, 16, cols_a // 2), BF16),
        pltpu.VMEM((n_ty, 16, inner_e // 2), BF16), pltpu.VMEM((n_ty, 16, inner_a // 2), BF16),
        pltpu.VMEM((n_tx, 16, width_e // 2), BF16), pltpu.VMEM((n_tx, 16, width_e // 2), BF16),
        pltpu.VMEM((n_tx, 16, width_a // 2), BF16), pltpu.VMEM((n_tx, 16, width_a // 2), BF16),
        pltpu.VMEM((8, HEAD), F32), pltpu.VMEM((n_ty, 8, HEAD), F32),
        pltpu.VMEM((8, HEAD), F32), pltpu.VMEM((n_ty, 8, HEAD), F32),
        pltpu.VMEM((n_flat, 16, width_e // 2), BF16), pltpu.VMEM((n_flat, 16, width_a // 2), BF16),
        pltpu.VMEM((2 * n_slab, n_ty, 16, SLAB), BF16), pltpu.VMEM((2 * n_slab, n_ty, 16, SLAB), BF16),
        pltpu.VMEM((8, HEAD), F32), pltpu.VMEM((n_flat, 8, HEAD), F32),
        pltpu.SemaphoreType.DMA((22,)),
        pltpu.SemaphoreType.DMA((7,)), pltpu.SemaphoreType.DMA((7,)),
        pltpu.SemaphoreType.DMA((4,)), pltpu.SemaphoreType.DMA((4, n_tx)),
        pltpu.SemaphoreType.DMA((2,)), pltpu.SemaphoreType.DMA((2,)),
        pltpu.SemaphoreType.DMA((2 * n_slab,)), pltpu.SemaphoreType.DMA((2 * n_slab,)),
        pltpu.SemaphoreType.DMA((1,)), pltpu.SemaphoreType.DMA((1,)),
    ]
    hbm = pl.BlockSpec(memory_space=pl.ANY)
    vmem = pl.BlockSpec(memory_space=pltpu.VMEM)
    macs = n_rows * (width_e * (cols_e + inner_e) + width_a * (cols_a + inner_a)) + 2 * n_rows * vocab * (width_e + width_a)
    read = sum(array.size * array.dtype.itemsize for array in args)
    return pl.pallas_call(
        functools.partial(kernel, axes, None),
        out_shape=(
            pltpu.VMEM((2, hid_e.shape[1] // n_ty, vocab), F32),
            pltpu.VMEM((2, hid_e.shape[1] // n_ty), F32),
        ),
        in_specs=[hbm] * len(args),
        out_specs=(vmem, vmem),
        scratch_shapes=scratch,
        compiler_params=pltpu.CompilerParams(
            collective_id=0, has_side_effects=True, vmem_limit_bytes=56 * 1024 * 1024
        ),
        cost_estimate=pl.CostEstimate(flops=2 * macs, bytes_accessed=read, transcendentals=0),
        name="contrast",
    )(*args)


def solution(mesh):
    model = (
        P(None, None, "ty"), P("ty"), P("ty", "tx"), P("ty", "tx"), P("ty", "tx"), P("tx", "ty"), P("ty"),
        P(("grp", "tx"), "ty"), P(("grp", "ty"), None, "tx"), P(("grp", "ty"), None, "tx"),
    )
    axes = tuple(mesh.shape[name] for name in ("grp", "tx", "ty"))
    return jax.shard_map(
        functools.partial(on_device, axes),
        mesh=mesh,
        in_specs=model + model + (P(("grp", "ty")), P(None, "ty")),
        out_specs=(P(None, "ty", ("grp", "tx")), P(None, "ty")),
        check_vma=False,
    )
```
